32 devices in a mesh: span: 8 (over z, x), plane: 4 (over y, core).
Axes of the slice: x: 2, y: 2, z: 4, core: 2. Of those that a mesh axis runs over, the one named last changes fastest.
Arguments:
- rhs: float32 [80, 512], P(None, ('span', 'plane')), may hold values from -6 to 6
- blocks: float32 [512, 70400], P(('span', 'plane')), as said below
- columns: int32 [11, 512], P(None, ('span', 'plane')), may hold values from 0 to 511, as said below
- line_slot: int32 [32, 16], P(('span', 'plane')), may hold values from 0 to 15, each once within a row
- line_lower: float32 [512, 6400], P(('span', 'plane')), may hold values from -0.2 to 0.2
- line_upper: float32 [512, 6400], P(('span', 'plane')), may hold values from -0.2 to 0.2
- pivot_inv: float32 [512, 6400], P(('span', 'plane')), as said below
Outputs:
- solution: float32 [80, 512], P(None, ('span', 'plane'))
- residual: float32 [80, 512], P(None, ('span', 'plane'))
The draws below stay inside these ranges and needn't reach their ends.
Inputs may be any that keep to these rules, and one draw needn't show every extreme that they name: columns[0, i] = i; the other columns name faces on the device itself, on the devices one step along span (wrapping) or one step along plane (not wrapping). Blocks 1 to 4 name faces on the span devices after and before and the plane devices after and before, or on the device itself where no such plane device exists. pivot_inv is a diagonal with entries between about 0.5 and 2.0 plus a full-rank off-diagonal part of small entries. `blocks`: block 0 of every row has an added diagonal of 1 to about 4.06.
All inputs are finite; a program needn't handle non-finite values.
Results may differ from the reference program's by a relative error of at most 0.0065.
Values sent between devices are 32-bit elements; how exact they have to be, the bound alone decides.
No kernel may reach another device: no remote copies, remote signals or barrier semaphores. Data moves between devices by JAX's collectives and lax.ppermute only.
A program may use at most 128 MiB of HBM per device.

```python
import jax
import jax.numpy as jnp
from jax import lax

B = 80
NBLK = 11
ITERS = 3
P_SIZE = 2
LPD = 2
F = 16
LEN = 8
NFACES = 512
LINES = 64
N_SPAN = 8
N_PLANE = 4
DEVICES = 32


def draw_blocks(key, part):
    key = jax.random.fold_in(key, 11)
    key_noise, key_diag = jax.random.split(key, 2)
    noise = jax.random.normal(key_noise, (NFACES, NBLK, B, B), jnp.float32)
    noise = noise * (0.35 / (B * NBLK) ** 0.5)
    diag = jnp.exp(jax.random.uniform(key_diag, (NFACES, B), jnp.float32, 0.0, 1.4))
    eye = jnp.eye(B, dtype=jnp.float32)[None, :, :] * diag[:, :, None]
    return noise.at[:, 0].add(eye).reshape(NFACES, NBLK * B * B)


def draw_columns(key, part):
    key = jax.random.fold_in(key, 23)
    key_dir, key_loc = jax.random.split(key)
    faces = jnp.arange(NFACES, dtype=jnp.int32)
    device = faces // F
    span_idx = device // N_PLANE
    plane_idx = device % N_PLANE
    fixed_dir = jnp.array([0, 1, 2, 3, 4, 0, 0, 0, 0, 0, 0], jnp.int32)[:NBLK]
    rand_dir = jax.random.randint(key_dir, (NBLK, NFACES), 0, 5)
    slot_k = jnp.arange(NBLK, dtype=jnp.int32)[:, None]
    direction = jnp.where(slot_k < 5, fixed_dir[:, None], rand_dir)
    dspan = jnp.where(direction == 1, 1, jnp.where(direction == 2, -1, 0))
    dplane = jnp.where(direction == 3, 1, jnp.where(direction == 4, -1, 0))
    span_new = (span_idx[None, :] + dspan + N_SPAN) % N_SPAN
    plane_new = plane_idx[None, :] + dplane
    plane_new = jnp.where((plane_new < 0) | (plane_new >= N_PLANE), plane_idx[None, :], plane_new)
    local = jax.random.randint(key_loc, (NBLK, NFACES), 0, F)
    target = (span_new * N_PLANE + plane_new) * F + local
    return jnp.where(slot_k == 0, faces[None, :], target).astype(jnp.int32)


def draw_pivot_inv(key, part):
    key = jax.random.fold_in(key, 37)
    key_noise, key_diag = jax.random.split(key)
    count = LINES * LEN
    noise = jax.random.normal(key_noise, (count, B, B), jnp.float32)
    noise = noise * (0.3 / B ** 0.5)
    diag = jnp.exp(jax.random.uniform(key_diag, (count, B), jnp.float32, -0.7, 0.7))
    eye = jnp.eye(B, dtype=jnp.float32)[None, :, :] * diag[:, :, None]
    return (noise + eye).reshape(count, B * B)


def levels(own_key, shape, cuts, least, high):
    def one(axis_at, shards_of):
        steps = jax.random.uniform(jax.random.fold_in(jax.random.fold_in(own_key, 6), axis_at), (shards_of,), jnp.float32, least / len(cuts), high / len(cuts))
        return jnp.repeat(jnp.exp(steps), shape[axis_at] // shards_of).reshape((-1,) + (1,) * (len(shape) - axis_at - 1))

    loudness = one(*cuts[0])
    for cut in cuts[1:]:
        loudness = loudness * one(*cut)
    return loudness


def bell_draw(key, dims, deviation, limit, cuts=(), kind=jnp.bfloat16):
    loudness = levels(key, dims, cuts, -0.22, 0.18) if cuts else 1.0
    values = jax.random.normal(key, dims, jnp.float32) * deviation * loudness
    return jnp.minimum(jnp.maximum(values, -limit), limit).astype(kind)


def setup_inputs(seed: int = 0) -> dict:
    seeds = jax.random.split(jax.random.key(seed), 8)
    rhs = bell_draw(seeds[0], (B, NFACES), 1.0, 6.0, ((1, 32),), jnp.float32)
    blocks = draw_blocks(jax.random.fold_in(seeds[7], 71), 0)
    columns = draw_columns(jax.random.fold_in(seeds[7], 71), 0)
    line_slot = jax.vmap(lambda own: jax.random.permutation(own, F))(jax.random.split(seeds[3], DEVICES)).reshape((DEVICES, F)).astype(jnp.int32)
    line_lower = bell_draw(seeds[4], (LINES * LEN, B * B), 0.03, 0.2, ((0, 32),), jnp.float32)
    line_upper = bell_draw(seeds[5], (LINES * LEN, B * B), 0.03, 0.2, ((0, 32),), jnp.float32)
    pivot_inv = draw_pivot_inv(jax.random.fold_in(seeds[7], 71), 0)
    return dict(rhs=rhs, blocks=blocks, columns=columns, line_slot=line_slot, line_lower=line_lower, line_upper=line_upper, pivot_inv=pivot_inv)


HIGH = lax.Precision.HIGHEST

def small_solve(factor, target):
    extent = target.shape[0]
    forward_vals = []
    for row in range(extent):
        running = target[row]
        for inner in range(row):
            running = running - factor[row, inner] * forward_vals[inner]
        forward_vals.append(running / factor[row, row])
    backward_vals = [None] * extent
    for row in reversed(range(extent)):
        running = forward_vals[row]
        for inner in range(row + 1, extent):
            running = running - factor[inner, row] * backward_vals[inner]
        backward_vals[row] = running / factor[row, row]
    return jnp.stack(backward_vals)

def to_sequence(factor_rows, nlines, length, width):
    return jnp.swapaxes(factor_rows.reshape(nlines, length, width, width), 0, 1)

def line_solve(rhs_lines, lseq, useq, pseq):
    rseq = jnp.moveaxis(rhs_lines, 2, 0)

    def forward(prev, items):
        right, low = items
        cur = right - jnp.einsum('mab,bm->am', low, prev, precision=HIGH)
        return (cur, cur)
    start = jnp.zeros(rseq.shape[1:], jnp.float32)
    _, yseq = lax.scan(forward, start, (rseq, lseq))

    def backward(nxt, items):
        yval, upp, piv = items
        inner = yval - jnp.einsum('mab,bm->am', upp, nxt, precision=HIGH)
        cur = jnp.einsum('mab,bm->am', piv, inner, precision=HIGH)
        return (cur, cur)
    _, zseq = lax.scan(backward, start, (yseq, useq, pseq), reverse=True)
    return jnp.moveaxis(zseq, 0, 2)

def reference(rhs, blocks, columns, line_slot, line_lower, line_upper, pivot_inv):
    nlines_group = LPD * N_PLANE
    devs = jnp.arange(DEVICES, dtype=jnp.int32)[:, None]
    slots = jnp.arange(F, dtype=jnp.int32)[None, :]
    span_idx = devs // N_PLANE
    plane_idx = devs % N_PLANE
    gline = span_idx * nlines_group + slots // P_SIZE + 0 * plane_idx
    gpos = plane_idx * P_SIZE + slots % P_SIZE
    faces = devs * F + line_slot
    face_of = jnp.zeros((LINES, LEN), jnp.int32).at[gline.ravel(), gpos.ravel()].set(faces.ravel())
    lower = to_sequence(line_lower, LINES, LEN, B)
    upper = to_sequence(line_upper, LINES, LEN, B)
    pivot = to_sequence(pivot_inv, LINES, LEN, B)
    shaped_blocks = blocks.reshape(NFACES, NBLK, B, B)

    def apply_a(vec):
        picked = vec[:, columns]
        return jnp.einsum('ikab,bki->ai', shaped_blocks, picked, precision=HIGH)

    def apply_m(vec):
        sol = line_solve(vec[:, face_of], lower, upper, pivot)
        return jnp.zeros_like(vec).at[:, face_of].set(sol)
    beta = jnp.sqrt(jnp.sum(rhs * rhs) + 1e-06)
    basis = [rhs / beta]
    hcols = []
    for step in range(ITERS):
        wvec = apply_a(apply_m(basis[step]))
        stacked = jnp.stack(basis)
        hvals = jnp.einsum('jai,ai->j', stacked, wvec, precision=HIGH)
        wvec = wvec - jnp.einsum('j,jai->ai', hvals, stacked, precision=HIGH)
        hnext = jnp.sqrt(jnp.sum(wvec * wvec) + 1e-06)
        basis.append(wvec / hnext)
        hcols.append(jnp.concatenate([hvals, hnext[None], jnp.zeros((ITERS - step - 1,), jnp.float32)]))
    hmat = jnp.stack(hcols, axis=1)
    gram_mat = jnp.dot(hmat.T, hmat, precision=HIGH)
    target = beta * hmat[0]
    factor = jnp.linalg.cholesky(gram_mat)
    coef = small_solve(factor, target)
    update = jnp.einsum('j,jai->ai', coef, jnp.stack(basis[:ITERS]), precision=HIGH)
    solution = apply_m(update)
    residual = rhs - apply_a(solution)
    return (solution, residual)
```

```python
import functools
import math

import jax
import jax.numpy as jnp
import numpy as np
from jax import lax
from jax.experimental import pallas as pl
from jax.experimental.pallas import tpu as pltpu
from jax.sharding import PartitionSpec as P

ITERS = 3
P_SIZE = 2
SHIFT = 2.0
EPS = 1e-6
VMEM_LIMIT = 16 * 1024 * 1024
HIGH = lax.Precision.HIGHEST
F32, BF16 = jnp.float32, jnp.bfloat16


def with_halo(x, sides, width, wrap):
    for axis, dim in sides:
        size, length = (lax.axis_size(axis), x.shape[dim])
        up = [(i, (i + 1) % size) for i in range(size if wrap else size - 1)]
        down = [(j, i) for i, j in up]
        last = lax.slice_in_dim(x, length - width, length, axis=dim)
        first = lax.slice_in_dim(x, 0, width, axis=dim)
        before = lax.ppermute(last, axis, up)
        after = lax.ppermute(first, axis, down)
        x = jnp.concatenate([before, x, after], axis=dim)
    return x


def small_solve(factor, target):
    extent = target.shape[0]
    forward_vals = []
    for row in range(extent):
        running = target[row]
        for inner in range(row):
            running = running - factor[row, inner] * forward_vals[inner]
        forward_vals.append(running / factor[row, row])
    backward_vals = [None] * extent
    for row in reversed(range(extent)):
        running = forward_vals[row]
        for inner in range(row + 1, extent):
            running = running - factor[inner, row] * backward_vals[inner]
        backward_vals[row] = running / factor[row, row]
    return jnp.stack(backward_vals)


def to_sequence(factor_rows, nlines, length, width):
    return jnp.swapaxes(factor_rows.reshape(nlines, length, width, width), 0, 1)


def line_solve(rhs_lines, lseq, useq, pseq):
    rseq = jnp.moveaxis(rhs_lines, 2, 0)

    def forward(prev, items):
        right, low = items
        cur = right - jnp.einsum("mab,bm->am", low, prev, precision=HIGH)
        return (cur, cur)

    start = jnp.zeros(rseq.shape[1:], F32)
    _, yseq = lax.scan(forward, start, (rseq, lseq))

    def backward(nxt, items):
        yval, upp, piv = items
        inner = yval - jnp.einsum("mab,bm->am", upp, nxt, precision=HIGH)
        cur = jnp.einsum("mab,bm->am", piv, inner, precision=HIGH)
        return (cur, cur)

    _, zseq = lax.scan(backward, start, (yseq, useq, pseq), reverse=True)
    return jnp.moveaxis(zseq, 0, 2)


def table_positions(columns, nfaces):
    nspan, nplane = lax.axis_size("span"), lax.axis_size("plane")
    my_span, my_plane = lax.axis_index("span"), lax.axis_index("plane")
    device_of = columns // nfaces
    span_of = device_of // nplane
    plane_of = device_of % nplane
    dspan = (span_of - my_span + 1 + nspan) % nspan - 1
    dplane = plane_of - my_plane
    selector = jnp.where(
        dspan == -1,
        1,
        jnp.where(dspan == 1, 2, jnp.where(dplane == -1, 3, jnp.where(dplane == 1, 4, 0))),
    )
    return selector * nfaces + columns % nfaces


def step_by_step(rhs, blocks, columns, line_slot, line_lower, line_upper, pivot_inv):
    width, nfaces = rhs.shape
    nblocks = columns.shape[0]
    nplane = lax.axis_size("plane")
    position = table_positions(columns, nfaces)
    slot = line_slot[0]
    lines_group = nfaces // P_SIZE
    owned = lines_group // nplane
    length = P_SIZE * nplane
    lower = to_sequence(line_lower, owned, length, width)
    upper = to_sequence(line_upper, owned, length, width)
    pivot = to_sequence(pivot_inv, owned, length, width)
    shaped_blocks = blocks.reshape(nfaces, nblocks, width, width)

    def apply_a(vec):
        shaped = vec.reshape(width, 1, 1, nfaces)
        span_side = with_halo(shaped, (("span", 1),), 1, True)
        plane_side = with_halo(shaped, (("plane", 2),), 1, False)
        below = plane_side[:, 0, 0]
        above = plane_side[:, 0, 2]
        table = jnp.concatenate([vec, span_side[:, 0, 0], span_side[:, 2, 0], below, above], axis=1)
        return jnp.einsum("ikab,bki->ai", shaped_blocks, table[:, position], precision=HIGH)

    def apply_m(vec):
        pieces = vec[:, slot].reshape(width, lines_group, P_SIZE)
        whole = lax.all_to_all(pieces, "plane", split_axis=1, concat_axis=2, tiled=True)
        solved = line_solve(whole, lower, upper, pivot)
        back = lax.all_to_all(solved, "plane", split_axis=2, concat_axis=1, tiled=True)
        return jnp.zeros_like(vec).at[:, slot].set(back.reshape(width, nfaces))

    beta = jnp.sqrt(lax.psum(jnp.sum(rhs * rhs), ("span", "plane")) + EPS)
    basis = [rhs / beta]
    hcols = []
    for step in range(ITERS):
        wvec = apply_a(apply_m(basis[step]))
        stacked = jnp.stack(basis)
        hvals = lax.psum(jnp.einsum("jai,ai->j", stacked, wvec, precision=HIGH), ("span", "plane"))
        wvec = wvec - jnp.einsum("j,jai->ai", hvals, stacked, precision=HIGH)
        hnext = jnp.sqrt(lax.psum(jnp.sum(wvec * wvec), ("span", "plane")) + EPS)
        basis.append(wvec / hnext)
        hcols.append(jnp.concatenate([hvals, hnext[None], jnp.zeros((ITERS - step - 1,), F32)]))
    hmat = jnp.stack(hcols, axis=1)
    factor = jnp.linalg.cholesky(jnp.dot(hmat.T, hmat, precision=HIGH))
    coef = small_solve(factor, beta * hmat[0])
    update = jnp.einsum("j,jai->ai", coef, jnp.stack(basis[:ITERS]), precision=HIGH)
    solution = apply_m(update)
    return solution, rhs - apply_a(solution)


def partner(me, k, size):
    if size & (size - 1) == 0:
        return me ^ k, me ^ k
    return (me + k) % size, (me + size - k) % size


def exchange(x, axis, k):
    size = lax.axis_size(axis)
    return lax.ppermute(x, axis, [(i, partner(i, k, size)[0]) for i in range(size)])


def start_kernel(nplane, me_ref, slot_ref, u_ref, tail_ref, *outs):
    per = slot_ref.shape[1] // nplane
    for k in range(nplane):
        to, _ = partner(me_ref[0], k, nplane)
        for i in range(per):
            outs[k][pl.ds(i, 1), :] = u_ref[pl.ds(slot_ref[0, to * per + i], 1), :]
        outs[k][pl.ds(per, 1), :] = tail_ref[...]


def line_kernel(nplane, nlines, me_ref, *refs):
    msgs, (low, low_t, upp, piv_t, z_ref, r_scr) = refs[:nplane], refs[nplane:]
    width = z_ref.shape[1]
    length = z_ref.shape[0] // nlines
    for k in range(nplane):
        _, source = partner(me_ref[0], k, nplane)
        for m in range(nlines):
            for q in range(P_SIZE):
                r_scr[m, pl.ds(source * P_SIZE + q, 1), :] = msgs[k][pl.ds(m * P_SIZE + q, 1), :]
    eye = lax.broadcasted_iota(jnp.int32, (width, width), 0) == lax.broadcasted_iota(jnp.int32, (width, width), 1)

    def column(row):
        return jnp.sum(jnp.where(eye, row, 0.0), axis=1, keepdims=True)

    rows = [[r_scr[m, pl.ds(j, 1), :] for m in range(nlines)] for j in range(length)]
    y_cols = [[None] * nlines for _ in range(length)]
    carry = [None] * nlines
    for j in range(length):
        for m in range(nlines):
            at = m * length + j
            if j == 0:
                carry[m] = rows[j][m]
            elif j % 2:
                carry[m] = column(rows[j][m]) - jnp.sum(low[at] * carry[m], axis=1, keepdims=True)
            else:
                carry[m] = rows[j][m] - jnp.sum(low_t[at] * carry[m], axis=0, keepdims=True)
            y_cols[j][m] = carry[m] if j % 2 else column(carry[m])
    after = [None] * nlines
    for j in reversed(range(length)):
        for m in range(nlines):
            at = m * length + j
            inner = y_cols[j][m]
            if j < length - 1:
                inner = inner - jnp.sum(upp[at] * after[m], axis=1, keepdims=True)
            after[m] = jnp.sum(piv_t[at] * inner, axis=0, keepdims=True)
            z_ref[pl.ds(at, 1), :] = after[m]


def faces_kernel(nplane, nlines, me_ref, slots_ref, *refs):
    solved, (mine_ref, sides_ref) = refs[:nplane], refs[nplane:]
    nfaces = mine_ref.shape[0]
    length = nfaces // nlines
    per = nlines * P_SIZE
    me = me_ref[0]
    for side, dplane in enumerate((0, -1, 1)):
        there = me + dplane
        safe = jnp.clip(there, 0, nplane - 1)
        for k in range(nplane):
            _, owner = partner(me, k, nplane)
            for i in range(per):
                face = slots_ref[safe, owner * per + i]
                row = solved[k][pl.ds((i // P_SIZE) * length + safe * P_SIZE + i % P_SIZE, 1), :]
                if side == 0:
                    mine_ref[pl.ds(face, 1), :] = row
                else:
                    sides_ref[pl.ds((side - 1) * nfaces + face, 1), :] = row


def apply_kernel(nplane, last, *refs):
    (me_ref, slot_ref, blocks, pick, seg, mine, before, after, sides), refs = refs[:9], refs[9:]
    nold = ITERS if last else 1
    olds, refs = refs[:nold], refs[nold:]
    next_ref, refs = refs[0], refs[1:]
    nfaces, width = mine.shape
    area = width * width
    nblocks = blocks.shape[1] // area
    chunk = seg.shape[0]
    copies = chunk // width
    table = jnp.concatenate([mine[...], before[...], after[...], sides[...]], axis=0)
    high = table.astype(BF16).astype(F32)
    both = jnp.concatenate([high, table - high], axis=0)
    wide = jnp.concatenate([both] * copies, axis=1).astype(BF16)
    x_scr = refs[-1]
    x_scr[...] = jnp.dot(pick[...], wide, preferred_element_type=F32)
    masks = lax.broadcasted_iota(jnp.int32, (nfaces, seg.shape[1]), 1) // copies
    total = jnp.zeros((nfaces, seg.shape[1]), F32)
    parts = []
    for c in range(area // chunk):
        acc = None
        for k in range(nblocks):
            at = k * area + c * chunk
            term = blocks[:, at : at + chunk] * x_scr[k * nfaces : (k + 1) * nfaces, :]
            acc = term if acc is None else acc + term
        acc_high = acc.astype(BF16)
        parts += [acc_high, (acc - acc_high.astype(F32)).astype(BF16)]
    sums = jnp.dot(jnp.concatenate(parts, axis=0), seg[...], preferred_element_type=F32)
    for c in range(area // chunk):
        pair = sums[2 * c * nfaces : (2 * c + 1) * nfaces] + sums[(2 * c + 1) * nfaces : (2 * c + 2) * nfaces]
        total = total + jnp.where(masks == c, pair, 0.0)
    u_next = total[:, :width] - SHIFT * olds[-1][...]
    next_ref[...] = u_next
    if last:
        gram_ref = refs[0]
        basis = [old[...] for old in olds] + [u_next]
        row = 0
        for i in range(ITERS + 1):
            for j in range(i, ITERS + 1):
                value = jnp.sum(jnp.sum(basis[i] * basis[j], axis=1, keepdims=True), axis=0, keepdims=True)
                gram_ref[pl.ds(row, 1), :] = jnp.broadcast_to(value, (1, gram_ref.shape[1]))
                row += 1
    else:
        outs = refs[:nplane]
        per = nfaces // nplane
        for k in range(nplane):
            to, _ = partner(me_ref[0], k, nplane)
            for i in range(per):
                outs[k][pl.ds(i, 1), :] = next_ref[pl.ds(slot_ref[0, to * per + i], 1), :]


def finish_kernel(gram_ref, *refs):
    us, zs = refs[: ITERS + 1], refs[ITERS + 1 : 2 * ITERS + 1]
    sol_ref, res_ref, ok_ref = refs[2 * ITERS + 1 :]
    width = sol_ref.shape[1]
    gram, row = {}, 0
    for i in range(ITERS + 1):
        for j in range(i, ITERS + 1):
            gram[i, j] = gram[j, i] = gram_ref[pl.ds(row, 1), :]
            row += 1
    largest = functools.reduce(jnp.maximum, [jnp.abs(g) for g in gram.values()])
    ok = largest < 1e30
    beta = jnp.sqrt(gram[0, 0] + EPS)
    basis = [[1.0 / beta]]
    hmat = {}
    for step in range(ITERS):
        own = basis[step]
        wvec = [SHIFT * own[0]] + [own[i] + SHIFT * own[i + 1] for i in range(step)] + [own[step]]
        images = [sum(gram[i, j] * wvec[j] for j in range(step + 2)) for i in range(step + 1)]
        for i in range(step + 1):
            hmat[i, step] = sum(basis[i][m] * images[m] for m in range(i + 1))
        for i in range(step + 1):
            for m in range(i + 1):
                wvec[m] = wvec[m] - hmat[i, step] * basis[i][m]
        terms = [wvec[i] * wvec[j] * gram[i, j] for i in range(step + 2) for j in range(step + 2)]
        square = jnp.maximum(sum(terms), 0.0)
        ok = ok & (square + EPS >= 2e-3 * sum(jnp.abs(term) for term in terms))
        hmat[step + 1, step] = jnp.sqrt(square + EPS)
        scale = 1.0 / hmat[step + 1, step]
        basis.append([w * scale for w in wvec])
    normal = {
        (i, j): sum(hmat[m, i] * hmat[m, j] for m in range(j + 2) if (m, i) in hmat and (m, j) in hmat)
        for i in range(ITERS)
        for j in range(i + 1)
    }
    factor, inverse = {}, []
    for j in range(ITERS):
        diag = jnp.sqrt(normal[j, j] - sum(factor[j, m] * factor[j, m] for m in range(j)))
        inverse.append(1.0 / diag)
        for i in range(j + 1, ITERS):
            factor[i, j] = (normal[i, j] - sum(factor[i, m] * factor[j, m] for m in range(j))) * inverse[j]
    forward = []
    for i in range(ITERS):
        forward.append((beta * hmat[0, i] - sum(factor[i, m] * forward[m] for m in range(i))) * inverse[i])
    coef = [None] * ITERS
    for i in reversed(range(ITERS)):
        coef[i] = (forward[i] - sum(factor[m, i] * coef[m] for m in range(i + 1, ITERS))) * inverse[i]
    mix = [sum(coef[s] * basis[s][m] for s in range(m, ITERS))[:, :width] for m in range(ITERS)]
    sol_ref[...] = sum(mix[m] * zs[m][...] for m in range(ITERS))
    image = sum(mix[m] * (us[m + 1][...] + SHIFT * us[m][...]) for m in range(ITERS))
    res_ref[...] = us[0][...] - image
    ok = ok & (functools.reduce(jnp.maximum, [jnp.abs(c) for c in coef]) < 1e30)
    ok_ref[...] = jnp.where(ok, 1.0, 0.0)


def call(kernel, args, outs, scratch=(), flops=0, pinned=True):
    spaces = [pltpu.SMEM if x.dtype == jnp.int32 else pltpu.VMEM for x in args]
    args = [x if s is pltpu.SMEM else pltpu.with_memory_space_constraint(x, s) for x, s in zip(args, spaces)]
    size = sum(4 * math.prod(x.shape) for x in args)
    return pl.pallas_call(
        kernel,
        out_shape=[pltpu.VMEM(shape, F32) if pinned else jax.ShapeDtypeStruct(shape, F32) for shape in outs],
        in_specs=[pl.BlockSpec(memory_space=s) for s in spaces],
        out_specs=[pl.BlockSpec(memory_space=pltpu.VMEM) for _ in outs],
        scratch_shapes=scratch,
        compiler_params=pltpu.CompilerParams(vmem_limit_bytes=VMEM_LIMIT),
        cost_estimate=pl.CostEstimate(flops=flops, bytes_accessed=size, transcendentals=0),
    )(*args)


def add_up(x, axis):
    size = lax.axis_size(axis)
    if size & (size - 1):
        return lax.psum(x, axis)
    step = 1
    while step < size:
        x = x + exchange(x, axis, step)
        step *= 2
    return x


def on_device(rhs, blocks, columns, line_slot, line_lower, line_upper, pivot_inv):
    width, nfaces = rhs.shape
    nblocks = columns.shape[0]
    nspan, nplane = lax.axis_size("span"), lax.axis_size("plane")
    owned = nfaces // P_SIZE // nplane
    length = P_SIZE * nplane
    per = owned * P_SIZE
    me = lax.axis_index("plane").astype(jnp.int32)[None]
    shape = (nfaces, width)

    position = table_positions(columns, nfaces).reshape(nblocks * nfaces, 1)
    places = 5 * nfaces
    pick = (lax.broadcasted_iota(jnp.int32, (1, 2 * places), 1) % places == position).astype(BF16)
    chunk = math.lcm(width, 128)
    seg = (np.arange(chunk)[:, None] // width == np.arange(128)[None, :] % (chunk // width)).astype(np.float32)
    seg = jnp.asarray(seg, BF16)
    low = line_lower.reshape(nfaces, width, width)
    low_t = jnp.swapaxes(low, 1, 2)
    upp = line_upper.reshape(nfaces, width, width)
    piv_t = jnp.swapaxes(pivot_inv.reshape(nfaces, width, width), 1, 2)

    us = [rhs.T]
    zs = []
    tail = jnp.pad(line_slot.astype(F32), ((0, 0), (0, width - nfaces)))
    send = call(
        functools.partial(start_kernel, nplane), [me, line_slot, us[0], tail], [(per + 1, width)] * nplane
    )
    up = [(i, (i + 1) % nspan) for i in range(nspan)]
    down = [(j, i) for i, j in up]
    slots = None
    for step in range(ITERS):
        got = [send[0]] + [exchange(send[k], "plane", k) for k in range(1, nplane)]
        if step == 0:
            owners = jnp.stack([partner(me[0], k, nplane)[1] for k in range(nplane)])
            known = jnp.concatenate([g[per:, :nfaces] for g in got], axis=0).astype(jnp.int32)
            slots = jnp.sum(
                jnp.where(owners[None, :, None] == jnp.arange(nplane)[:, None, None], known[None], 0), axis=1
            ).astype(jnp.int32)
        (solved,) = call(
            functools.partial(line_kernel, nplane, owned),
            [me, *got, low, low_t, upp, piv_t],
            [shape],
            [pltpu.VMEM((owned, length, width), F32)],
            flops=6 * nfaces * width * width,
        )
        pieces = [solved] + [exchange(solved, "plane", k) for k in range(1, nplane)]
        mine, sides = call(
            functools.partial(faces_kernel, nplane, owned), [me, slots, *pieces], [shape, (2 * nfaces, width)]
        )
        zs.append(mine)
        before = lax.ppermute(mine, "span", up)
        after = lax.ppermute(mine, "span", down)
        last = step == ITERS - 1
        out = call(
            functools.partial(apply_kernel, nplane, last),
            [me, line_slot, blocks, pick, seg, mine, before, after, sides, *(us if last else us[-1:])],
            [shape] + ([(16, 128)] if last else [(per, width)] * nplane),
            [pltpu.VMEM((nblocks * nfaces, chunk), F32)],
            flops=2 * nblocks * nfaces * width * width,
        )
        us.append(out[0])
        send = out[1:]
    gram = add_up(add_up(send[0], "plane"), "span")
    sol, res, ok = call(finish_kernel, [gram, *us, *zs], [shape, shape, (1, 128)], pinned=False)
    return lax.cond(
        ok[0, 0] > 0.5,
        lambda *_: (sol.T, res.T),
        step_by_step,
        rhs, blocks, columns, line_slot, line_lower, line_upper, pivot_inv,
    )


def solution(mesh):
    both = ("span", "plane")
    return jax.shard_map(
        on_device,
        mesh=mesh,
        in_specs=(
            P(None, both),
            P(both, None),
            P(None, both),
            P(both, None),
            P(both, None),
            P(both, None),
            P(both, None),
        ),
        out_specs=(P(None, both), P(None, both)),
        check_vma=False,
    )
```

```python
import functools
import math

import jax
import jax.numpy as jnp
import numpy as np
from jax import lax
from jax.experimental import pallas as pl
from jax.experimental.pallas import tpu as pltpu
from jax.sharding import PartitionSpec as P

ITERS = 3
P_SIZE = 2
SHIFT = 2.0
EPS = 1e-6
VMEM_LIMIT = 16 * 1024 * 1024
HIGH = lax.Precision.HIGHEST
F32, BF16 = jnp.float32, jnp.bfloat16


def with_halo(x, sides, width, wrap):
    for axis, dim in sides:
        size, length = (lax.axis_size(axis), x.shape[dim])
        up = [(i, (i + 1) % size) for i in range(size if wrap else size - 1)]
        down = [(j, i) for i, j in up]
        last = lax.slice_in_dim(x, length - width, length, axis=dim)
        first = lax.slice_in_dim(x, 0, width, axis=dim)
        before = lax.ppermute(last, axis, up)
        after = lax.ppermute(first, axis, down)
        x = jnp.concatenate([before, x, after], axis=dim)
    return x


def small_solve(factor, target):
    extent = target.shape[0]
    forward_vals = []
    for row in range(extent):
        running = target[row]
        for inner in range(row):
            running = running - factor[row, inner] * forward_vals[inner]
        forward_vals.append(running / factor[row, row])
    backward_vals = [None] * extent
    for row in reversed(range(extent)):
        running = forward_vals[row]
        for inner in range(row + 1, extent):
            running = running - factor[inner, row] * backward_vals[inner]
        backward_vals[row] = running / factor[row, row]
    return jnp.stack(backward_vals)


def to_sequence(factor_rows, nlines, length, width):
    return jnp.swapaxes(factor_rows.reshape(nlines, length, width, width), 0, 1)


def line_solve(rhs_lines, lseq, useq, pseq):
    rseq = jnp.moveaxis(rhs_lines, 2, 0)

    def forward(prev, items):
        right, low = items
        cur = right - jnp.einsum("mab,bm->am", low, prev, precision=HIGH)
        return (cur, cur)

    start = jnp.zeros(rseq.shape[1:], F32)
    _, yseq = lax.scan(forward, start, (rseq, lseq))

    def backward(nxt, items):
        yval, upp, piv = items
        inner = yval - jnp.einsum("mab,bm->am", upp, nxt, precision=HIGH)
        cur = jnp.einsum("mab,bm->am", piv, inner, precision=HIGH)
        return (cur, cur)

    _, zseq = lax.scan(backward, start, (yseq, useq, pseq), reverse=True)
    return jnp.moveaxis(zseq, 0, 2)


def table_positions(columns, nfaces):
    nspan, nplane = lax.axis_size("span"), lax.axis_size("plane")
    my_span, my_plane = lax.axis_index("span"), lax.axis_index("plane")
    device_of = columns // nfaces
    span_of = device_of // nplane
    plane_of = device_of % nplane
    dspan = (span_of - my_span + 1 + nspan) % nspan - 1
    dplane = plane_of - my_plane
    selector = jnp.where(
        dspan == -1,
        1,
        jnp.where(dspan == 1, 2, jnp.where(dplane == -1, 3, jnp.where(dplane == 1, 4, 0))),
    )
    return selector * nfaces + columns % nfaces


def step_by_step(rhs, blocks, columns, line_slot, line_lower, line_upper, pivot_inv):
    width, nfaces = rhs.shape
    nblocks = columns.shape[0]
    nplane = lax.axis_size("plane")
    position = table_positions(columns, nfaces)
    slot = line_slot[0]
    lines_group = nfaces // P_SIZE
    owned = lines_group // nplane
    length = P_SIZE * nplane
    lower = to_sequence(line_lower, owned, length, width)
    upper = to_sequence(line_upper, owned, length, width)
    pivot = to_sequence(pivot_inv, owned, length, width)
    shaped_blocks = blocks.reshape(nfaces, nblocks, width, width)

    def apply_a(vec):
        shaped = vec.reshape(width, 1, 1, nfaces)
        span_side = with_halo(shaped, (("span", 1),), 1, True)
        plane_side = with_halo(shaped, (("plane", 2),), 1, False)
        below = plane_side[:, 0, 0]
        above = plane_side[:, 0, 2]
        table = jnp.concatenate([vec, span_side[:, 0, 0], span_side[:, 2, 0], below, above], axis=1)
        return jnp.einsum("ikab,bki->ai", shaped_blocks, table[:, position], precision=HIGH)

    def apply_m(vec):
        pieces = vec[:, slot].reshape(width, lines_group, P_SIZE)
        whole = lax.all_to_all(pieces, "plane", split_axis=1, concat_axis=2, tiled=True)
        solved = line_solve(whole, lower, upper, pivot)
        back = lax.all_to_all(solved, "plane", split_axis=2, concat_axis=1, tiled=True)
        return jnp.zeros_like(vec).at[:, slot].set(back.reshape(width, nfaces))

    beta = jnp.sqrt(lax.psum(jnp.sum(rhs * rhs), ("span", "plane")) + EPS)
    basis = [rhs / beta]
    hcols = []
    for step in range(ITERS):
        wvec = apply_a(apply_m(basis[step]))
        stacked = jnp.stack(basis)
        hvals = lax.psum(jnp.einsum("jai,ai->j", stacked, wvec, precision=HIGH), ("span", "plane"))
        wvec = wvec - jnp.einsum("j,jai->ai", hvals, stacked, precision=HIGH)
        hnext = jnp.sqrt(lax.psum(jnp.sum(wvec * wvec), ("span", "plane")) + EPS)
        basis.append(wvec / hnext)
        hcols.append(jnp.concatenate([hvals, hnext[None], jnp.zeros((ITERS - step - 1,), F32)]))
    hmat = jnp.stack(hcols, axis=1)
    factor = jnp.linalg.cholesky(jnp.dot(hmat.T, hmat, precision=HIGH))
    coef = small_solve(factor, beta * hmat[0])
    update = jnp.einsum("j,jai->ai", coef, jnp.stack(basis[:ITERS]), precision=HIGH)
    solution = apply_m(update)
    return solution, rhs - apply_a(solution)


def partner(me, k, size):
    if size & (size - 1) == 0:
        return me ^ k, me ^ k
    return (me + k) % size, (me + size - k) % size


def exchange(x, axis, k):
    size = lax.axis_size(axis)
    return lax.ppermute(x, axis, [(i, partner(i, k, size)[0]) for i in range(size)])


def split(x, parts):
    out = []
    for _ in range(parts):
        out.append(x.astype(BF16).astype(F32))
        x = x - out[-1]
    return jnp.concatenate(out, axis=0)


def start_kernel(nplane, slot_ref, u_ref, *outs):
    nfaces, width = u_ref.shape
    per = nfaces // nplane
    me = lax.axis_index("plane")
    lane = lax.broadcasted_iota(jnp.int32, (1, width), 1)
    tail = jnp.zeros((1, width), F32)
    for t in range(nfaces):
        tail = jnp.where(lane == t, slot_ref[0, t].astype(F32), tail)
    for k in range(nplane):
        to, _ = partner(me, k, nplane)
        for i in range(per):
            outs[k][pl.ds(i, 1), :] = u_ref[pl.ds(slot_ref[0, to * per + i], 1), :]
        outs[k][pl.ds(per, 1), :] = tail


def square_kernel(length, low, upp, piv, low_out, upp_out, piv_out):
    nrows, width = low.shape[0], low_out.shape[1]
    chunk = math.lcm(width, 128)
    for src, dst in ((low, low_out), (upp, upp_out), (piv, piv_out)):
        for c in range(width * width // chunk):
            piece = src[:, c * chunk : (c + 1) * chunk]
            for r in range(chunk // width):
                a = c * (chunk // width) + r
                dst[pl.ds(a, nrows, stride=width), :] = piece[:, r * width : (r + 1) * width]
    for at in range(nrows):
        here = slice(at * width, (at + 1) * width)
        if at % length % 2 == 0 and at % length:
            low_out[here, :] = low_out[here, :].T
        piv_out[here, :] = piv_out[here, :].T


def line_kernel(nplane, nlines, *refs):
    msgs, (low, upp, piv_t, z_ref, r_scr) = refs[:nplane], refs[nplane:]
    width = z_ref.shape[1]
    length = z_ref.shape[0] // nlines
    me = lax.axis_index("plane")
    for k in range(nplane):
        _, source = partner(me, k, nplane)
        for m in range(nlines):
            for q in range(P_SIZE):
                r_scr[m, pl.ds(source * P_SIZE + q, 1), :] = msgs[k][pl.ds(m * P_SIZE + q, 1), :]
    eye = lax.broadcasted_iota(jnp.int32, (width, width), 0) == lax.broadcasted_iota(jnp.int32, (width, width), 1)

    def column(row):
        return jnp.sum(jnp.where(eye, row, 0.0), axis=1, keepdims=True)

    rows = [[r_scr[m, pl.ds(j, 1), :] for m in range(nlines)] for j in range(length)]
    y_cols = [[None] * nlines for _ in range(length)]
    carry = [None] * nlines
    for j in range(length):
        for m in range(nlines):
            at = m * length + j
            if j == 0:
                carry[m] = rows[j][m]
            elif j % 2:
                carry[m] = column(rows[j][m]) - jnp.sum(low[at] * carry[m], axis=1, keepdims=True)
            else:
                carry[m] = rows[j][m] - jnp.sum(low[at] * carry[m], axis=0, keepdims=True)
            y_cols[j][m] = carry[m] if j % 2 else column(carry[m])
    after = [None] * nlines
    for j in reversed(range(length)):
        for m in range(nlines):
            at = m * length + j
            inner = y_cols[j][m]
            if j < length - 1:
                inner = inner - jnp.sum(upp[at] * after[m], axis=1, keepdims=True)
            after[m] = jnp.sum(piv_t[at] * inner, axis=0, keepdims=True)
            z_ref[pl.ds(at, 1), :] = after[m]


def faces_kernel(nplane, choose, *refs):
    solved, (mine_ref, sides_ref) = refs[:nplane], refs[nplane:]
    nfaces = mine_ref.shape[0]
    table = split(jnp.concatenate([s[...] for s in solved], axis=0), 3).astype(BF16)
    out = jnp.dot(choose[...], table, preferred_element_type=F32)
    mine_ref[...] = out[:nfaces]
    sides_ref[...] = out[nfaces:]


def fetch_and_apply(ks, blocks, pick, seg, faces, scratch):
    buf, x_scr, acc, sems = scratch
    nfaces, width = faces[0].shape
    area = width * width
    chunk = seg.shape[0]
    copies = chunk // width

    def fetch(n):
        return pltpu.make_async_copy(
            blocks.at[:, pl.ds(ks[n] * area, area)], buf.at[:, pl.ds(n * area, area)], sems.at[n]
        )

    for n in range(len(ks)):
        fetch(n).start()
    both = split(jnp.concatenate([f[...] for f in faces], axis=0), 2)
    wide = jnp.concatenate([both] * copies, axis=1).astype(BF16)
    x_scr[...] = jnp.dot(pick[...], wide, preferred_element_type=F32)
    group = 3
    for first in range(0, len(ks), group):
        some = range(first, min(first + group, len(ks)))
        for n in some:
            fetch(n).wait()
        for v in range(0, chunk, 128):
            xs = [x_scr[n * nfaces : (n + 1) * nfaces, v : v + 128] for n in some]
            for c in range(area // chunk):
                at = c * chunk + v
                total = None if first == 0 else acc[:, at : at + 128]
                for n, x in zip(some, xs):
                    term = buf[:, n * area + at : n * area + at + 128] * x
                    total = term if total is None else total + term
                acc[:, at : at + 128] = total
    parts = []
    for c in range(area // chunk):
        value = acc[:, c * chunk : (c + 1) * chunk]
        high = value.astype(BF16)
        parts += [high, (value - high.astype(F32)).astype(BF16)]
    sums = jnp.dot(jnp.concatenate(parts, axis=0), seg[...], preferred_element_type=F32)
    place = lax.broadcasted_iota(jnp.int32, (nfaces, seg.shape[1]), 1) // copies
    total = jnp.zeros((nfaces, seg.shape[1]), F32)
    for c in range(area // chunk):
        at = 2 * c * nfaces
        total = total + jnp.where(place == c, sums[at : at + nfaces] + sums[at + nfaces : at + 2 * nfaces], 0.0)
    return total[:, :width]


def near_kernel(ks, blocks, pick, seg, mine, sides, out_ref, *scratch):
    out_ref[...] = fetch_and_apply(ks, blocks, pick, seg, [mine, sides], scratch)


def far_kernel(ks, nplane, last, *refs):
    (blocks, slot, pick, seg, pair, other, near), refs = refs[:7], refs[7:]
    nold = ITERS if last else 1
    olds, refs = refs[:nold], refs[nold:]
    next_ref, refs = refs[0], refs[1:]
    nfaces = next_ref.shape[0]
    if not last:
        slot_scr, slot_sem = refs[-2:]
        refs = refs[:-2]
        slots = pltpu.make_async_copy(slot, slot_scr, slot_sem)
        slots.start()
    far = fetch_and_apply(ks, blocks, pick, seg, [pair, other], refs[-4:])
    u_next = near[...] + far - SHIFT * olds[-1][...]
    next_ref[...] = u_next
    if last:
        gram_ref = refs[0]
        basis = [old[...] for old in olds] + [u_next]
        lane = lax.broadcasted_iota(jnp.int32, gram_ref.shape, 1)
        gram, at = jnp.zeros(gram_ref.shape, F32), 0
        for i in range(ITERS + 1):
            for j in range(i, ITERS + 1):
                value = jnp.sum(jnp.sum(basis[i] * basis[j], axis=0, keepdims=True), axis=1, keepdims=True)
                gram, at = jnp.where(lane == at, value, gram), at + 1
        gram_ref[...] = gram
    else:
        per = nfaces // nplane
        me = lax.axis_index("plane")
        slots.wait()
        for k in range(nplane):
            to, _ = partner(me, k, nplane)
            for i in range(per):
                refs[k][pl.ds(i, 1), :] = next_ref[pl.ds(slot_scr[0, to * per + i], 1), :]


def finish_kernel(gram_ref, *refs):
    us, zs = refs[: ITERS + 1], refs[ITERS + 1 : 2 * ITERS + 1]
    sol_ref, res_ref, ok_ref = refs[2 * ITERS + 1 :]
    width = sol_ref.shape[1]
    lane = lax.broadcasted_iota(jnp.int32, gram_ref.shape, 1)
    gram, at = {}, 0
    for i in range(ITERS + 1):
        for j in range(i, ITERS + 1):
            value = jnp.sum(jnp.where(lane == at, gram_ref[...], 0.0), axis=1, keepdims=True)
            gram[i, j] = gram[j, i] = jnp.broadcast_to(value, gram_ref.shape)
            at += 1
    largest = functools.reduce(jnp.maximum, [jnp.abs(g) for g in gram.values()])
    ok = largest < 1e30
    beta = jnp.sqrt(gram[0, 0] + EPS)
    basis = [[1.0 / beta]]
    hmat = {}
    for step in range(ITERS):
        own = basis[step]
        wvec = [SHIFT * own[0]] + [own[i] + SHIFT * own[i + 1] for i in range(step)] + [own[step]]
        images = [sum(gram[i, j] * wvec[j] for j in range(step + 2)) for i in range(step + 1)]
        for i in range(step + 1):
            hmat[i, step] = sum(basis[i][m] * images[m] for m in range(i + 1))
        for i in range(step + 1):
            for m in range(i + 1):
                wvec[m] = wvec[m] - hmat[i, step] * basis[i][m]
        terms = [wvec[i] * wvec[j] * gram[i, j] for i in range(step + 2) for j in range(step + 2)]
        square = jnp.maximum(sum(terms), 0.0)
        ok = ok & (square + EPS >= 2e-3 * sum(jnp.abs(term) for term in terms))
        hmat[step + 1, step] = jnp.sqrt(square + EPS)
        scale = 1.0 / hmat[step + 1, step]
        basis.append([w * scale for w in wvec])
    normal = {
        (i, j): sum(hmat[m, i] * hmat[m, j] for m in range(j + 2) if (m, i) in hmat and (m, j) in hmat)
        for i in range(ITERS)
        for j in range(i + 1)
    }
    factor, inverse = {}, []
    for j in range(ITERS):
        diag = jnp.sqrt(normal[j, j] - sum(factor[j, m] * factor[j, m] for m in range(j)))
        inverse.append(1.0 / diag)
        for i in range(j + 1, ITERS):
            factor[i, j] = (normal[i, j] - sum(factor[i, m] * factor[j, m] for m in range(j))) * inverse[j]
    forward = []
    for i in range(ITERS):
        forward.append((beta * hmat[0, i] - sum(factor[i, m] * forward[m] for m in range(i))) * inverse[i])
    coef = [None] * ITERS
    for i in reversed(range(ITERS)):
        coef[i] = (forward[i] - sum(factor[m, i] * coef[m] for m in range(i + 1, ITERS))) * inverse[i]
    mix = [sum(coef[s] * basis[s][m] for s in range(m, ITERS))[:, :width] for m in range(ITERS)]
    sol_ref[...] = sum(mix[m] * zs[m][...] for m in range(ITERS))
    image = sum(mix[m] * (us[m + 1][...] + SHIFT * us[m][...]) for m in range(ITERS))
    res_ref[...] = us[0][...] - image
    ok = ok & (functools.reduce(jnp.maximum, [jnp.abs(c) for c in coef]) < 1e30)
    ok_ref[...] = jnp.where(ok, 1.0, 0.0)


def call(kernel, args, outs, spaces=None, scratch=(), flops=0, pinned=True, ready=True):
    spaces = [pltpu.VMEM] * len(args) if spaces is None else spaces
    if ready:
        args = [pltpu.with_memory_space_constraint(x, s) if s is pltpu.VMEM else x for x, s in zip(args, spaces)]
    size = sum(x.dtype.itemsize * math.prod(x.shape) for x in args)
    return pl.pallas_call(
        kernel,
        out_shape=[pltpu.VMEM(shape, F32) if pinned else jax.ShapeDtypeStruct(shape, F32) for shape in outs],
        in_specs=[pl.BlockSpec(memory_space=s) for s in spaces],
        out_specs=[pl.BlockSpec(memory_space=pltpu.VMEM) for _ in outs],
        scratch_shapes=scratch,
        compiler_params=pltpu.CompilerParams(vmem_limit_bytes=VMEM_LIMIT),
        cost_estimate=pl.CostEstimate(flops=flops, bytes_accessed=size, transcendentals=0),
    )(*args)


def add_up(x):
    count = lax.axis_size("span") * lax.axis_size("plane")
    if count & (count - 1):
        return lax.psum(x, ("span", "plane"))
    step = 1
    while step < count:
        x = x + lax.ppermute(x, ("span", "plane"), [(i, i ^ step) for i in range(count)])
        step *= 2
    return x


def one_hot(index, count, copies):
    lanes = lax.broadcasted_iota(jnp.int32, (1, copies * count), 1) % count
    return (lanes == index.reshape(-1, 1)).astype(BF16)


def on_device(rhs, blocks, columns, line_slot, line_lower, line_upper, pivot_inv):
    width, nfaces = rhs.shape
    nblocks = columns.shape[0]
    nspan, nplane = lax.axis_size("span"), lax.axis_size("plane")
    owned = nfaces // P_SIZE // nplane
    length = P_SIZE * nplane
    per = owned * P_SIZE
    me = lax.axis_index("plane")
    shape = (nfaces, width)
    area = width * width

    us = [rhs.T]
    send = call(
        functools.partial(start_kernel, nplane),
        [line_slot, us[0]],
        [(per + 1, width)] * nplane,
        [pltpu.SMEM, pltpu.VMEM],
        ready=False,
    )

    if nspan % 2 == 0:
        pairs = [(i, i ^ 1) for i in range(nspan)]
        others = [(i, (i + 1 if i % 2 else i - 1) % nspan) for i in range(nspan)]
        before_first = lax.axis_index("span") % 2 == 1
    else:
        pairs = [(i, (i + 1) % nspan) for i in range(nspan)]
        others = [(i, (i - 1) % nspan) for i in range(nspan)]
        before_first = True

    chunk = math.lcm(width, 128)
    seg = (np.arange(chunk)[:, None] // width == np.arange(128)[None, :] % (chunk // width)).astype(np.float32)
    seg = jnp.asarray(seg, BF16)

    factors = call(
        functools.partial(square_kernel, length),
        [line_lower, line_upper, pivot_inv],
        [(nfaces * width, width)] * 3,
        flops=nfaces * area,
        ready=False,
    )
    factors = [x.reshape(nfaces, width, width) for x in factors]

    def scratch(count):
        return [
            pltpu.VMEM((nfaces, count * area), F32),
            pltpu.VMEM((count * nfaces, chunk), F32),
            pltpu.VMEM((nfaces, area), F32),
            pltpu.SemaphoreType.DMA((count,)),
        ]

    near_ks = [0] + list(range(3, nblocks))
    far_ks = [1, 2] + list(range(5, nblocks))
    zs = []
    choose = near_pick = far_pick = None
    for step in range(ITERS):
        got = [send[0]] + [exchange(send[k], "plane", k) for k in range(1, nplane)]
        if step == 0:
            owners = jnp.stack([jnp.asarray(partner(me, k, nplane)[1], jnp.int32) for k in range(nplane)])
            known = jnp.concatenate([g[per:, :nfaces] for g in got], axis=0).astype(jnp.int32)
            places = jnp.arange(nplane, dtype=jnp.int32)
            slots = jnp.sum(jnp.where(owners[None, :, None] == places[:, None, None], known[None], 0), axis=1)
            slots = slots.reshape(1, nplane, nplane, owned, P_SIZE)
            by_owner = jnp.where(owners[:, None, None, None, None] == places[None, None, :, None, None], slots, 0)
            face_row = jnp.swapaxes(jnp.sum(by_owner, axis=2), 1, 2).reshape(1, 1, -1)
            device_row = jnp.broadcast_to(places[None, None, :, None], (nplane, owned, nplane, P_SIZE)).reshape(1, 1, -1)
            there = jnp.clip(me + jnp.array([0, -1, 1], jnp.int32), 0, nplane - 1)[:, None, None]
            choose = (device_row == there) & (face_row == jnp.arange(nfaces, dtype=jnp.int32)[None, :, None])
            choose = jnp.tile(choose.reshape(3 * nfaces, -1), (1, 3)).astype(BF16)
        (solved,) = call(
            functools.partial(line_kernel, nplane, owned),
            [*got, *factors],
            [shape],
            scratch=[pltpu.VMEM((owned, length, width), F32)],
            flops=6 * nfaces * area,
        )
        if step == 0:
            position = table_positions(lax.optimization_barrier((columns, solved))[0], nfaces)
            selector, face = position // nfaces, position % nfaces
            near_at = jnp.where(selector == 0, 0, jnp.where(selector >= 3, selector - 2, -nfaces)) * nfaces + face
            far_at = jnp.where(
                (selector == 1) | (selector == 2), jnp.where((selector == 1) == before_first, 0, 1), -nfaces
            ) * nfaces + face
            near_pick = one_hot(jnp.concatenate([near_at[:1], near_at[3:]], axis=0), 3 * nfaces, 2)
            far_pick = one_hot(jnp.concatenate([far_at[1:3], far_at[5:]], axis=0), 2 * nfaces, 2)
        pieces = [solved]
        for k in range(1, nplane):
            relayed = k % 2 and k > 1 and nplane & (nplane - 1) == 0
            pieces.append(exchange(pieces[k - 1], "plane", 1) if relayed else exchange(solved, "plane", k))
        mine, sides = call(
            functools.partial(faces_kernel, nplane), [choose, *pieces], [shape, (2 * nfaces, width)]
        )
        zs.append(mine)
        other = lax.ppermute(mine, "span", others)
        pair = lax.ppermute(mine, "span", pairs)
        (near,) = call(
            functools.partial(near_kernel, near_ks),
            [blocks, near_pick, seg, mine, sides],
            [shape],
            [pl.ANY] + [pltpu.VMEM] * 4,
            scratch(len(near_ks)),
            flops=2 * len(near_ks) * nfaces * area,
        )
        last = step == ITERS - 1
        args = [blocks, line_slot, far_pick, seg, pair, other, near, *(us if last else us[-1:])]
        out = call(
            functools.partial(far_kernel, far_ks, nplane, last),
            args,
            [shape] + ([(1, 128)] if last else [(per, width)] * nplane),
            [pl.ANY] + [pltpu.VMEM] * (len(args) - 1),
            scratch(len(far_ks)) + ([] if last else [pltpu.SMEM(line_slot.shape, jnp.int32), pltpu.SemaphoreType.DMA]),
            flops=2 * len(far_ks) * nfaces * area,
        )
        us.append(out[0])
        send = out[1:]
    gram = add_up(send[0])
    sol, res, ok = call(finish_kernel, [gram, *us, *zs], [shape, shape, (1, 128)], pinned=False)
    given = (rhs, blocks, columns, line_slot, line_lower, line_upper, pivot_inv)
    _, sol, res = lax.while_loop(
        lambda state: state[0], lambda _: (jnp.array(False), *step_by_step(*given)), (ok[0, 0] < 0.5, sol.T, res.T)
    )
    return sol, res


def solution(mesh):
    both = ("span", "plane")
    return jax.shard_map(
        on_device,
        mesh=mesh,
        in_specs=(
            P(None, both),
            P(both, None),
            P(None, both),
            P(both, None),
            P(both, None),
            P(both, None),
            P(both, None),
        ),
        out_specs=(P(None, both), P(None, both)),
        check_vma=False,
    )
```

```python
import functools
import math

import jax
import jax.numpy as jnp
import numpy as np
from jax import lax
from jax.experimental import pallas as pl
from jax.experimental.pallas import tpu as pltpu
from jax.sharding import PartitionSpec as P

ITERS = 3
P_SIZE = 2
SHIFT = 2.0
EPS = 1e-6
VMEM_LIMIT = 16 * 1024 * 1024
HIGH = lax.Precision.HIGHEST
F32, BF16 = jnp.float32, jnp.bfloat16


def with_halo(x, sides, width, wrap):
    for axis, dim in sides:
        size, length = (lax.axis_size(axis), x.shape[dim])
        up = [(i, (i + 1) % size) for i in range(size if wrap else size - 1)]
        down = [(j, i) for i, j in up]
        last = lax.slice_in_dim(x, length - width, length, axis=dim)
        first = lax.slice_in_dim(x, 0, width, axis=dim)
        before = lax.ppermute(last, axis, up)
        after = lax.ppermute(first, axis, down)
        x = jnp.concatenate([before, x, after], axis=dim)
    return x


def small_solve(factor, target):
    extent = target.shape[0]
    forward_vals = []
    for row in range(extent):
        running = target[row]
        for inner in range(row):
            running = running - factor[row, inner] * forward_vals[inner]
        forward_vals.append(running / factor[row, row])
    backward_vals = [None] * extent
    for row in reversed(range(extent)):
        running = forward_vals[row]
        for inner in range(row + 1, extent):
            running = running - factor[inner, row] * backward_vals[inner]
        backward_vals[row] = running / factor[row, row]
    return jnp.stack(backward_vals)


def to_sequence(factor_rows, nlines, length, width):
    return jnp.swapaxes(factor_rows.reshape(nlines, length, width, width), 0, 1)


def line_solve(rhs_lines, lseq, useq, pseq):
    rseq = jnp.moveaxis(rhs_lines, 2, 0)

    def forward(prev, items):
        right, low = items
        cur = right - jnp.einsum("mab,bm->am", low, prev, precision=HIGH)
        return (cur, cur)

    start = jnp.zeros(rseq.shape[1:], F32)
    _, yseq = lax.scan(forward, start, (rseq, lseq))

    def backward(nxt, items):
        yval, upp, piv = items
        inner = yval - jnp.einsum("mab,bm->am", upp, nxt, precision=HIGH)
        cur = jnp.einsum("mab,bm->am", piv, inner, precision=HIGH)
        return (cur, cur)

    _, zseq = lax.scan(backward, start, (yseq, useq, pseq), reverse=True)
    return jnp.moveaxis(zseq, 0, 2)


def table_positions(columns, nfaces):
    nspan, nplane = lax.axis_size("span"), lax.axis_size("plane")
    my_span, my_plane = lax.axis_index("span"), lax.axis_index("plane")
    device_of = columns // nfaces
    span_of = device_of // nplane
    plane_of = device_of % nplane
    dspan = (span_of - my_span + 1 + nspan) % nspan - 1
    dplane = plane_of - my_plane
    selector = jnp.where(
        dspan == -1,
        1,
        jnp.where(dspan == 1, 2, jnp.where(dplane == -1, 3, jnp.where(dplane == 1, 4, 0))),
    )
    return selector * nfaces + columns % nfaces


def step_by_step(rhs, blocks, columns, line_slot, line_lower, line_upper, pivot_inv):
    width, nfaces = rhs.shape
    nblocks = columns.shape[0]
    nplane = lax.axis_size("plane")
    position = table_positions(columns, nfaces)
    slot = line_slot[0]
    lines_group = nfaces // P_SIZE
    owned = lines_group // nplane
    length = P_SIZE * nplane
    lower = to_sequence(line_lower, owned, length, width)
    upper = to_sequence(line_upper, owned, length, width)
    pivot = to_sequence(pivot_inv, owned, length, width)
    shaped_blocks = blocks.reshape(nfaces, nblocks, width, width)

    def apply_a(vec):
        shaped = vec.reshape(width, 1, 1, nfaces)
        span_side = with_halo(shaped, (("span", 1),), 1, True)
        plane_side = with_halo(shaped, (("plane", 2),), 1, False)
        below = plane_side[:, 0, 0]
        above = plane_side[:, 0, 2]
        table = jnp.concatenate([vec, span_side[:, 0, 0], span_side[:, 2, 0], below, above], axis=1)
        return jnp.einsum("ikab,bki->ai", shaped_blocks, table[:, position], precision=HIGH)

    def apply_m(vec):
        pieces = vec[:, slot].reshape(width, lines_group, P_SIZE)
        whole = lax.all_to_all(pieces, "plane", split_axis=1, concat_axis=2, tiled=True)
        solved = line_solve(whole, lower, upper, pivot)
        back = lax.all_to_all(solved, "plane", split_axis=2, concat_axis=1, tiled=True)
        return jnp.zeros_like(vec).at[:, slot].set(back.reshape(width, nfaces))

    beta = jnp.sqrt(lax.psum(jnp.sum(rhs * rhs), ("span", "plane")) + EPS)
    basis = [rhs / beta]
    hcols = []
    for step in range(ITERS):
        wvec = apply_a(apply_m(basis[step]))
        stacked = jnp.stack(basis)
        hvals = lax.psum(jnp.einsum("jai,ai->j", stacked, wvec, precision=HIGH), ("span", "plane"))
        wvec = wvec - jnp.einsum("j,jai->ai", hvals, stacked, precision=HIGH)
        hnext = jnp.sqrt(lax.psum(jnp.sum(wvec * wvec), ("span", "plane")) + EPS)
        basis.append(wvec / hnext)
        hcols.append(jnp.concatenate([hvals, hnext[None], jnp.zeros((ITERS - step - 1,), F32)]))
    hmat = jnp.stack(hcols, axis=1)
    factor = jnp.linalg.cholesky(jnp.dot(hmat.T, hmat, precision=HIGH))
    coef = small_solve(factor, beta * hmat[0])
    update = jnp.einsum("j,jai->ai", coef, jnp.stack(basis[:ITERS]), precision=HIGH)
    solution = apply_m(update)
    return solution, rhs - apply_a(solution)


def partner(me, k, size):
    if size & (size - 1) == 0:
        return me ^ k, me ^ k
    return (me + k) % size, (me + size - k) % size


def exchange(x, axis, k):
    size = lax.axis_size(axis)
    return lax.ppermute(x, axis, [(i, partner(i, k, size)[0]) for i in range(size)])


def split(x, parts):
    out = []
    for _ in range(parts):
        out.append(x.astype(BF16).astype(F32))
        x = x - out[-1]
    return jnp.concatenate(out, axis=0)


def start_kernel(nplane, slot_ref, u_ref, *outs):
    per = outs[0].shape[0]
    me = lax.axis_index("plane")
    for k in range(nplane):
        to, _ = partner(me, k, nplane)
        for i in range(per):
            outs[k][pl.ds(i, 1), :] = u_ref[pl.ds(slot_ref[0, to * per + i], 1), :]


def square_kernel(length, low, upp, piv, low_out, upp_out, piv_out):
    nrows, width = low.shape[0], low_out.shape[1]
    chunk = math.lcm(width, 128)
    for src, dst in ((low, low_out), (upp, upp_out), (piv, piv_out)):
        for c in range(width * width // chunk):
            piece = src[:, c * chunk : (c + 1) * chunk]
            for r in range(chunk // width):
                a = c * (chunk // width) + r
                dst[pl.ds(a, nrows, stride=width), :] = piece[:, r * width : (r + 1) * width]
    for at in range(nrows):
        here = slice(at * width, (at + 1) * width)
        if at % length % 2 == 0 and at % length:
            low_out[here, :] = low_out[here, :].T
        piv_out[here, :] = piv_out[here, :].T


def line_kernel(nplane, nlines, *refs):
    msgs, (low, upp, piv_t), outs, (r_scr, z_scr) = refs[:nplane], refs[nplane:-nplane-2], refs[-nplane-2:-2], refs[-2:]
    _, length, width = r_scr.shape
    me = lax.axis_index("plane")
    for k in range(nplane):
        _, source = partner(me, k, nplane)
        for m in range(nlines):
            for q in range(P_SIZE):
                r_scr[m, pl.ds(source * P_SIZE + q, 1), :] = msgs[k][pl.ds(m * P_SIZE + q, 1), :]
    eye = lax.broadcasted_iota(jnp.int32, (width, width), 0) == lax.broadcasted_iota(jnp.int32, (width, width), 1)

    def column(row):
        return jnp.sum(jnp.where(eye, row, 0.0), axis=1, keepdims=True)

    rows = [[r_scr[m, pl.ds(j, 1), :] for m in range(nlines)] for j in range(length)]
    y_cols = [[None] * nlines for _ in range(length)]
    carry = [None] * nlines
    for j in range(length):
        for m in range(nlines):
            at = m * length + j
            if j == 0:
                carry[m] = rows[j][m]
            elif j % 2:
                carry[m] = column(rows[j][m]) - jnp.sum(low[at] * carry[m], axis=1, keepdims=True)
            else:
                carry[m] = rows[j][m] - jnp.sum(low[at] * carry[m], axis=0, keepdims=True)
            y_cols[j][m] = carry[m] if j % 2 else column(carry[m])
    after = [None] * nlines
    for j in reversed(range(length)):
        for m in range(nlines):
            at = m * length + j
            inner = y_cols[j][m]
            if j < length - 1:
                inner = inner - jnp.sum(upp[at] * after[m], axis=1, keepdims=True)
            after[m] = jnp.sum(piv_t[at] * inner, axis=0, keepdims=True)
            z_scr[m, pl.ds(j, 1), :] = after[m]
    for k in range(nplane):
        to, _ = partner(me, k, nplane)
        for m in range(nlines):
            for q in range(P_SIZE):
                outs[k][pl.ds(m * P_SIZE + q, 1), :] = z_scr[m, pl.ds(to * P_SIZE + q, 1), :]


def faces_kernel(choose, *refs):
    solved, mine_ref = refs[:-1], refs[-1]
    table = split(jnp.concatenate([s[...] for s in solved], axis=0), 3).astype(BF16)
    mine_ref[...] = jnp.dot(choose[...], table, preferred_element_type=F32)


def apply_kernel(nplane, nblocks, last, *refs):
    (blocks, slot, pick), faces, refs = refs[:3], refs[3:8], refs[8:]
    nold = ITERS if last else 1
    olds, refs = refs[:nold], refs[nold:]
    next_ref, outs, (buf, x_scr, parts, sems, slot_scr, slot_sem) = refs[0], refs[1:-6], refs[-6:]
    nfaces, width = faces[0].shape
    area = width * width
    chunk = math.lcm(width, 128)
    copies, count = chunk // width, area // chunk
    lane = lax.broadcasted_iota(jnp.int32, (1, 128), 1)

    bounds = [0, 3 * count // 10, 6 * count // 10, 8 * count // 10, count]
    bounds = sorted(set(bounds))
    copies_of = []
    for g, (first, end) in enumerate(zip(bounds, bounds[1:])):
        some = []
        for k in range(nblocks):
            where = pl.ds(k * area + first * chunk, (end - first) * chunk)
            some.append(pltpu.make_async_copy(blocks.at[:, where], buf.at[:, where], sems.at[g, k]))
            some[-1].start()
        copies_of.append(some)
    if not last:
        slots = pltpu.make_async_copy(slot, slot_scr, slot_sem)
        slots.start()

    both = split(jnp.concatenate([f[...] for f in faces], axis=0), 2)
    wide = jnp.concatenate([both] * copies, axis=1).astype(BF16)
    x_scr[...] = jnp.dot(pick[...], wide, preferred_element_type=F32)
    seg = [jnp.broadcast_to(jnp.where(lane % copies == r, 1.0, 0.0), (width, 128)) for r in range(copies)]
    seg = jnp.concatenate(seg, axis=0).astype(BF16)
    total = jnp.zeros((nfaces, 128), F32)
    for first, end, some in zip(bounds, bounds[1:], copies_of):
        for copy in some:
            copy.wait()
        for v in range(0, chunk, 128):
            xs = [x_scr[k * nfaces : (k + 1) * nfaces, v : v + 128] for k in range(nblocks)]
            for c in range(first, end):
                acc = None
                for k in range(nblocks):
                    at = k * area + c * chunk + v
                    term = buf[:, at : at + 128] * xs[k]
                    acc = term if acc is None else acc + term
                high = acc.astype(BF16)
                at = 2 * c * nfaces
                parts[at : at + nfaces, v : v + 128] = high
                parts[at + nfaces : at + 2 * nfaces, v : v + 128] = (acc - high.astype(F32)).astype(BF16)
        base = 2 * first * nfaces
        sums = jnp.dot(parts[base : 2 * end * nfaces, :], seg, preferred_element_type=F32)
        for c in range(first, end):
            at = 2 * c * nfaces - base
            both_sums = sums[at : at + nfaces] + sums[at + nfaces : at + 2 * nfaces]
            total = total + jnp.where(lane // copies == c, both_sums, 0.0)
    u_next = total[:, :width] - SHIFT * olds[-1][...]
    next_ref[...] = u_next
    if last:
        gram_ref = outs[0]
        basis = [old[...] for old in olds] + [u_next]
        gram, at = jnp.zeros(gram_ref.shape, F32), 0
        for i in range(ITERS + 1):
            for j in range(i, ITERS + 1):
                value = jnp.sum(jnp.sum(basis[i] * basis[j], axis=0, keepdims=True), axis=1, keepdims=True)
                gram, at = jnp.where(lane == at, value, gram), at + 1
        gram_ref[...] = gram
    else:
        per = nfaces // nplane
        me = lax.axis_index("plane")
        slots.wait()
        for k in range(nplane):
            to, _ = partner(me, k, nplane)
            for i in range(per):
                outs[k][pl.ds(i, 1), :] = next_ref[pl.ds(slot_scr[0, to * per + i], 1), :]


def finish_kernel(gram_ref, *refs):
    us, zs = refs[: ITERS + 1], refs[ITERS + 1 : 2 * ITERS + 1]
    sol_ref, res_ref, ok_ref = refs[2 * ITERS + 1 :]
    width = sol_ref.shape[1]
    lane = lax.broadcasted_iota(jnp.int32, gram_ref.shape, 1)
    gram, at = {}, 0
    for i in range(ITERS + 1):
        for j in range(i, ITERS + 1):
            value = jnp.sum(jnp.where(lane == at, gram_ref[...], 0.0), axis=1, keepdims=True)
            gram[i, j] = gram[j, i] = jnp.broadcast_to(value, gram_ref.shape)
            at += 1
    largest = functools.reduce(jnp.maximum, [jnp.abs(g) for g in gram.values()])
    ok = largest < 1e30
    beta = jnp.sqrt(gram[0, 0] + EPS)
    basis = [[1.0 / beta]]
    hmat = {}
    for step in range(ITERS):
        own = basis[step]
        wvec = [SHIFT * own[0]] + [own[i] + SHIFT * own[i + 1] for i in range(step)] + [own[step]]
        images = [sum(gram[i, j] * wvec[j] for j in range(step + 2)) for i in range(step + 1)]
        for i in range(step + 1):
            hmat[i, step] = sum(basis[i][m] * images[m] for m in range(i + 1))
        for i in range(step + 1):
            for m in range(i + 1):
                wvec[m] = wvec[m] - hmat[i, step] * basis[i][m]
        terms = [wvec[i] * wvec[j] * gram[i, j] for i in range(step + 2) for j in range(step + 2)]
        square = jnp.maximum(sum(terms), 0.0)
        ok = ok & (square + EPS >= 2e-3 * sum(jnp.abs(term) for term in terms))
        hmat[step + 1, step] = jnp.sqrt(square + EPS)
        scale = 1.0 / hmat[step + 1, step]
        basis.append([w * scale for w in wvec])
    normal = {
        (i, j): sum(hmat[m, i] * hmat[m, j] for m in range(j + 2) if (m, i) in hmat and (m, j) in hmat)
        for i in range(ITERS)
        for j in range(i + 1)
    }
    factor, inverse = {}, []
    for j in range(ITERS):
        diag = jnp.sqrt(normal[j, j] - sum(factor[j, m] * factor[j, m] for m in range(j)))
        inverse.append(1.0 / diag)
        for i in range(j + 1, ITERS):
            factor[i, j] = (normal[i, j] - sum(factor[i, m] * factor[j, m] for m in range(j))) * inverse[j]
    forward = []
    for i in range(ITERS):
        forward.append((beta * hmat[0, i] - sum(factor[i, m] * forward[m] for m in range(i))) * inverse[i])
    coef = [None] * ITERS
    for i in reversed(range(ITERS)):
        coef[i] = (forward[i] - sum(factor[m, i] * coef[m] for m in range(i + 1, ITERS))) * inverse[i]
    mix = [sum(coef[s] * basis[s][m] for s in range(m, ITERS))[:, :width] for m in range(ITERS)]
    sol_ref[...] = sum(mix[m] * zs[m][...] for m in range(ITERS))
    image = sum(mix[m] * (us[m + 1][...] + SHIFT * us[m][...]) for m in range(ITERS))
    res_ref[...] = us[0][...] - image
    ok = ok & (functools.reduce(jnp.maximum, [jnp.abs(c) for c in coef]) < 1e30)
    ok_ref[...] = jnp.where(ok, 1.0, 0.0)


def call(kernel, args, outs, spaces=None, scratch=(), flops=0, pinned=True, ready=True):
    spaces = [pltpu.VMEM] * len(args) if spaces is None else spaces
    if ready:
        args = [pltpu.with_memory_space_constraint(x, s) if s is pltpu.VMEM else x for x, s in zip(args, spaces)]
    size = sum(x.dtype.itemsize * math.prod(x.shape) for x in args)
    return pl.pallas_call(
        kernel,
        out_shape=[pltpu.VMEM(shape, F32) if pinned else jax.ShapeDtypeStruct(shape, F32) for shape in outs],
        in_specs=[pl.BlockSpec(memory_space=s) for s in spaces],
        out_specs=[pl.BlockSpec(memory_space=pltpu.VMEM) for _ in outs],
        scratch_shapes=scratch,
        compiler_params=pltpu.CompilerParams(vmem_limit_bytes=VMEM_LIMIT),
        cost_estimate=pl.CostEstimate(flops=flops, bytes_accessed=size, transcendentals=0),
    )(*args)


def add_up(x):
    count = lax.axis_size("span") * lax.axis_size("plane")
    if count & (count - 1):
        return lax.psum(x, ("span", "plane"))
    steps = [1 << i for i in range(count.bit_length() - 1)]

    def of(flip):
        return lax.ppermute(x, ("span", "plane"), [(i, i ^ flip) for i in range(count)])

    for bits in [steps[:1], steps[1:3], *([step] for step in steps[3:])]:
        if len(bits) == 2:
            both, one, other = of(sum(bits)), of(bits[0]), of(bits[1])
            x = (x + one) + (other + both)
        elif bits:
            x = x + of(bits[0])
    return x


def pairings(size):
    if size % 2:
        return [(i, (i + 1) % size) for i in range(size)], [(i, (i - 1) % size) for i in range(size)]
    return [(i, i ^ 1) for i in range(size)], [(i, (i + 1 if i % 2 else i - 1) % size) for i in range(size)]


def on_device(rhs, blocks, columns, line_slot, line_lower, line_upper, pivot_inv):
    width, nfaces = rhs.shape
    nblocks = columns.shape[0]
    nspan, nplane = lax.axis_size("span"), lax.axis_size("plane")
    owned = nfaces // P_SIZE // nplane
    length = P_SIZE * nplane
    per = owned * P_SIZE
    area = width * width
    shape = (nfaces, width)
    span_pairs, span_others = pairings(nspan)
    plane_pairs, plane_others = pairings(nplane)

    us = [rhs.T]
    send = call(
        functools.partial(start_kernel, nplane),
        [line_slot, us[0]],
        [(per, width)] * nplane,
        [pltpu.SMEM, pltpu.VMEM],
        ready=False,
    )
    factors = call(
        functools.partial(square_kernel, length),
        [line_lower, line_upper, pivot_inv],
        [(nfaces * width, width)] * 3,
        flops=nfaces * area,
        ready=False,
    )
    factors = [x.reshape(nfaces, width, width) for x in factors]

    zs = []
    choose = pick = None
    for step in range(ITERS):
        got = [send[0]] + [exchange(send[k], "plane", k) for k in range(1, nplane)]
        solved = call(
            functools.partial(line_kernel, nplane, owned),
            [*got, *factors],
            [(per, width)] * nplane,
            scratch=[pltpu.VMEM((owned, length, width), F32)] * 2,
            flops=6 * nfaces * area,
        )
        if step == 0:
            slot = lax.optimization_barrier((line_slot, solved[0]))[0].reshape(nplane, per)
            me = lax.axis_index("plane")
            owners = jnp.stack([jnp.asarray(partner(me, k, nplane)[1], jnp.int32) for k in range(nplane)])
            places = jnp.arange(nplane, dtype=jnp.int32)
            back = jnp.sum(jnp.where(owners[:, None, None] == places[None, :, None], slot[None], 0), axis=1)
            back = jnp.tile(back.reshape(1, nfaces), (1, 3))
            choose = (back == jnp.arange(nfaces, dtype=jnp.int32)[:, None]).astype(BF16)
        pieces = [solved[0]] + [exchange(solved[k], "plane", k) for k in range(1, nplane)]
        (mine,) = call(faces_kernel, [choose, *pieces], [shape])
        zs.append(mine)
        if step == 0:
            position = table_positions(lax.optimization_barrier((columns, mine))[0], nfaces)
            selector, face = position // nfaces, position % nfaces
            span_first = 1 if nspan % 2 else lax.axis_index("span") % 2
            plane_first = 1 if nplane % 2 else lax.axis_index("plane") % 2
            group = jnp.where(selector >= 3, selector - 3 + 1 - plane_first, selector - 1 + 1 - span_first) % 2
            group = jnp.where(selector == 0, 0, group + jnp.where(selector >= 3, 3, 1))
            lanes = lax.broadcasted_iota(jnp.int32, (1, 10 * nfaces), 1) % (5 * nfaces)
            pick = (lanes == (group * nfaces + face).reshape(-1, 1)).astype(BF16)
        far = lax.ppermute(mine, "span", span_others)
        faces = [
            mine,
            lax.ppermute(mine, "span", span_pairs),
            far,
            lax.ppermute(mine, "plane", plane_pairs),
            lax.ppermute(mine, "plane", plane_others),
        ]
        last = step == ITERS - 1
        args = [blocks, line_slot, pick, *faces, *(us if last else us[-1:])]
        out = call(
            functools.partial(apply_kernel, nplane, nblocks, last),
            args,
            [shape] + ([(1, 128)] if last else [(per, width)] * nplane),
            [pl.ANY] + [pltpu.VMEM] * (len(args) - 1),
            [
                pltpu.VMEM((nfaces, nblocks * area), F32),
                pltpu.VMEM((nblocks * nfaces, math.lcm(width, 128)), F32),
                pltpu.VMEM((2 * nfaces * area // math.lcm(width, 128), math.lcm(width, 128)), BF16),
                pltpu.SemaphoreType.DMA((4, nblocks)),
                pltpu.SMEM(line_slot.shape, jnp.int32),
                pltpu.SemaphoreType.DMA,
            ],
            flops=2 * nblocks * nfaces * area,
        )
        us.append(out[0])
        send = out[1:]
    gram = add_up(send[0])
    sol, res, ok = call(finish_kernel, [gram, *us, *zs], [shape, shape, (1, 128)], pinned=False)
    given = (rhs, blocks, columns, line_slot, line_lower, line_upper, pivot_inv)
    _, sol, res = lax.while_loop(
        lambda state: state[0], lambda _: (jnp.array(False), *step_by_step(*given)), (ok[0, 0] < 0.5, sol.T, res.T)
    )
    return sol, res


def solution(mesh):
    both = ("span", "plane")
    return jax.shard_map(
        on_device,
        mesh=mesh,
        in_specs=(
            P(None, both),
            P(both, None),
            P(None, both),
            P(both, None),
            P(both, None),
            P(both, None),
            P(both, None),
        ),
        out_specs=(P(None, both), P(None, both)),
        check_vma=False,
    )
```

```python
import functools
import math

import jax
import jax.numpy as jnp
import numpy as np
from jax import lax
from jax.experimental import pallas as pl
from jax.experimental.pallas import tpu as pltpu
from jax.sharding import PartitionSpec as P

ITERS = 3
P_SIZE = 2
SHIFT = 2.0
EPS = 1e-6
VMEM_LIMIT = 16 * 1024 * 1024
HIGH = lax.Precision.HIGHEST
F32, BF16 = jnp.float32, jnp.bfloat16


def with_halo(x, sides, width, wrap):
    for axis, dim in sides:
        size, length = (lax.axis_size(axis), x.shape[dim])
        up = [(i, (i + 1) % size) for i in range(size if wrap else size - 1)]
        down = [(j, i) for i, j in up]
        last = lax.slice_in_dim(x, length - width, length, axis=dim)
        first = lax.slice_in_dim(x, 0, width, axis=dim)
        before = lax.ppermute(last, axis, up)
        after = lax.ppermute(first, axis, down)
        x = jnp.concatenate([before, x, after], axis=dim)
    return x


def small_solve(factor, target):
    extent = target.shape[0]
    forward_vals = []
    for row in range(extent):
        running = target[row]
        for inner in range(row):
            running = running - factor[row, inner] * forward_vals[inner]
        forward_vals.append(running / factor[row, row])
    backward_vals = [None] * extent
    for row in reversed(range(extent)):
        running = forward_vals[row]
        for inner in range(row + 1, extent):
            running = running - factor[inner, row] * backward_vals[inner]
        backward_vals[row] = running / factor[row, row]
    return jnp.stack(backward_vals)


def to_sequence(factor_rows, nlines, length, width):
    return jnp.swapaxes(factor_rows.reshape(nlines, length, width, width), 0, 1)


def line_solve(rhs_lines, lseq, useq, pseq):
    rseq = jnp.moveaxis(rhs_lines, 2, 0)

    def forward(prev, items):
        right, low = items
        cur = right - jnp.einsum("mab,bm->am", low, prev, precision=HIGH)
        return (cur, cur)

    start = jnp.zeros(rseq.shape[1:], F32)
    _, yseq = lax.scan(forward, start, (rseq, lseq))

    def backward(nxt, items):
        yval, upp, piv = items
        inner = yval - jnp.einsum("mab,bm->am", upp, nxt, precision=HIGH)
        cur = jnp.einsum("mab,bm->am", piv, inner, precision=HIGH)
        return (cur, cur)

    _, zseq = lax.scan(backward, start, (yseq, useq, pseq), reverse=True)
    return jnp.moveaxis(zseq, 0, 2)


def table_positions(columns, nfaces, my_span, my_plane, nspan, nplane):
    device_of = columns // nfaces
    span_of = device_of // nplane
    plane_of = device_of % nplane
    dspan = (span_of - my_span + 1 + nspan) % nspan - 1
    dplane = plane_of - my_plane
    selector = jnp.where(
        dspan == -1,
        1,
        jnp.where(dspan == 1, 2, jnp.where(dplane == -1, 3, jnp.where(dplane == 1, 4, 0))),
    )
    return selector * nfaces + columns % nfaces


def step_by_step(rhs, blocks, columns, line_slot, line_lower, line_upper, pivot_inv):
    width, nfaces = rhs.shape
    nblocks = columns.shape[0]
    nplane = lax.axis_size("plane")
    position = table_positions(
        columns, nfaces, lax.axis_index("span"), lax.axis_index("plane"), lax.axis_size("span"), nplane
    )
    slot = line_slot[0]
    lines_group = nfaces // P_SIZE
    owned = lines_group // nplane
    length = P_SIZE * nplane
    lower = to_sequence(line_lower, owned, length, width)
    upper = to_sequence(line_upper, owned, length, width)
    pivot = to_sequence(pivot_inv, owned, length, width)
    shaped_blocks = blocks.reshape(nfaces, nblocks, width, width)

    def apply_a(vec):
        shaped = vec.reshape(width, 1, 1, nfaces)
        span_side = with_halo(shaped, (("span", 1),), 1, True)
        plane_side = with_halo(shaped, (("plane", 2),), 1, False)
        below = plane_side[:, 0, 0]
        above = plane_side[:, 0, 2]
        table = jnp.concatenate([vec, span_side[:, 0, 0], span_side[:, 2, 0], below, above], axis=1)
        return jnp.einsum("ikab,bki->ai", shaped_blocks, table[:, position], precision=HIGH)

    def apply_m(vec):
        pieces = vec[:, slot].reshape(width, lines_group, P_SIZE)
        whole = lax.all_to_all(pieces, "plane", split_axis=1, concat_axis=2, tiled=True)
        solved = line_solve(whole, lower, upper, pivot)
        back = lax.all_to_all(solved, "plane", split_axis=2, concat_axis=1, tiled=True)
        return jnp.zeros_like(vec).at[:, slot].set(back.reshape(width, nfaces))

    beta = jnp.sqrt(lax.psum(jnp.sum(rhs * rhs), ("span", "plane")) + EPS)
    basis = [rhs / beta]
    hcols = []
    for step in range(ITERS):
        wvec = apply_a(apply_m(basis[step]))
        stacked = jnp.stack(basis)
        hvals = lax.psum(jnp.einsum("jai,ai->j", stacked, wvec, precision=HIGH), ("span", "plane"))
        wvec = wvec - jnp.einsum("j,jai->ai", hvals, stacked, precision=HIGH)
        hnext = jnp.sqrt(lax.psum(jnp.sum(wvec * wvec), ("span", "plane")) + EPS)
        basis.append(wvec / hnext)
        hcols.append(jnp.concatenate([hvals, hnext[None], jnp.zeros((ITERS - step - 1,), F32)]))
    hmat = jnp.stack(hcols, axis=1)
    factor = jnp.linalg.cholesky(jnp.dot(hmat.T, hmat, precision=HIGH))
    coef = small_solve(factor, beta * hmat[0])
    update = jnp.einsum("j,jai->ai", coef, jnp.stack(basis[:ITERS]), precision=HIGH)
    solution = apply_m(update)
    return solution, rhs - apply_a(solution)


def partner(me, k, size):
    if size & (size - 1) == 0:
        return me ^ k, me ^ k
    return (me + k) % size, (me + size - k) % size


def exchange(x, axis, k):
    size = lax.axis_size(axis)
    return lax.ppermute(x, axis, [(i, partner(i, k, size)[0]) for i in range(size)])


def split(x, parts):
    out = []
    for _ in range(parts):
        out.append(x.astype(BF16).astype(F32))
        x = x - out[-1]
    return jnp.concatenate(out, axis=0)


def start_kernel(nplane, slot_ref, u_ref, copy_ref, choose_ref, *outs):
    nfaces = u_ref.shape[0]
    per = nfaces // nplane
    me = lax.axis_index("plane")
    for k in range(nplane):
        to, _ = partner(me, k, nplane)
        for i in range(per):
            outs[k][pl.ds(i, 1), :] = u_ref[pl.ds(slot_ref[0, to * per + i], 1), :]
    copy_ref[...] = u_ref[...]
    face = lax.broadcasted_iota(jnp.int32, choose_ref.shape, 0)
    piece = lax.broadcasted_iota(jnp.int32, choose_ref.shape, 1) % nfaces
    choose = jnp.zeros(choose_ref.shape, F32)
    for k in range(nplane):
        _, source = partner(me, k, nplane)
        for i in range(per):
            hit = (face == slot_ref[0, source * per + i]) & (piece == k * per + i)
            choose = jnp.where(hit, 1.0, choose)
    choose_ref[...] = choose


def square_kernel(length, low, upp, piv, low_out, upp_out, piv_out, low_scr, upp_scr, piv_scr, sems):
    nrows, width = low.shape[0], low_out.shape[1]
    chunk = math.lcm(width, 128)
    work = ((low, low_scr, low_out), (piv, piv_scr, piv_out), (upp, upp_scr, upp_out))
    fetches = [pltpu.make_async_copy(src, scr, sems.at[n]) for n, (src, scr, _) in enumerate(work)]
    for fetch in fetches:
        fetch.start()
    for fetch, (src, scr, dst) in zip(fetches, work):
        fetch.wait()
        for c in range(width * width // chunk):
            piece = scr[:, c * chunk : (c + 1) * chunk]
            for r in range(chunk // width):
                a = c * (chunk // width) + r
                dst[pl.ds(a, nrows, stride=width), :] = piece[:, r * width : (r + 1) * width]
        for at in range(nrows):
            here = slice(at * width, (at + 1) * width)
            if src is piv or (src is low and at % length % 2 == 0 and at % length):
                dst[here, :] = dst[here, :].T


def pick_kernel(nspan, nplane, columns_ref, pick_ref):
    nblocks, nfaces = columns_ref.shape
    span, plane = lax.axis_index("span"), lax.axis_index("plane")
    position = table_positions(columns_ref[...], nfaces, span, plane, nspan, nplane)
    selector, face = position // nfaces, position % nfaces
    span_first = 1 if nspan % 2 else span % 2
    plane_first = 1 if nplane % 2 else plane % 2
    group = jnp.where(selector >= 3, selector - 2 - plane_first, selector - span_first)
    group = jnp.where(group == 2, 0, group) + jnp.where(selector >= 3, 3, 1)
    at = jnp.where(selector == 0, 0, group) * nfaces + face
    eye = lax.broadcasted_iota(jnp.int32, (nfaces, nfaces), 0) == lax.broadcasted_iota(jnp.int32, (nfaces, nfaces), 1)
    lane = lax.broadcasted_iota(jnp.int32, (nfaces, pick_ref.shape[1]), 1) % (pick_ref.shape[1] // 2)
    for k in range(nblocks):
        column = jnp.sum(jnp.where(eye, at[k : k + 1, :].astype(F32), 0.0), axis=1, keepdims=True).astype(jnp.int32)
        pick_ref[k * nfaces : (k + 1) * nfaces, :] = jnp.where(lane == column, 1.0, 0.0)


def line_kernel(nplane, nlines, *refs):
    msgs, (low, upp, piv_t), outs, (r_scr, z_scr) = refs[:nplane], refs[nplane:-nplane-2], refs[-nplane-2:-2], refs[-2:]
    _, length, width = r_scr.shape
    me = lax.axis_index("plane")
    for k in range(nplane):
        _, source = partner(me, k, nplane)
        for m in range(nlines):
            for q in range(P_SIZE):
                r_scr[m, pl.ds(source * P_SIZE + q, 1), :] = msgs[k][pl.ds(m * P_SIZE + q, 1), :]
    eye = lax.broadcasted_iota(jnp.int32, (width, width), 0) == lax.broadcasted_iota(jnp.int32, (width, width), 1)

    def column(row):
        return jnp.sum(jnp.where(eye, row, 0.0), axis=1, keepdims=True)

    rows = [[r_scr[m, pl.ds(j, 1), :] for m in range(nlines)] for j in range(length)]
    y_cols = [[None] * nlines for _ in range(length)]
    carry = [None] * nlines
    for j in range(length):
        for m in range(nlines):
            at = m * length + j
            if j == 0:
                carry[m] = rows[j][m]
            elif j % 2:
                carry[m] = column(rows[j][m]) - jnp.sum(low[at] * carry[m], axis=1, keepdims=True)
            else:
                carry[m] = rows[j][m] - jnp.sum(low[at] * carry[m], axis=0, keepdims=True)
            y_cols[j][m] = carry[m] if j % 2 else column(carry[m])
    after = [None] * nlines
    for j in reversed(range(length)):
        for m in range(nlines):
            at = m * length + j
            inner = y_cols[j][m]
            if j < length - 1:
                inner = inner - jnp.sum(upp[at] * after[m], axis=1, keepdims=True)
            after[m] = jnp.sum(piv_t[at] * inner, axis=0, keepdims=True)
            z_scr[m, pl.ds(j, 1), :] = after[m]
    for k in range(nplane):
        to, _ = partner(me, k, nplane)
        for m in range(nlines):
            for q in range(P_SIZE):
                outs[k][pl.ds(m * P_SIZE + q, 1), :] = z_scr[m, pl.ds(to * P_SIZE + q, 1), :]


def faces_kernel(choose, *refs):
    solved, mine_ref = refs[:-1], refs[-1]
    table = split(jnp.concatenate([s[...] for s in solved], axis=0), 3).astype(BF16)
    mine_ref[...] = jnp.dot(choose[...].astype(BF16), table, preferred_element_type=F32)


def apply_kernel(nplane, nblocks, last, *refs):
    (blocks, slot, pick), faces, refs = refs[:3], refs[3:8], refs[8:]
    nold = ITERS if last else 1
    olds, refs = refs[:nold], refs[nold:]
    next_ref, outs, (buf, x_scr, acc_scr, parts, sems, slot_scr, slot_sem) = refs[0], refs[1:-7], refs[-7:]
    nfaces, width = faces[0].shape
    area = width * width
    chunk = math.lcm(width, 128)
    copies, count = chunk // width, area // chunk
    lane = lax.broadcasted_iota(jnp.int32, (1, 128), 1)

    bounds = [0, nblocks - 7, nblocks - 3, nblocks - 1, nblocks]
    runs = []
    for g, (first, end) in enumerate(zip(bounds, bounds[1:])):
        where = pl.ds(first * area, (end - first) * area)
        runs.append(pltpu.make_async_copy(blocks.at[:, where], buf.at[:, where], sems.at[g]))
        runs[-1].start()
    if not last:
        slots = pltpu.make_async_copy(slot, slot_scr, slot_sem)
        slots.start()

    both = split(jnp.concatenate([f[...] for f in faces], axis=0), 2).astype(BF16)
    picked = jnp.dot(pick[...].astype(BF16), both, preferred_element_type=F32)
    x_scr[...] = jnp.concatenate([picked] * copies, axis=1)
    seg = [jnp.broadcast_to(jnp.where(lane % copies == r, 1.0, 0.0), (width, 128)) for r in range(copies)]
    seg = jnp.concatenate(seg, axis=0).astype(BF16)
    for first, end, run in zip(bounds, bounds[1:], runs):
        run.wait()
        for v in range(0, chunk, 128):
            xs = [x_scr[k * nfaces : (k + 1) * nfaces, v : v + 128] for k in range(first, end)]
            for c in range(count):
                at = c * chunk + v
                total = None if first == 0 else acc_scr[:, at : at + 128]
                for k in range(first, end):
                    term = buf[:, k * area + at : k * area + at + 128] * xs[k - first]
                    total = term if total is None else total + term
                if end < nblocks:
                    acc_scr[:, at : at + 128] = total
                else:
                    high = total.astype(BF16)
                    row = 2 * c * nfaces
                    parts[row : row + nfaces, v : v + 128] = high
                    parts[row + nfaces : row + 2 * nfaces, v : v + 128] = (total - high.astype(F32)).astype(BF16)
    sums = jnp.dot(parts[...], seg, preferred_element_type=F32)
    total = jnp.zeros((nfaces, 128), F32)
    for c in range(count):
        at = 2 * c * nfaces
        pair = sums[at : at + nfaces] + sums[at + nfaces : at + 2 * nfaces]
        total = total + jnp.where(lane // copies == c, pair, 0.0)
    u_next = total[:, :width] - SHIFT * olds[-1][...]
    next_ref[...] = u_next
    if last:
        gram_ref = outs[0]
        basis = [old[...] for old in olds] + [u_next]
        gram, at = jnp.zeros(gram_ref.shape, F32), 0
        for i in range(ITERS + 1):
            for j in range(i, ITERS + 1):
                value = jnp.sum(jnp.sum(basis[i] * basis[j], axis=0, keepdims=True), axis=1, keepdims=True)
                gram, at = jnp.where(lane == at, value, gram), at + 1
        gram_ref[...] = gram
    else:
        per = nfaces // nplane
        me = lax.axis_index("plane")
        slots.wait()
        for k in range(nplane):
            to, _ = partner(me, k, nplane)
            for i in range(per):
                outs[k][pl.ds(i, 1), :] = next_ref[pl.ds(slot_scr[0, to * per + i], 1), :]


def finish_kernel(gram_ref, *refs):
    us, zs = refs[: ITERS + 1], refs[ITERS + 1 : 2 * ITERS + 1]
    sol_ref, res_ref, ok_ref = refs[2 * ITERS + 1 :]
    width = sol_ref.shape[1]
    rows = jnp.sum(gram_ref[...], axis=0, keepdims=True)
    lane = lax.broadcasted_iota(jnp.int32, rows.shape, 1)
    gram, at = {}, 0
    for i in range(ITERS + 1):
        for j in range(i, ITERS + 1):
            value = jnp.sum(jnp.where(lane == at, rows, 0.0), axis=1, keepdims=True)
            gram[i, j] = gram[j, i] = jnp.broadcast_to(value, rows.shape)
            at += 1
    largest = functools.reduce(jnp.maximum, [jnp.abs(g) for g in gram.values()])
    ok = largest < 1e30
    beta = jnp.sqrt(gram[0, 0] + EPS)
    basis = [[1.0 / beta]]
    hmat = {}
    for step in range(ITERS):
        own = basis[step]
        wvec = [SHIFT * own[0]] + [own[i] + SHIFT * own[i + 1] for i in range(step)] + [own[step]]
        images = [sum(gram[i, j] * wvec[j] for j in range(step + 2)) for i in range(step + 1)]
        for i in range(step + 1):
            hmat[i, step] = sum(basis[i][m] * images[m] for m in range(i + 1))
        for i in range(step + 1):
            for m in range(i + 1):
                wvec[m] = wvec[m] - hmat[i, step] * basis[i][m]
        terms = [wvec[i] * wvec[j] * gram[i, j] for i in range(step + 2) for j in range(step + 2)]
        square = jnp.maximum(sum(terms), 0.0)
        ok = ok & (square + EPS >= 2e-3 * sum(jnp.abs(term) for term in terms))
        hmat[step + 1, step] = jnp.sqrt(square + EPS)
        scale = 1.0 / hmat[step + 1, step]
        basis.append([w * scale for w in wvec])
    normal = {
        (i, j): sum(hmat[m, i] * hmat[m, j] for m in range(j + 2) if (m, i) in hmat and (m, j) in hmat)
        for i in range(ITERS)
        for j in range(i + 1)
    }
    factor, inverse = {}, []
    for j in range(ITERS):
        diag = jnp.sqrt(normal[j, j] - sum(factor[j, m] * factor[j, m] for m in range(j)))
        inverse.append(1.0 / diag)
        for i in range(j + 1, ITERS):
            factor[i, j] = (normal[i, j] - sum(factor[i, m] * factor[j, m] for m in range(j))) * inverse[j]
    forward = []
    for i in range(ITERS):
        forward.append((beta * hmat[0, i] - sum(factor[i, m] * forward[m] for m in range(i))) * inverse[i])
    coef = [None] * ITERS
    for i in reversed(range(ITERS)):
        coef[i] = (forward[i] - sum(factor[m, i] * coef[m] for m in range(i + 1, ITERS))) * inverse[i]
    mix = [sum(coef[s] * basis[s][m] for s in range(m, ITERS))[:, :width] for m in range(ITERS)]
    sol_ref[...] = sum(mix[m] * zs[m][...] for m in range(ITERS))
    image = sum(mix[m] * (us[m + 1][...] + SHIFT * us[m][...]) for m in range(ITERS))
    res_ref[...] = us[0][...] - image
    ok = ok & (functools.reduce(jnp.maximum, [jnp.abs(c) for c in coef]) < 1e30)
    ok_ref[...] = jnp.where(ok, 1.0, 0.0)


def call(kernel, args, outs, spaces=None, scratch=(), flops=0, pinned=True, ready=True):
    spaces = [pltpu.VMEM] * len(args) if spaces is None else spaces
    if ready:
        args = [pltpu.with_memory_space_constraint(x, s) if s is pltpu.VMEM else x for x, s in zip(args, spaces)]
    size = sum(x.dtype.itemsize * math.prod(x.shape) for x in args)
    return pl.pallas_call(
        kernel,
        out_shape=[pltpu.VMEM(shape, F32) if pinned else jax.ShapeDtypeStruct(shape, F32) for shape in outs],
        in_specs=[pl.BlockSpec(memory_space=s) for s in spaces],
        out_specs=[pl.BlockSpec(memory_space=pltpu.VMEM) for _ in outs],
        scratch_shapes=scratch,
        compiler_params=pltpu.CompilerParams(vmem_limit_bytes=VMEM_LIMIT),
        cost_estimate=pl.CostEstimate(flops=flops, bytes_accessed=size, transcendentals=0),
    )(*args)


def add_up(x):
    count = lax.axis_size("span") * lax.axis_size("plane")
    rows = jnp.broadcast_to(x, (count, x.shape[1]))
    return lax.all_to_all(rows, ("span", "plane"), split_axis=0, concat_axis=0, tiled=True)


def pairings(size):
    if size % 2:
        return [(i, (i + 1) % size) for i in range(size)], [(i, (i - 1) % size) for i in range(size)]
    return [(i, i ^ 1) for i in range(size)], [(i, (i + 1 if i % 2 else i - 1) % size) for i in range(size)]


def on_device(rhs, blocks, columns, line_slot, line_lower, line_upper, pivot_inv):
    width, nfaces = rhs.shape
    nblocks = columns.shape[0]
    nspan, nplane = lax.axis_size("span"), lax.axis_size("plane")
    owned = nfaces // P_SIZE // nplane
    length = P_SIZE * nplane
    per = owned * P_SIZE
    area = width * width
    shape = (nfaces, width)
    span_pairs, span_others = pairings(nspan)
    plane_pairs, plane_others = pairings(nplane)

    u_first, choose, *send = call(
        functools.partial(start_kernel, nplane),
        [line_slot, rhs.T],
        [shape, (nfaces, 3 * nfaces)] + [(per, width)] * nplane,
        [pltpu.SMEM, pltpu.VMEM],
        ready=False,
    )
    us = [u_first]
    factors = call(
        functools.partial(square_kernel, length),
        [line_lower, line_upper, pivot_inv],
        [(nfaces * width, width)] * 3,
        [pl.ANY] * 3,
        [pltpu.VMEM((nfaces, area), F32)] * 3 + [pltpu.SemaphoreType.DMA((3,))],
        flops=nfaces * area,
    )
    factors = [x.reshape(nfaces, width, width) for x in factors]

    zs = []
    pick = None
    for step in range(ITERS):
        got = [send[0]] + [exchange(send[k], "plane", k) for k in range(1, nplane)]
        solved = call(
            functools.partial(line_kernel, nplane, owned),
            [*got, *factors],
            [(per, width)] * nplane,
            scratch=[pltpu.VMEM((owned, length, width), F32)] * 2,
            flops=6 * nfaces * area,
        )
        if step == 0:
            (pick,) = call(
                functools.partial(pick_kernel, nspan, nplane),
                [lax.optimization_barrier((columns, solved[0]))[0]],
                [(nblocks * nfaces, 10 * nfaces)],
                ready=False,
            )
        pieces = [solved[0]] + [exchange(solved[k], "plane", k) for k in range(1, nplane)]
        (mine,) = call(faces_kernel, [choose, *pieces], [shape])
        zs.append(mine)
        far = lax.ppermute(mine, "span", span_others)
        faces = [
            mine,
            lax.ppermute(mine, "span", span_pairs),
            far,
            lax.ppermute(mine, "plane", plane_pairs),
            lax.ppermute(mine, "plane", plane_others),
        ]
        last = step == ITERS - 1
        args = [blocks, line_slot, pick, *faces, *(us if last else us[-1:])]
        out = call(
            functools.partial(apply_kernel, nplane, nblocks, last),
            args,
            [shape] + ([(1, 128)] if last else [(per, width)] * nplane),
            [pl.ANY] * 2 + [pltpu.VMEM] * (len(args) - 2),
            [
                pltpu.VMEM((nfaces, nblocks * area), F32),
                pltpu.VMEM((nblocks * nfaces, math.lcm(width, 128)), F32),
                pltpu.VMEM((nfaces, area), F32),
                pltpu.VMEM((2 * nfaces * area // math.lcm(width, 128), math.lcm(width, 128)), BF16),
                pltpu.SemaphoreType.DMA((4,)),
                pltpu.SMEM(line_slot.shape, jnp.int32),
                pltpu.SemaphoreType.DMA,
            ],
            flops=2 * nblocks * nfaces * area,
        )
        us.append(out[0])
        send = out[1:]
    gram = add_up(send[0])
    sol, res, ok = call(finish_kernel, [gram, *us, *zs], [shape, shape, (1, 128)], pinned=False)
    given = (rhs, blocks, columns, line_slot, line_lower, line_upper, pivot_inv)
    _, sol, res = lax.while_loop(
        lambda state: state[0], lambda _: (jnp.array(False), *step_by_step(*given)), (ok[0, 0] < 0.5, sol.T, res.T)
    )
    return sol, res


def solution(mesh):
    both = ("span", "plane")
    return jax.shard_map(
        on_device,
        mesh=mesh,
        in_specs=(
            P(None, both),
            P(both, None),
            P(None, both),
            P(both, None),
            P(both, None),
            P(both, None),
            P(both, None),
        ),
        out_specs=(P(None, both), P(None, both)),
        check_vma=False,
    )
```

```python
import functools
import math

import jax
import jax.numpy as jnp
import numpy as np
from jax import lax
from jax.experimental import pallas as pl
from jax.experimental.pallas import tpu as pltpu
from jax.sharding import PartitionSpec as P

ITERS = 3
P_SIZE = 2
SHIFT = 2.0
EPS = 1e-6
VMEM_LIMIT = 16 * 1024 * 1024
HIGH = lax.Precision.HIGHEST
F32, BF16 = jnp.float32, jnp.bfloat16


def with_halo(x, sides, width, wrap):
    for axis, dim in sides:
        size, length = (lax.axis_size(axis), x.shape[dim])
        up = [(i, (i + 1) % size) for i in range(size if wrap else size - 1)]
        down = [(j, i) for i, j in up]
        last = lax.slice_in_dim(x, length - width, length, axis=dim)
        first = lax.slice_in_dim(x, 0, width, axis=dim)
        before = lax.ppermute(last, axis, up)
        after = lax.ppermute(first, axis, down)
        x = jnp.concatenate([before, x, after], axis=dim)
    return x


def small_solve(factor, target):
    extent = target.shape[0]
    forward_vals = []
    for row in range(extent):
        running = target[row]
        for inner in range(row):
            running = running - factor[row, inner] * forward_vals[inner]
        forward_vals.append(running / factor[row, row])
    backward_vals = [None] * extent
    for row in reversed(range(extent)):
        running = forward_vals[row]
        for inner in range(row + 1, extent):
            running = running - factor[inner, row] * backward_vals[inner]
        backward_vals[row] = running / factor[row, row]
    return jnp.stack(backward_vals)


def to_sequence(factor_rows, nlines, length, width):
    return jnp.swapaxes(factor_rows.reshape(nlines, length, width, width), 0, 1)


def line_solve(rhs_lines, lseq, useq, pseq):
    rseq = jnp.moveaxis(rhs_lines, 2, 0)

    def forward(prev, items):
        right, low = items
        cur = right - jnp.einsum("mab,bm->am", low, prev, precision=HIGH)
        return (cur, cur)

    start = jnp.zeros(rseq.shape[1:], F32)
    _, yseq = lax.scan(forward, start, (rseq, lseq))

    def backward(nxt, items):
        yval, upp, piv = items
        inner = yval - jnp.einsum("mab,bm->am", upp, nxt, precision=HIGH)
        cur = jnp.einsum("mab,bm->am", piv, inner, precision=HIGH)
        return (cur, cur)

    _, zseq = lax.scan(backward, start, (yseq, useq, pseq), reverse=True)
    return jnp.moveaxis(zseq, 0, 2)


def table_positions(columns, nfaces, my_span, my_plane, nspan, nplane):
    device_of = columns // nfaces
    span_of = device_of // nplane
    plane_of = device_of % nplane
    dspan = (span_of - my_span + 1 + nspan) % nspan - 1
    dplane = plane_of - my_plane
    selector = jnp.where(
        dspan == -1,
        1,
        jnp.where(dspan == 1, 2, jnp.where(dplane == -1, 3, jnp.where(dplane == 1, 4, 0))),
    )
    return selector * nfaces + columns % nfaces


def step_by_step(rhs, blocks, columns, line_slot, line_lower, line_upper, pivot_inv):
    width, nfaces = rhs.shape
    nblocks = columns.shape[0]
    nplane = lax.axis_size("plane")
    position = table_positions(
        columns, nfaces, lax.axis_index("span"), lax.axis_index("plane"), lax.axis_size("span"), nplane
    )
    slot = line_slot[0]
    lines_group = nfaces // P_SIZE
    owned = lines_group // nplane
    length = P_SIZE * nplane
    lower = to_sequence(line_lower, owned, length, width)
    upper = to_sequence(line_upper, owned, length, width)
    pivot = to_sequence(pivot_inv, owned, length, width)
    shaped_blocks = blocks.reshape(nfaces, nblocks, width, width)

    def apply_a(vec):
        shaped = vec.reshape(width, 1, 1, nfaces)
        span_side = with_halo(shaped, (("span", 1),), 1, True)
        plane_side = with_halo(shaped, (("plane", 2),), 1, False)
        below = plane_side[:, 0, 0]
        above = plane_side[:, 0, 2]
        table = jnp.concatenate([vec, span_side[:, 0, 0], span_side[:, 2, 0], below, above], axis=1)
        return jnp.einsum("ikab,bki->ai", shaped_blocks, table[:, position], precision=HIGH)

    def apply_m(vec):
        pieces = vec[:, slot].reshape(width, lines_group, P_SIZE)
        whole = lax.all_to_all(pieces, "plane", split_axis=1, concat_axis=2, tiled=True)
        solved = line_solve(whole, lower, upper, pivot)
        back = lax.all_to_all(solved, "plane", split_axis=2, concat_axis=1, tiled=True)
        return jnp.zeros_like(vec).at[:, slot].set(back.reshape(width, nfaces))

    beta = jnp.sqrt(lax.psum(jnp.sum(rhs * rhs), ("span", "plane")) + EPS)
    basis = [rhs / beta]
    hcols = []
    for step in range(ITERS):
        wvec = apply_a(apply_m(basis[step]))
        stacked = jnp.stack(basis)
        hvals = lax.psum(jnp.einsum("jai,ai->j", stacked, wvec, precision=HIGH), ("span", "plane"))
        wvec = wvec - jnp.einsum("j,jai->ai", hvals, stacked, precision=HIGH)
        hnext = jnp.sqrt(lax.psum(jnp.sum(wvec * wvec), ("span", "plane")) + EPS)
        basis.append(wvec / hnext)
        hcols.append(jnp.concatenate([hvals, hnext[None], jnp.zeros((ITERS - step - 1,), F32)]))
    hmat = jnp.stack(hcols, axis=1)
    factor = jnp.linalg.cholesky(jnp.dot(hmat.T, hmat, precision=HIGH))
    coef = small_solve(factor, beta * hmat[0])
    update = jnp.einsum("j,jai->ai", coef, jnp.stack(basis[:ITERS]), precision=HIGH)
    solution = apply_m(update)
    return solution, rhs - apply_a(solution)


def partner(me, k, size):
    if size & (size - 1) == 0:
        return me ^ k, me ^ k
    return (me + k) % size, (me + size - k) % size


def exchange(x, axis, k):
    size = lax.axis_size(axis)
    return lax.ppermute(x, axis, [(i, partner(i, k, size)[0]) for i in range(size)])


def split(x, parts):
    out = []
    for _ in range(parts):
        out.append(x.astype(BF16).astype(F32))
        x = x - out[-1]
    return jnp.concatenate(out, axis=0)


def start_kernel(nplane, slot_ref, u_ref, copy_ref, choose_ref, *outs):
    nfaces = u_ref.shape[0]
    per = nfaces // nplane
    me = lax.axis_index("plane")
    for k in range(nplane):
        to, _ = partner(me, k, nplane)
        for i in range(per):
            outs[k][pl.ds(i, 1), :] = u_ref[pl.ds(slot_ref[0, to * per + i], 1), :]
    copy_ref[...] = u_ref[...]
    face = lax.broadcasted_iota(jnp.int32, choose_ref.shape, 0)
    piece = lax.broadcasted_iota(jnp.int32, choose_ref.shape, 1) % nfaces
    choose = jnp.zeros(choose_ref.shape, F32)
    for k in range(nplane):
        _, source = partner(me, k, nplane)
        for i in range(per):
            hit = (face == slot_ref[0, source * per + i]) & (piece == k * per + i)
            choose = jnp.where(hit, 1.0, choose)
    choose_ref[...] = choose


def square_kernel(length, low, upp, piv, _, low_out, upp_out, piv_out, low_scr, upp_scr, piv_scr, sems):
    nrows, width = low.shape[0], low_out.shape[1]
    chunk = math.lcm(width, 128)
    work = ((low, low_scr, low_out), (piv, piv_scr, piv_out), (upp, upp_scr, upp_out))
    fetches = [pltpu.make_async_copy(src, scr, sems.at[n]) for n, (src, scr, _) in enumerate(work)]
    for fetch in fetches:
        fetch.start()
    for fetch, (src, scr, dst) in zip(fetches, work):
        fetch.wait()
        for c in range(width * width // chunk):
            piece = scr[:, c * chunk : (c + 1) * chunk]
            for r in range(chunk // width):
                a = c * (chunk // width) + r
                dst[pl.ds(a, nrows, stride=width), :] = piece[:, r * width : (r + 1) * width]
        for at in range(nrows):
            here = slice(at * width, (at + 1) * width)
            if src is piv or (src is low and at % length % 2 == 0 and at % length):
                dst[here, :] = dst[here, :].T


def parities():
    return [1 if lax.axis_size(a) % 2 else lax.axis_index(a) % 2 for a in ("span", "plane")]


def early_blocks():
    span_odd, plane_odd = parities()
    return (1 + span_odd, 3 + plane_odd), (2 - span_odd, 4 - plane_odd)


def pick_kernel(nspan, nplane, columns_ref, early_ref, late_ref):
    nblocks, nfaces = columns_ref.shape
    span, plane = lax.axis_index("span"), lax.axis_index("plane")
    position = table_positions(columns_ref[...], nfaces, span, plane, nspan, nplane)
    selector, face = position // nfaces, position % nfaces
    span_odd, plane_odd = [parity == 1 for parity in parities()]
    of_span = jnp.where((selector == 1) == span_odd, 1, 3)
    of_plane = jnp.where((selector == 3) == plane_odd, 2, 4)
    group = jnp.where(selector == 0, 0, jnp.where(selector <= 2, of_span, of_plane))
    at = (group * nfaces + face).astype(F32)
    eye = lax.broadcasted_iota(jnp.int32, (nfaces, nfaces), 0) == lax.broadcasted_iota(jnp.int32, (nfaces, nfaces), 1)
    first, second = jnp.where(span_odd, at[2:3], at[1:2]), jnp.where(span_odd, at[1:2], at[2:3])
    third, fourth = jnp.where(plane_odd, at[4:5], at[3:4]), jnp.where(plane_odd, at[3:4], at[4:5])
    rest = [at[k : k + 1] for k in range(5, nblocks)]
    for ref, rows in ((early_ref, [at[0:1], first, third]), (late_ref, [second, fourth, *rest])):
        lane = lax.broadcasted_iota(jnp.int32, (nfaces, ref.shape[1]), 1) % (ref.shape[1] // 2)
        for n, row in enumerate(rows):
            column = jnp.sum(jnp.where(eye, row, 0.0), axis=1, keepdims=True).astype(jnp.int32)
            ref[n * nfaces : (n + 1) * nfaces, :] = jnp.where(lane == column, 1.0, 0.0).astype(BF16)


def line_kernel(nplane, nlines, *refs):
    msgs, (low, upp, piv_t), outs, (r_scr, z_scr) = refs[:nplane], refs[nplane:-nplane-2], refs[-nplane-2:-2], refs[-2:]
    _, length, width = r_scr.shape
    me = lax.axis_index("plane")
    for k in range(nplane):
        _, source = partner(me, k, nplane)
        for m in range(nlines):
            for q in range(P_SIZE):
                r_scr[m, pl.ds(source * P_SIZE + q, 1), :] = msgs[k][pl.ds(m * P_SIZE + q, 1), :]
    eye = lax.broadcasted_iota(jnp.int32, (width, width), 0) == lax.broadcasted_iota(jnp.int32, (width, width), 1)

    def column(row):
        return jnp.sum(jnp.where(eye, row, 0.0), axis=1, keepdims=True)

    rows = [[r_scr[m, pl.ds(j, 1), :] for m in range(nlines)] for j in range(length)]
    y_cols = [[None] * nlines for _ in range(length)]
    carry = [None] * nlines
    for j in range(length):
        for m in range(nlines):
            at = m * length + j
            if j == 0:
                carry[m] = rows[j][m]
            elif j % 2:
                carry[m] = column(rows[j][m]) - jnp.sum(low[at] * carry[m], axis=1, keepdims=True)
            else:
                carry[m] = rows[j][m] - jnp.sum(low[at] * carry[m], axis=0, keepdims=True)
            y_cols[j][m] = carry[m] if j % 2 else column(carry[m])
    after = [None] * nlines
    for j in reversed(range(length)):
        for m in range(nlines):
            at = m * length + j
            inner = y_cols[j][m]
            if j < length - 1:
                inner = inner - jnp.sum(upp[at] * after[m], axis=1, keepdims=True)
            after[m] = jnp.sum(piv_t[at] * inner, axis=0, keepdims=True)
            z_scr[m, pl.ds(j, 1), :] = after[m]
    for k in range(nplane):
        to, _ = partner(me, k, nplane)
        for m in range(nlines):
            for q in range(P_SIZE):
                outs[k][pl.ds(m * P_SIZE + q, 1), :] = z_scr[m, pl.ds(to * P_SIZE + q, 1), :]


def faces_kernel(choose, *refs):
    solved, mine_ref = refs[:-1], refs[-1]
    table = split(jnp.concatenate([s[...] for s in solved], axis=0), 3).astype(BF16)
    mine_ref[...] = jnp.dot(choose[...].astype(BF16), table, preferred_element_type=F32)


def repeat_faces(faces, pick, copies):
    both = split(jnp.concatenate([f[...] for f in faces], axis=0), 2).astype(BF16)
    picked = jnp.dot(pick[...], both, preferred_element_type=F32)
    return jnp.concatenate([picked] * copies, axis=1)


def add_products(work, x_scr, acc_scr, parts, width):
    nfaces, area = acc_scr.shape
    chunk = x_scr.shape[1]
    copies, count = chunk // width, area // chunk
    lane = lax.broadcasted_iota(jnp.int32, (1, 128), 1)
    seg = [jnp.broadcast_to(jnp.where(lane % copies == r, 1.0, 0.0), (width, 128)) for r in range(copies)]
    seg = jnp.concatenate(seg, axis=0).astype(BF16)
    total = jnp.zeros((nfaces, 128), F32)
    done = 0
    for n, (places, fetch) in enumerate(work):
        if fetch is not None:
            fetch.wait()
        last = n == len(work) - 1
        for half in ((0, count // 2), (count // 2, count)):
            for v in range(0, chunk, 128):
                rows = range(done * nfaces, (done + len(places)) * nfaces, nfaces)
                xs = [x_scr[row : row + nfaces, v : v + 128] for row in rows]
                for c in range(*half):
                    at = c * chunk + v
                    value = acc_scr[:, at : at + 128] if n else None
                    for (ref, column), x in zip(places, xs):
                        term = ref[:, column + at : column + at + 128] * x
                        value = term if value is None else value + term
                    if not last:
                        acc_scr[:, at : at + 128] = value
                        continue
                    high = value.astype(BF16)
                    row = 2 * c * nfaces
                    parts[row : row + nfaces, v : v + 128] = high
                    parts[row + nfaces : row + 2 * nfaces, v : v + 128] = (value - high.astype(F32)).astype(BF16)
            if last:
                base = 2 * half[0] * nfaces
                sums = jnp.dot(parts[base : 2 * half[1] * nfaces, :], seg, preferred_element_type=F32)
                for c in range(*half):
                    at = 2 * c * nfaces - base
                    pair = sums[at : at + nfaces] + sums[at + nfaces : at + 2 * nfaces]
                    total = total + jnp.where(lane // copies == c, pair, 0.0)
        done += len(places)
    return total[:, :width]


def early_kernel(nblocks, blocks, pick, *refs):
    faces, (sum_ref, held, buf, x_scr, acc_scr, parts, sems) = refs[:3], refs[3:]
    width = faces[0].shape[1]
    area = width * width
    early, late = early_blocks()

    def fetch(k, count, dst, column, n):
        start = pl.multiple_of(k * area, 128) if not isinstance(k, int) else k * area
        return pltpu.make_async_copy(
            blocks.at[:, pl.ds(start, count * area)], dst.at[:, pl.ds(column, count * area)], sems.at[n]
        )

    mine = [fetch(k, 1, buf, n * area, n) for n, k in enumerate((0, *early))]
    kept = [fetch(late[1], 1, held, 0, 3), fetch(5, nblocks - 5, held, area, 4)]
    for copy in mine + kept:
        copy.start()
    x_scr[...] = repeat_faces(faces, pick, x_scr.shape[1] // width)
    work = [([(buf, n * area)], copy) for n, copy in enumerate(mine)]
    sum_ref[...] = add_products(work, x_scr, acc_scr, parts, width)
    for copy in kept:
        copy.wait()


def late_kernel(nplane, last, *refs):
    (blocks, slot, held, pick, early_sum), faces, refs = refs[:5], refs[5:10], refs[10:]
    nold = ITERS if last else 1
    olds, refs = refs[:nold], refs[nold:]
    next_ref, outs, (buf, x_scr, acc_scr, parts, sem, slot_scr, slot_sem) = refs[0], refs[1:-7], refs[-7:]
    nfaces, width = faces[0].shape
    area = width * width
    _, late = early_blocks()
    fetch = pltpu.make_async_copy(blocks.at[:, pl.ds(pl.multiple_of(late[0] * area, 128), area)], buf, sem)
    fetch.start()
    if not last:
        slots = pltpu.make_async_copy(slot, slot_scr, slot_sem)
        slots.start()
    repeated = repeat_faces(faces, pick, x_scr.shape[1] // width)
    x_scr[...] = jnp.concatenate([repeated[nfaces:], repeated[:nfaces]], axis=0)
    work = [([(held, column) for column in range(0, held.shape[1], area)], None), ([(buf, 0)], fetch)]
    u_next = early_sum[...] + add_products(work, x_scr, acc_scr, parts, width) - SHIFT * olds[-1][...]
    next_ref[...] = u_next
    if last:
        gram_ref = outs[0]
        lane = lax.broadcasted_iota(jnp.int32, gram_ref.shape, 1)
        basis = [old[...] for old in olds] + [u_next]
        gram, at = jnp.zeros(gram_ref.shape, F32), 0
        for i in range(ITERS + 1):
            for j in range(i, ITERS + 1):
                value = jnp.sum(jnp.sum(basis[i] * basis[j], axis=0, keepdims=True), axis=1, keepdims=True)
                gram, at = jnp.where(lane == at, value, gram), at + 1
        gram_ref[...] = gram
    else:
        per = nfaces // nplane
        me = lax.axis_index("plane")
        slots.wait()
        for k in range(nplane):
            to, _ = partner(me, k, nplane)
            for i in range(per):
                outs[k][pl.ds(i, 1), :] = next_ref[pl.ds(slot_scr[0, to * per + i], 1), :]


def finish_kernel(gram_ref, *refs):
    us, zs = refs[: ITERS + 1], refs[ITERS + 1 : 2 * ITERS + 1]
    sol_ref, res_ref, ok_ref = refs[2 * ITERS + 1 :]
    width = sol_ref.shape[1]
    rows = jnp.sum(gram_ref[...], axis=0, keepdims=True)
    lane = lax.broadcasted_iota(jnp.int32, rows.shape, 1)
    gram, at = {}, 0
    for i in range(ITERS + 1):
        for j in range(i, ITERS + 1):
            value = jnp.sum(jnp.where(lane == at, rows, 0.0), axis=1, keepdims=True)
            gram[i, j] = gram[j, i] = jnp.broadcast_to(value, rows.shape)
            at += 1
    largest = functools.reduce(jnp.maximum, [jnp.abs(g) for g in gram.values()])
    ok = largest < 1e30
    beta = jnp.sqrt(gram[0, 0] + EPS)
    basis = [[1.0 / beta]]
    hmat = {}
    for step in range(ITERS):
        own = basis[step]
        wvec = [SHIFT * own[0]] + [own[i] + SHIFT * own[i + 1] for i in range(step)] + [own[step]]
        images = [sum(gram[i, j] * wvec[j] for j in range(step + 2)) for i in range(step + 1)]
        for i in range(step + 1):
            hmat[i, step] = sum(basis[i][m] * images[m] for m in range(i + 1))
        for i in range(step + 1):
            for m in range(i + 1):
                wvec[m] = wvec[m] - hmat[i, step] * basis[i][m]
        terms = [wvec[i] * wvec[j] * gram[i, j] for i in range(step + 2) for j in range(step + 2)]
        square = jnp.maximum(sum(terms), 0.0)
        ok = ok & (square + EPS >= 2e-3 * sum(jnp.abs(term) for term in terms))
        hmat[step + 1, step] = jnp.sqrt(square + EPS)
        scale = 1.0 / hmat[step + 1, step]
        basis.append([w * scale for w in wvec])
    normal = {
        (i, j): sum(hmat[m, i] * hmat[m, j] for m in range(j + 2) if (m, i) in hmat and (m, j) in hmat)
        for i in range(ITERS)
        for j in range(i + 1)
    }
    factor, inverse = {}, []
    for j in range(ITERS):
        diag = jnp.sqrt(normal[j, j] - sum(factor[j, m] * factor[j, m] for m in range(j)))
        inverse.append(1.0 / diag)
        for i in range(j + 1, ITERS):
            factor[i, j] = (normal[i, j] - sum(factor[i, m] * factor[j, m] for m in range(j))) * inverse[j]
    forward = []
    for i in range(ITERS):
        forward.append((beta * hmat[0, i] - sum(factor[i, m] * forward[m] for m in range(i))) * inverse[i])
    coef = [None] * ITERS
    for i in reversed(range(ITERS)):
        coef[i] = (forward[i] - sum(factor[m, i] * coef[m] for m in range(i + 1, ITERS))) * inverse[i]
    mix = [sum(coef[s] * basis[s][m] for s in range(m, ITERS))[:, :width] for m in range(ITERS)]
    sol_ref[...] = sum(mix[m] * zs[m][...] for m in range(ITERS))
    image = sum(mix[m] * (us[m + 1][...] + SHIFT * us[m][...]) for m in range(ITERS))
    res_ref[...] = us[0][...] - image
    ok = ok & (functools.reduce(jnp.maximum, [jnp.abs(c) for c in coef]) < 1e30)
    ok_ref[...] = jnp.where(ok, 1.0, 0.0)


def call(kernel, args, outs, spaces=None, scratch=(), flops=0, pinned=True, ready=True, kind=F32):
    spaces = [pltpu.VMEM] * len(args) if spaces is None else spaces
    if ready:
        args = [pltpu.with_memory_space_constraint(x, s) if s is pltpu.VMEM else x for x, s in zip(args, spaces)]
    size = sum(x.dtype.itemsize * math.prod(x.shape) for x in args)
    return pl.pallas_call(
        kernel,
        out_shape=[pltpu.VMEM(shape, kind) if pinned else jax.ShapeDtypeStruct(shape, kind) for shape in outs],
        in_specs=[pl.BlockSpec(memory_space=s) for s in spaces],
        out_specs=[pl.BlockSpec(memory_space=pltpu.VMEM) for _ in outs],
        scratch_shapes=scratch,
        compiler_params=pltpu.CompilerParams(vmem_limit_bytes=VMEM_LIMIT),
        cost_estimate=pl.CostEstimate(flops=flops, bytes_accessed=size, transcendentals=0),
    )(*args)


def add_up(x):
    count = lax.axis_size("span") * lax.axis_size("plane")
    rows = jnp.broadcast_to(x, (count, x.shape[1]))
    return lax.all_to_all(rows, ("span", "plane"), split_axis=0, concat_axis=0, tiled=True)


def pairings(size):
    if size % 2:
        return [(i, (i + 1) % size) for i in range(size)], [(i, (i - 1) % size) for i in range(size)]
    return [(i, i ^ 1) for i in range(size)], [(i, (i + 1 if i % 2 else i - 1) % size) for i in range(size)]


def on_device(rhs, blocks, columns, line_slot, line_lower, line_upper, pivot_inv):
    width, nfaces = rhs.shape
    nblocks = columns.shape[0]
    nspan, nplane = lax.axis_size("span"), lax.axis_size("plane")
    owned = nfaces // P_SIZE // nplane
    length = P_SIZE * nplane
    per = owned * P_SIZE
    area = width * width
    shape = (nfaces, width)
    span_pairs, span_others = pairings(nspan)
    plane_pairs, plane_others = pairings(nplane)

    u_first, choose, *send = call(
        functools.partial(start_kernel, nplane),
        [line_slot, rhs.T],
        [shape, (nfaces, 3 * nfaces)] + [(per, width)] * nplane,
        [pltpu.SMEM, pltpu.VMEM],
        ready=False,
    )
    us = [u_first]
    zs = []
    picks = None
    for step in range(ITERS):
        factors = call(
            functools.partial(square_kernel, length),
            [line_lower, line_upper, pivot_inv, us[-1]],
            [(nfaces * width, width)] * 3,
            [pl.ANY] * 4,
            [pltpu.VMEM((nfaces, area), F32)] * 3 + [pltpu.SemaphoreType.DMA((3,))],
            flops=nfaces * area,
        )
        factors = [x.reshape(nfaces, width, width) for x in factors]
        got = [send[0]] + [exchange(send[k], "plane", k) for k in range(1, nplane)]
        solved = call(
            functools.partial(line_kernel, nplane, owned),
            [*got, *factors],
            [(per, width)] * nplane,
            scratch=[pltpu.VMEM((owned, length, width), F32)] * 2,
            flops=6 * nfaces * area,
        )
        if step == 0:
            picks = call(
                functools.partial(pick_kernel, nspan, nplane),
                [lax.optimization_barrier((columns, solved[0]))[0]],
                [(3 * nfaces, 6 * nfaces), ((nblocks - 3) * nfaces, 10 * nfaces)],
                ready=False,
                kind=BF16,
            )
        pieces = [solved[0]] + [exchange(solved[k], "plane", k) for k in range(1, nplane)]
        (mine,) = call(faces_kernel, [choose, *pieces], [shape])
        zs.append(mine)
        other = lax.ppermute(mine, "span", span_others)
        near = [mine, lax.ppermute(mine, "span", span_pairs), lax.ppermute(mine, "plane", plane_pairs)]
        far = [other, lax.ppermute(mine, "plane", plane_others)]
        chunk = math.lcm(width, 128)

        def scratch(count, fetched):
            return [
                pltpu.VMEM((nfaces, fetched * area), F32),
                pltpu.VMEM((count * nfaces, chunk), F32),
                pltpu.VMEM((nfaces, area), F32),
                pltpu.VMEM((2 * nfaces * area // chunk, chunk), BF16),
            ]

        early_sum, held = call(
            functools.partial(early_kernel, nblocks),
            [blocks, picks[0], *near],
            [shape, (nfaces, (nblocks - 4) * area)],
            [pl.ANY] + [pltpu.VMEM] * 4,
            scratch(3, 3) + [pltpu.SemaphoreType.DMA((5,))],
            flops=6 * nfaces * area,
        )
        last = step == ITERS - 1
        args = [blocks, line_slot, held, picks[1], early_sum, *near, *far, *(us if last else us[-1:])]
        out = call(
            functools.partial(late_kernel, nplane, last),
            args,
            [shape] + ([(1, 128)] if last else [(per, width)] * nplane),
            [pl.ANY] * 2 + [pltpu.VMEM] * (len(args) - 2),
            scratch(nblocks - 3, 1)
            + [pltpu.SemaphoreType.DMA, pltpu.SMEM(line_slot.shape, jnp.int32), pltpu.SemaphoreType.DMA],
            flops=2 * nblocks * nfaces * area,
        )
        us.append(out[0])
        send = out[1:]
    gram = add_up(send[0])
    sol, res, ok = call(finish_kernel, [gram, *us, *zs], [shape, shape, (1, 128)], pinned=False)
    given = (rhs, blocks, columns, line_slot, line_lower, line_upper, pivot_inv)
    _, sol, res = lax.while_loop(
        lambda state: state[0], lambda _: (jnp.array(False), *step_by_step(*given)), (ok[0, 0] < 0.5, sol.T, res.T)
    )
    return sol, res


def solution(mesh):
    both = ("span", "plane")
    return jax.shard_map(
        on_device,
        mesh=mesh,
        in_specs=(
            P(None, both),
            P(both, None),
            P(None, both),
            P(both, None),
            P(both, None),
            P(both, None),
            P(both, None),
        ),
        out_specs=(P(None, both), P(None, both)),
        check_vma=False,
    )
```

```python
import functools
import math

import jax
import jax.numpy as jnp
import numpy as np
from jax import lax
from jax.experimental import pallas as pl
from jax.experimental.pallas import tpu as pltpu
from jax.sharding import PartitionSpec as P

ITERS = 3
P_SIZE = 2
SHIFT = 2.0
EPS = 1e-6
VMEM_LIMIT = 16 * 1024 * 1024
HIGH = lax.Precision.HIGHEST
F32, BF16 = jnp.float32, jnp.bfloat16


def with_halo(x, sides, width, wrap):
    for axis, dim in sides:
        size, length = (lax.axis_size(axis), x.shape[dim])
        up = [(i, (i + 1) % size) for i in range(size if wrap else size - 1)]
        down = [(j, i) for i, j in up]
        last = lax.slice_in_dim(x, length - width, length, axis=dim)
        first = lax.slice_in_dim(x, 0, width, axis=dim)
        before = lax.ppermute(last, axis, up)
        after = lax.ppermute(first, axis, down)
        x = jnp.concatenate([before, x, after], axis=dim)
    return x


def small_solve(factor, target):
    extent = target.shape[0]
    forward_vals = []
    for row in range(extent):
        running = target[row]
        for inner in range(row):
            running = running - factor[row, inner] * forward_vals[inner]
        forward_vals.append(running / factor[row, row])
    backward_vals = [None] * extent
    for row in reversed(range(extent)):
        running = forward_vals[row]
        for inner in range(row + 1, extent):
            running = running - factor[inner, row] * backward_vals[inner]
        backward_vals[row] = running / factor[row, row]
    return jnp.stack(backward_vals)


def to_sequence(factor_rows, nlines, length, width):
    return jnp.swapaxes(factor_rows.reshape(nlines, length, width, width), 0, 1)


def line_solve(rhs_lines, lseq, useq, pseq):
    rseq = jnp.moveaxis(rhs_lines, 2, 0)

    def forward(prev, items):
        right, low = items
        cur = right - jnp.einsum("mab,bm->am", low, prev, precision=HIGH)
        return (cur, cur)

    start = jnp.zeros(rseq.shape[1:], F32)
    _, yseq = lax.scan(forward, start, (rseq, lseq))

    def backward(nxt, items):
        yval, upp, piv = items
        inner = yval - jnp.einsum("mab,bm->am", upp, nxt, precision=HIGH)
        cur = jnp.einsum("mab,bm->am", piv, inner, precision=HIGH)
        return (cur, cur)

    _, zseq = lax.scan(backward, start, (yseq, useq, pseq), reverse=True)
    return jnp.moveaxis(zseq, 0, 2)


def table_positions(columns, nfaces, my_span, my_plane, nspan, nplane):
    device_of = columns // nfaces
    span_of = device_of // nplane
    plane_of = device_of % nplane
    dspan = (span_of - my_span + 1 + nspan) % nspan - 1
    dplane = plane_of - my_plane
    selector = jnp.where(
        dspan == -1,
        1,
        jnp.where(dspan == 1, 2, jnp.where(dplane == -1, 3, jnp.where(dplane == 1, 4, 0))),
    )
    return selector * nfaces + columns % nfaces


def step_by_step(rhs, blocks, columns, line_slot, line_lower, line_upper, pivot_inv):
    width, nfaces = rhs.shape
    nblocks = columns.shape[0]
    nplane = lax.axis_size("plane")
    position = table_positions(
        columns, nfaces, lax.axis_index("span"), lax.axis_index("plane"), lax.axis_size("span"), nplane
    )
    slot = line_slot[0]
    lines_group = nfaces // P_SIZE
    owned = lines_group // nplane
    length = P_SIZE * nplane
    lower = to_sequence(line_lower, owned, length, width)
    upper = to_sequence(line_upper, owned, length, width)
    pivot = to_sequence(pivot_inv, owned, length, width)
    shaped_blocks = blocks.reshape(nfaces, nblocks, width, width)

    def apply_a(vec):
        shaped = vec.reshape(width, 1, 1, nfaces)
        span_side = with_halo(shaped, (("span", 1),), 1, True)
        plane_side = with_halo(shaped, (("plane", 2),), 1, False)
        below = plane_side[:, 0, 0]
        above = plane_side[:, 0, 2]
        table = jnp.concatenate([vec, span_side[:, 0, 0], span_side[:, 2, 0], below, above], axis=1)
        return jnp.einsum("ikab,bki->ai", shaped_blocks, table[:, position], precision=HIGH)

    def apply_m(vec):
        pieces = vec[:, slot].reshape(width, lines_group, P_SIZE)
        whole = lax.all_to_all(pieces, "plane", split_axis=1, concat_axis=2, tiled=True)
        solved = line_solve(whole, lower, upper, pivot)
        back = lax.all_to_all(solved, "plane", split_axis=2, concat_axis=1, tiled=True)
        return jnp.zeros_like(vec).at[:, slot].set(back.reshape(width, nfaces))

    beta = jnp.sqrt(lax.psum(jnp.sum(rhs * rhs), ("span", "plane")) + EPS)
    basis = [rhs / beta]
    hcols = []
    for step in range(ITERS):
        wvec = apply_a(apply_m(basis[step]))
        stacked = jnp.stack(basis)
        hvals = lax.psum(jnp.einsum("jai,ai->j", stacked, wvec, precision=HIGH), ("span", "plane"))
        wvec = wvec - jnp.einsum("j,jai->ai", hvals, stacked, precision=HIGH)
        hnext = jnp.sqrt(lax.psum(jnp.sum(wvec * wvec), ("span", "plane")) + EPS)
        basis.append(wvec / hnext)
        hcols.append(jnp.concatenate([hvals, hnext[None], jnp.zeros((ITERS - step - 1,), F32)]))
    hmat = jnp.stack(hcols, axis=1)
    factor = jnp.linalg.cholesky(jnp.dot(hmat.T, hmat, precision=HIGH))
    coef = small_solve(factor, beta * hmat[0])
    update = jnp.einsum("j,jai->ai", coef, jnp.stack(basis[:ITERS]), precision=HIGH)
    solution = apply_m(update)
    return solution, rhs - apply_a(solution)


def partner(me, k, size):
    if size & (size - 1) == 0:
        return me ^ k, me ^ k
    return (me + k) % size, (me + size - k) % size


def exchange(x, axis, k):
    size = lax.axis_size(axis)
    return lax.ppermute(x, axis, [(i, partner(i, k, size)[0]) for i in range(size)])


def split(x, parts):
    out = []
    for _ in range(parts):
        out.append(x.astype(BF16).astype(F32))
        x = x - out[-1]
    return jnp.concatenate(out, axis=0)


def start_kernel(nplane, slot_ref, u_ref, copy_ref, choose_ref, *outs):
    nfaces = u_ref.shape[0]
    per = nfaces // nplane
    me = lax.axis_index("plane")
    for k in range(nplane):
        to, _ = partner(me, k, nplane)
        for i in range(per):
            outs[k][pl.ds(i, 1), :] = u_ref[pl.ds(slot_ref[0, to * per + i], 1), :]
    copy_ref[...] = u_ref[...]
    face = lax.broadcasted_iota(jnp.int32, choose_ref.shape, 0)
    piece = lax.broadcasted_iota(jnp.int32, choose_ref.shape, 1) % nfaces
    choose = jnp.zeros(choose_ref.shape, F32)
    for k in range(nplane):
        _, source = partner(me, k, nplane)
        for i in range(per):
            hit = (face == slot_ref[0, source * per + i]) & (piece == k * per + i)
            choose = jnp.where(hit, 1.0, choose)
    choose_ref[...] = choose


def square_kernel(length, low, upp, piv, _, low_out, upp_out, piv_out, low_scr, upp_scr, piv_scr, sems):
    nrows, width = low.shape[0], low_out.shape[1]
    chunk = math.lcm(width, 128)
    work = ((low, low_scr, low_out), (piv, piv_scr, piv_out), (upp, upp_scr, upp_out))
    fetches = [pltpu.make_async_copy(src, scr, sems.at[n]) for n, (src, scr, _) in enumerate(work)]
    for fetch in fetches:
        fetch.start()
    for fetch, (src, scr, dst) in zip(fetches, work):
        fetch.wait()
        for c in range(width * width // chunk):
            piece = scr[:, c * chunk : (c + 1) * chunk]
            for r in range(chunk // width):
                a = c * (chunk // width) + r
                dst[pl.ds(a, nrows, stride=width), :] = piece[:, r * width : (r + 1) * width]
        for at in range(nrows):
            here = slice(at * width, (at + 1) * width)
            if src is piv or (src is low and at % length % 2 == 0 and at % length):
                dst[here, :] = dst[here, :].T


def parities():
    return [1 if lax.axis_size(a) % 2 else lax.axis_index(a) % 2 for a in ("span", "plane")]


def early_blocks():
    span_odd, plane_odd = parities()
    return (1 + span_odd, 3 + plane_odd), (2 - span_odd, 4 - plane_odd)


def pick_kernel(nspan, nplane, columns_ref, early_ref, late_ref):
    nblocks, nfaces = columns_ref.shape
    span, plane = lax.axis_index("span"), lax.axis_index("plane")
    position = table_positions(columns_ref[...], nfaces, span, plane, nspan, nplane)
    selector, face = position // nfaces, position % nfaces
    span_odd, plane_odd = [parity == 1 for parity in parities()]
    of_span = jnp.where((selector == 1) == span_odd, 1, 3)
    of_plane = jnp.where((selector == 3) == plane_odd, 2, 4)
    group = jnp.where(selector == 0, 0, jnp.where(selector <= 2, of_span, of_plane))
    at = (group * nfaces + face).astype(F32)
    eye = lax.broadcasted_iota(jnp.int32, (nfaces, nfaces), 0) == lax.broadcasted_iota(jnp.int32, (nfaces, nfaces), 1)
    first, second = jnp.where(span_odd, at[2:3], at[1:2]), jnp.where(span_odd, at[1:2], at[2:3])
    third, fourth = jnp.where(plane_odd, at[4:5], at[3:4]), jnp.where(plane_odd, at[3:4], at[4:5])
    rest = [at[k : k + 1] for k in range(5, nblocks)]
    for ref, rows in ((early_ref, [at[0:1], first, third]), (late_ref, [second, fourth, *rest])):
        lane = lax.broadcasted_iota(jnp.int32, (nfaces, ref.shape[1]), 1) % (ref.shape[1] // 2)
        for n, row in enumerate(rows):
            column = jnp.sum(jnp.where(eye, row, 0.0), axis=1, keepdims=True).astype(jnp.int32)
            ref[n * nfaces : (n + 1) * nfaces, :] = jnp.where(lane == column, 1.0, 0.0).astype(BF16)


def line_kernel(nplane, nlines, *refs):
    msgs, (low, upp, piv_t), outs, (r_scr, z_scr) = refs[:nplane], refs[nplane:-nplane-2], refs[-nplane-2:-2], refs[-2:]
    _, length, width = r_scr.shape
    me = lax.axis_index("plane")
    for k in range(nplane):
        _, source = partner(me, k, nplane)
        for m in range(nlines):
            for q in range(P_SIZE):
                r_scr[m, pl.ds(source * P_SIZE + q, 1), :] = msgs[k][pl.ds(m * P_SIZE + q, 1), :]
    eye = lax.broadcasted_iota(jnp.int32, (width, width), 0) == lax.broadcasted_iota(jnp.int32, (width, width), 1)

    def column(row):
        return jnp.sum(jnp.where(eye, row, 0.0), axis=1, keepdims=True)

    rows = [[r_scr[m, pl.ds(j, 1), :] for m in range(nlines)] for j in range(length)]
    y_cols = [[None] * nlines for _ in range(length)]
    carry = [None] * nlines
    for j in range(length):
        for m in range(nlines):
            at = m * length + j
            if j == 0:
                carry[m] = rows[j][m]
            elif j % 2:
                carry[m] = column(rows[j][m]) - jnp.sum(low[at] * carry[m], axis=1, keepdims=True)
            else:
                carry[m] = rows[j][m] - jnp.sum(low[at] * carry[m], axis=0, keepdims=True)
            y_cols[j][m] = carry[m] if j % 2 else column(carry[m])
    after = [None] * nlines
    for j in reversed(range(length)):
        for m in range(nlines):
            at = m * length + j
            inner = y_cols[j][m]
            if j < length - 1:
                inner = inner - jnp.sum(upp[at] * after[m], axis=1, keepdims=True)
            after[m] = jnp.sum(piv_t[at] * inner, axis=0, keepdims=True)
            z_scr[m, pl.ds(j, 1), :] = after[m]
    for k in range(nplane):
        to, _ = partner(me, k, nplane)
        for m in range(nlines):
            for q in range(P_SIZE):
                outs[k][pl.ds(m * P_SIZE + q, 1), :] = z_scr[m, pl.ds(to * P_SIZE + q, 1), :]


def faces_kernel(choose, *refs):
    solved, mine_ref = refs[:-1], refs[-1]
    table = split(jnp.concatenate([s[...] for s in solved], axis=0), 3).astype(BF16)
    mine_ref[...] = jnp.dot(choose[...].astype(BF16), table, preferred_element_type=F32)


def repeat_faces(faces, pick, copies):
    both = split(jnp.concatenate([f[...] for f in faces], axis=0), 2).astype(BF16)
    picked = jnp.dot(pick[...], both, preferred_element_type=F32)
    return jnp.concatenate([picked] * copies, axis=1)


def add_products(work, x_scr, acc_scr, parts, width):
    nfaces, area = acc_scr.shape
    chunk = x_scr.shape[1]
    copies, count = chunk // width, area // chunk
    lane = lax.broadcasted_iota(jnp.int32, (1, 128), 1)
    seg = [jnp.broadcast_to(jnp.where(lane % copies == r, 1.0, 0.0), (width, 128)) for r in range(copies)]
    seg = jnp.concatenate(seg, axis=0).astype(BF16)
    total = jnp.zeros((nfaces, 128), F32)
    done = 0
    for n, (places, fetch) in enumerate(work):
        if fetch is not None:
            fetch.wait()
        last = n == len(work) - 1
        for half in ((0, count // 2), (count // 2, count)):
            for v in range(0, chunk, 128):
                rows = range(done * nfaces, (done + len(places)) * nfaces, nfaces)
                xs = [x_scr[row : row + nfaces, v : v + 128] for row in rows]
                for c in range(*half):
                    at = c * chunk + v
                    value = acc_scr[:, at : at + 128] if n else None
                    for (ref, column), x in zip(places, xs):
                        term = ref[:, column + at : column + at + 128] * x
                        value = term if value is None else value + term
                    if not last:
                        acc_scr[:, at : at + 128] = value
                        continue
                    high = value.astype(BF16)
                    row = 2 * c * nfaces
                    parts[row : row + nfaces, v : v + 128] = high
                    parts[row + nfaces : row + 2 * nfaces, v : v + 128] = (value - high.astype(F32)).astype(BF16)
            if last:
                base = 2 * half[0] * nfaces
                sums = jnp.dot(parts[base : 2 * half[1] * nfaces, :], seg, preferred_element_type=F32)
                for c in range(*half):
                    at = 2 * c * nfaces - base
                    pair = sums[at : at + nfaces] + sums[at + nfaces : at + 2 * nfaces]
                    total = total + jnp.where(lane // copies == c, pair, 0.0)
        done += len(places)
    return total[:, :width]


def early_kernel(nblocks, blocks, pick, *refs):
    faces, (sum_ref, held, buf, x_scr, acc_scr, parts, sems) = refs[:3], refs[3:]
    width = faces[0].shape[1]
    area = width * width
    early, late = early_blocks()

    def fetch(k, count, dst, column, n):
        start = pl.multiple_of(k * area, 128) if not isinstance(k, int) else k * area
        return pltpu.make_async_copy(
            blocks.at[:, pl.ds(start, count * area)], dst.at[:, pl.ds(column, count * area)], sems.at[n]
        )

    mine = [fetch(k, 1, buf, n * area, n) for n, k in enumerate((0, *early))]
    kept = [fetch(k, 1, held, n * area, 3 + n) for n, k in enumerate(late)]
    kept.append(fetch(5, nblocks - 5, held, 2 * area, 5))
    for copy in mine + kept:
        copy.start()
    x_scr[...] = repeat_faces(faces, pick, x_scr.shape[1] // width)
    work = [([(buf, n * area)], copy) for n, copy in enumerate(mine)]
    sum_ref[...] = add_products(work, x_scr, acc_scr, parts, width)
    for copy in kept:
        copy.wait()


def late_kernel(nplane, last, *refs):
    (slot, held, pick, early_sum), faces, refs = refs[:4], refs[4:9], refs[9:]
    nold = ITERS if last else 1
    olds, refs = refs[:nold], refs[nold:]
    next_ref, outs, (x_scr, acc_scr, parts, slot_scr, slot_sem) = refs[0], refs[1:-5], refs[-5:]
    nfaces, width = faces[0].shape
    area = width * width
    if not last:
        slots = pltpu.make_async_copy(slot, slot_scr, slot_sem)
        slots.start()
    x_scr[...] = repeat_faces(faces, pick, x_scr.shape[1] // width)
    work = [([(held, column) for column in range(0, held.shape[1], area)], None)]
    u_next = early_sum[...] + add_products(work, x_scr, acc_scr, parts, width) - SHIFT * olds[-1][...]
    next_ref[...] = u_next
    if last:
        gram_ref = outs[0]
        lane = lax.broadcasted_iota(jnp.int32, gram_ref.shape, 1)
        basis = [old[...] for old in olds] + [u_next]
        gram, at = jnp.zeros(gram_ref.shape, F32), 0
        for i in range(ITERS + 1):
            for j in range(i, ITERS + 1):
                value = jnp.sum(jnp.sum(basis[i] * basis[j], axis=0, keepdims=True), axis=1, keepdims=True)
                gram, at = jnp.where(lane == at, value, gram), at + 1
        gram_ref[...] = gram
    else:
        per = nfaces // nplane
        me = lax.axis_index("plane")
        slots.wait()
        for k in range(nplane):
            to, _ = partner(me, k, nplane)
            for i in range(per):
                outs[k][pl.ds(i, 1), :] = next_ref[pl.ds(slot_scr[0, to * per + i], 1), :]


def finish_kernel(gram_ref, *refs):
    us, zs = refs[: ITERS + 1], refs[ITERS + 1 : 2 * ITERS + 1]
    sol_ref, res_ref, ok_ref = refs[2 * ITERS + 1 :]
    width = sol_ref.shape[1]
    rows = jnp.sum(gram_ref[...], axis=0, keepdims=True)
    lane = lax.broadcasted_iota(jnp.int32, rows.shape, 1)
    gram, at = {}, 0
    for i in range(ITERS + 1):
        for j in range(i, ITERS + 1):
            value = jnp.sum(jnp.where(lane == at, rows, 0.0), axis=1, keepdims=True)
            gram[i, j] = gram[j, i] = jnp.broadcast_to(value, rows.shape)
            at += 1
    largest = functools.reduce(jnp.maximum, [jnp.abs(g) for g in gram.values()])
    ok = largest < 1e30
    beta = jnp.sqrt(gram[0, 0] + EPS)
    basis = [[1.0 / beta]]
    hmat = {}
    for step in range(ITERS):
        own = basis[step]
        wvec = [SHIFT * own[0]] + [own[i] + SHIFT * own[i + 1] for i in range(step)] + [own[step]]
        images = [sum(gram[i, j] * wvec[j] for j in range(step + 2)) for i in range(step + 1)]
        for i in range(step + 1):
            hmat[i, step] = sum(basis[i][m] * images[m] for m in range(i + 1))
        for i in range(step + 1):
            for m in range(i + 1):
                wvec[m] = wvec[m] - hmat[i, step] * basis[i][m]
        terms = [wvec[i] * wvec[j] * gram[i, j] for i in range(step + 2) for j in range(step + 2)]
        square = jnp.maximum(sum(terms), 0.0)
        ok = ok & (square + EPS >= 2e-3 * sum(jnp.abs(term) for term in terms))
        hmat[step + 1, step] = jnp.sqrt(square + EPS)
        scale = 1.0 / hmat[step + 1, step]
        basis.append([w * scale for w in wvec])
    normal = {
        (i, j): sum(hmat[m, i] * hmat[m, j] for m in range(j + 2) if (m, i) in hmat and (m, j) in hmat)
        for i in range(ITERS)
        for j in range(i + 1)
    }
    factor, inverse = {}, []
    for j in range(ITERS):
        diag = jnp.sqrt(normal[j, j] - sum(factor[j, m] * factor[j, m] for m in range(j)))
        inverse.append(1.0 / diag)
        for i in range(j + 1, ITERS):
            factor[i, j] = (normal[i, j] - sum(factor[i, m] * factor[j, m] for m in range(j))) * inverse[j]
    forward = []
    for i in range(ITERS):
        forward.append((beta * hmat[0, i] - sum(factor[i, m] * forward[m] for m in range(i))) * inverse[i])
    coef = [None] * ITERS
    for i in reversed(range(ITERS)):
        coef[i] = (forward[i] - sum(factor[m, i] * coef[m] for m in range(i + 1, ITERS))) * inverse[i]
    mix = [sum(coef[s] * basis[s][m] for s in range(m, ITERS))[:, :width] for m in range(ITERS)]
    sol_ref[...] = sum(mix[m] * zs[m][...] for m in range(ITERS))
    image = sum(mix[m] * (us[m + 1][...] + SHIFT * us[m][...]) for m in range(ITERS))
    res_ref[...] = us[0][...] - image
    ok = ok & (functools.reduce(jnp.maximum, [jnp.abs(c) for c in coef]) < 1e30)
    ok_ref[...] = jnp.where(ok, 1.0, 0.0)


def call(kernel, args, outs, spaces=None, scratch=(), flops=0, pinned=True, ready=True, kind=F32):
    spaces = [pltpu.VMEM] * len(args) if spaces is None else spaces
    if ready:
        args = [pltpu.with_memory_space_constraint(x, s) if s is pltpu.VMEM else x for x, s in zip(args, spaces)]
    size = sum(x.dtype.itemsize * math.prod(x.shape) for x in args)
    return pl.pallas_call(
        kernel,
        out_shape=[pltpu.VMEM(shape, kind) if pinned else jax.ShapeDtypeStruct(shape, kind) for shape in outs],
        in_specs=[pl.BlockSpec(memory_space=s) for s in spaces],
        out_specs=[pl.BlockSpec(memory_space=pltpu.VMEM) for _ in outs],
        scratch_shapes=scratch,
        compiler_params=pltpu.CompilerParams(vmem_limit_bytes=VMEM_LIMIT),
        cost_estimate=pl.CostEstimate(flops=flops, bytes_accessed=size, transcendentals=0),
    )(*args)


def add_up(x):
    return lax.all_gather(x, ("span", "plane"), axis=0, tiled=True)


def pairings(size):
    if size % 2:
        return [(i, (i + 1) % size) for i in range(size)], [(i, (i - 1) % size) for i in range(size)]
    return [(i, i ^ 1) for i in range(size)], [(i, (i + 1 if i % 2 else i - 1) % size) for i in range(size)]


def on_device(rhs, blocks, columns, line_slot, line_lower, line_upper, pivot_inv):
    width, nfaces = rhs.shape
    nblocks = columns.shape[0]
    nspan, nplane = lax.axis_size("span"), lax.axis_size("plane")
    owned = nfaces // P_SIZE // nplane
    length = P_SIZE * nplane
    per = owned * P_SIZE
    area = width * width
    shape = (nfaces, width)
    span_pairs, span_others = pairings(nspan)
    plane_pairs, plane_others = pairings(nplane)

    u_first, choose, *send = call(
        functools.partial(start_kernel, nplane),
        [line_slot, rhs.T],
        [shape, (nfaces, 3 * nfaces)] + [(per, width)] * nplane,
        [pltpu.SMEM, pltpu.VMEM],
        ready=False,
    )
    us = [u_first]
    zs = []
    picks = None
    for step in range(ITERS):
        factors = call(
            functools.partial(square_kernel, length),
            [line_lower, line_upper, pivot_inv, us[-1]],
            [(nfaces * width, width)] * 3,
            [pl.ANY] * 4,
            [pltpu.VMEM((nfaces, area), F32)] * 3 + [pltpu.SemaphoreType.DMA((3,))],
            flops=nfaces * area,
        )
        factors = [x.reshape(nfaces, width, width) for x in factors]
        got = [send[0]] + [exchange(send[k], "plane", k) for k in range(1, nplane)]
        solved = call(
            functools.partial(line_kernel, nplane, owned),
            [*got, *factors],
            [(per, width)] * nplane,
            scratch=[pltpu.VMEM((owned, length, width), F32)] * 2,
            flops=6 * nfaces * area,
        )
        if step == 0:
            picks = call(
                functools.partial(pick_kernel, nspan, nplane),
                [lax.optimization_barrier((columns, solved[0]))[0]],
                [(3 * nfaces, 6 * nfaces), ((nblocks - 3) * nfaces, 10 * nfaces)],
                ready=False,
                kind=BF16,
            )
        pieces = [solved[0]] + [exchange(solved[k], "plane", k) for k in range(1, nplane)]
        (mine,) = call(faces_kernel, [choose, *pieces], [shape])
        zs.append(mine)
        other = lax.ppermute(mine, "span", span_others)
        near = [mine, lax.ppermute(mine, "span", span_pairs), lax.ppermute(mine, "plane", plane_pairs)]
        far = [other, lax.ppermute(mine, "plane", plane_others)]
        chunk = math.lcm(width, 128)

        def scratch(count):
            return [
                pltpu.VMEM((count * nfaces, chunk), F32),
                pltpu.VMEM((nfaces, area), F32),
                pltpu.VMEM((2 * nfaces * area // chunk, chunk), BF16),
            ]

        early_sum, held = call(
            functools.partial(early_kernel, nblocks),
            [blocks, picks[0], *near],
            [shape, (nfaces, (nblocks - 3) * area)],
            [pl.ANY] + [pltpu.VMEM] * 4,
            [pltpu.VMEM((nfaces, 3 * area), F32)] + scratch(3) + [pltpu.SemaphoreType.DMA((6,))],
            flops=6 * nfaces * area,
        )
        last = step == ITERS - 1
        args = [line_slot, held, picks[1], early_sum, *near, *far, *(us if last else us[-1:])]
        out = call(
            functools.partial(late_kernel, nplane, last),
            args,
            [shape] + ([(1, 128)] if last else [(per, width)] * nplane),
            [pl.ANY] + [pltpu.VMEM] * (len(args) - 1),
            scratch(nblocks - 3) + [pltpu.SMEM(line_slot.shape, jnp.int32), pltpu.SemaphoreType.DMA],
            flops=2 * nblocks * nfaces * area,
        )
        us.append(out[0])
        send = out[1:]
    gram = add_up(send[0])
    sol, res, ok = call(finish_kernel, [gram, *us, *zs], [shape, shape, (1, 128)], pinned=False)
    given = (rhs, blocks, columns, line_slot, line_lower, line_upper, pivot_inv)
    _, sol, res = lax.while_loop(
        lambda state: state[0], lambda _: (jnp.array(False), *step_by_step(*given)), (ok[0, 0] < 0.5, sol.T, res.T)
    )
    return sol, res


def solution(mesh):
    both = ("span", "plane")
    return jax.shard_map(
        on_device,
        mesh=mesh,
        in_specs=(
            P(None, both),
            P(both, None),
            P(None, both),
            P(both, None),
            P(both, None),
            P(both, None),
            P(both, None),
        ),
        out_specs=(P(None, both), P(None, both)),
        check_vma=False,
    )
```

```python
import functools
import math

import jax
import jax.numpy as jnp
import numpy as np
from jax import lax
from jax.experimental import pallas as pl
from jax.experimental.pallas import tpu as pltpu
from jax.sharding import PartitionSpec as P

ITERS = 3
P_SIZE = 2
SHIFT = 2.0
EPS = 1e-6
VMEM_LIMIT = 16 * 1024 * 1024
HIGH = lax.Precision.HIGHEST
F32, BF16 = jnp.float32, jnp.bfloat16


def with_halo(x, sides, width, wrap):
    for axis, dim in sides:
        size, length = (lax.axis_size(axis), x.shape[dim])
        up = [(i, (i + 1) % size) for i in range(size if wrap else size - 1)]
        down = [(j, i) for i, j in up]
        last = lax.slice_in_dim(x, length - width, length, axis=dim)
        first = lax.slice_in_dim(x, 0, width, axis=dim)
        before = lax.ppermute(last, axis, up)
        after = lax.ppermute(first, axis, down)
        x = jnp.concatenate([before, x, after], axis=dim)
    return x


def small_solve(factor, target):
    extent = target.shape[0]
    forward_vals = []
    for row in range(extent):
        running = target[row]
        for inner in range(row):
            running = running - factor[row, inner] * forward_vals[inner]
        forward_vals.append(running / factor[row, row])
    backward_vals = [None] * extent
    for row in reversed(range(extent)):
        running = forward_vals[row]
        for inner in range(row + 1, extent):
            running = running - factor[inner, row] * backward_vals[inner]
        backward_vals[row] = running / factor[row, row]
    return jnp.stack(backward_vals)


def to_sequence(factor_rows, nlines, length, width):
    return jnp.swapaxes(factor_rows.reshape(nlines, length, width, width), 0, 1)


def line_solve(rhs_lines, lseq, useq, pseq):
    rseq = jnp.moveaxis(rhs_lines, 2, 0)

    def forward(prev, items):
        right, low = items
        cur = right - jnp.einsum("mab,bm->am", low, prev, precision=HIGH)
        return (cur, cur)

    start = jnp.zeros(rseq.shape[1:], F32)
    _, yseq = lax.scan(forward, start, (rseq, lseq))

    def backward(nxt, items):
        yval, upp, piv = items
        inner = yval - jnp.einsum("mab,bm->am", upp, nxt, precision=HIGH)
        cur = jnp.einsum("mab,bm->am", piv, inner, precision=HIGH)
        return (cur, cur)

    _, zseq = lax.scan(backward, start, (yseq, useq, pseq), reverse=True)
    return jnp.moveaxis(zseq, 0, 2)


def table_positions(columns, nfaces, my_span, my_plane, nspan, nplane):
    device_of = columns // nfaces
    span_of = device_of // nplane
    plane_of = device_of % nplane
    dspan = (span_of - my_span + 1 + nspan) % nspan - 1
    dplane = plane_of - my_plane
    selector = jnp.where(
        dspan == -1,
        1,
        jnp.where(dspan == 1, 2, jnp.where(dplane == -1, 3, jnp.where(dplane == 1, 4, 0))),
    )
    return selector * nfaces + columns % nfaces


def step_by_step(rhs, blocks, columns, line_slot, line_lower, line_upper, pivot_inv):
    width, nfaces = rhs.shape
    nblocks = columns.shape[0]
    nplane = lax.axis_size("plane")
    position = table_positions(
        columns, nfaces, lax.axis_index("span"), lax.axis_index("plane"), lax.axis_size("span"), nplane
    )
    slot = line_slot[0]
    lines_group = nfaces // P_SIZE
    owned = lines_group // nplane
    length = P_SIZE * nplane
    lower = to_sequence(line_lower, owned, length, width)
    upper = to_sequence(line_upper, owned, length, width)
    pivot = to_sequence(pivot_inv, owned, length, width)
    shaped_blocks = blocks.reshape(nfaces, nblocks, width, width)

    def apply_a(vec):
        shaped = vec.reshape(width, 1, 1, nfaces)
        span_side = with_halo(shaped, (("span", 1),), 1, True)
        plane_side = with_halo(shaped, (("plane", 2),), 1, False)
        below = plane_side[:, 0, 0]
        above = plane_side[:, 0, 2]
        table = jnp.concatenate([vec, span_side[:, 0, 0], span_side[:, 2, 0], below, above], axis=1)
        return jnp.einsum("ikab,bki->ai", shaped_blocks, table[:, position], precision=HIGH)

    def apply_m(vec):
        pieces = vec[:, slot].reshape(width, lines_group, P_SIZE)
        whole = lax.all_to_all(pieces, "plane", split_axis=1, concat_axis=2, tiled=True)
        solved = line_solve(whole, lower, upper, pivot)
        back = lax.all_to_all(solved, "plane", split_axis=2, concat_axis=1, tiled=True)
        return jnp.zeros_like(vec).at[:, slot].set(back.reshape(width, nfaces))

    beta = jnp.sqrt(lax.psum(jnp.sum(rhs * rhs), ("span", "plane")) + EPS)
    basis = [rhs / beta]
    hcols = []
    for step in range(ITERS):
        wvec = apply_a(apply_m(basis[step]))
        stacked = jnp.stack(basis)
        hvals = lax.psum(jnp.einsum("jai,ai->j", stacked, wvec, precision=HIGH), ("span", "plane"))
        wvec = wvec - jnp.einsum("j,jai->ai", hvals, stacked, precision=HIGH)
        hnext = jnp.sqrt(lax.psum(jnp.sum(wvec * wvec), ("span", "plane")) + EPS)
        basis.append(wvec / hnext)
        hcols.append(jnp.concatenate([hvals, hnext[None], jnp.zeros((ITERS - step - 1,), F32)]))
    hmat = jnp.stack(hcols, axis=1)
    factor = jnp.linalg.cholesky(jnp.dot(hmat.T, hmat, precision=HIGH))
    coef = small_solve(factor, beta * hmat[0])
    update = jnp.einsum("j,jai->ai", coef, jnp.stack(basis[:ITERS]), precision=HIGH)
    solution = apply_m(update)
    return solution, rhs - apply_a(solution)


def partner(me, k, size):
    if size & (size - 1) == 0:
        return me ^ k, me ^ k
    return (me + k) % size, (me + size - k) % size


def far_first(size):
    return list(reversed(range(size)))


def exchange(x, axis, k):
    size = lax.axis_size(axis)
    return lax.ppermute(x, axis, [(i, partner(i, k, size)[0]) for i in range(size)])


def split(x, parts):
    out = []
    for _ in range(parts):
        out.append(x.astype(BF16).astype(F32))
        x = x - out[-1]
    return jnp.concatenate(out, axis=0)


def start_kernel(nplane, slot_ref, u_ref, copy_ref, choose_ref, *outs):
    nfaces = u_ref.shape[0]
    per = nfaces // nplane
    me = lax.axis_index("plane")
    for k in range(nplane):
        to, _ = partner(me, k, nplane)
        for i in range(per):
            outs[k][pl.ds(i, 1), :] = u_ref[pl.ds(slot_ref[0, to * per + i], 1), :]
    copy_ref[...] = u_ref[...]
    face = lax.broadcasted_iota(jnp.int32, choose_ref.shape, 0)
    piece = lax.broadcasted_iota(jnp.int32, choose_ref.shape, 1) % nfaces
    choose = jnp.zeros(choose_ref.shape, F32)
    for n, k in enumerate(far_first(nplane)):
        _, source = partner(me, k, nplane)
        for i in range(per):
            hit = (face == slot_ref[0, source * per + i]) & (piece == n * per + i)
            choose = jnp.where(hit, 1.0, choose)
    choose_ref[...] = choose


def square_kernel(length, low, upp, piv, _, low_out, upp_out, piv_out, low_scr, upp_scr, piv_scr, sems):
    nrows, width = low.shape[0], low_out.shape[1]
    chunk = math.lcm(width, 128)
    work = ((low, low_scr, low_out), (piv, piv_scr, piv_out), (upp, upp_scr, upp_out))
    fetches = [pltpu.make_async_copy(src, scr, sems.at[n]) for n, (src, scr, _) in enumerate(work)]
    for fetch in fetches:
        fetch.start()
    for fetch, (src, scr, dst) in zip(fetches, work):
        fetch.wait()
        for c in range(width * width // chunk):
            piece = scr[:, c * chunk : (c + 1) * chunk]
            for r in range(chunk // width):
                a = c * (chunk // width) + r
                dst[pl.ds(a, nrows, stride=width), :] = piece[:, r * width : (r + 1) * width]
        for at in range(nrows):
            here = slice(at * width, (at + 1) * width)
            if src is piv or (src is low and at % length % 2 == 0 and at % length):
                dst[here, :] = dst[here, :].T


def parities():
    return [1 if lax.axis_size(a) % 2 else lax.axis_index(a) % 2 for a in ("span", "plane")]


def early_blocks():
    span_odd, plane_odd = parities()
    return (1 + span_odd, 3 + plane_odd), (2 - span_odd, 4 - plane_odd)


def pick_kernel(nspan, nplane, columns_ref, early_ref, late_ref):
    nblocks, nfaces = columns_ref.shape
    span, plane = lax.axis_index("span"), lax.axis_index("plane")
    position = table_positions(columns_ref[...], nfaces, span, plane, nspan, nplane)
    selector, face = position // nfaces, position % nfaces
    span_odd, plane_odd = [parity == 1 for parity in parities()]
    of_span = jnp.where((selector == 1) == span_odd, 1, 3)
    of_plane = jnp.where((selector == 3) == plane_odd, 2, 4)
    group = jnp.where(selector == 0, 0, jnp.where(selector <= 2, of_span, of_plane))
    at = (group * nfaces + face).astype(F32)
    eye = lax.broadcasted_iota(jnp.int32, (nfaces, nfaces), 0) == lax.broadcasted_iota(jnp.int32, (nfaces, nfaces), 1)
    first, second = jnp.where(span_odd, at[2:3], at[1:2]), jnp.where(span_odd, at[1:2], at[2:3])
    third, fourth = jnp.where(plane_odd, at[4:5], at[3:4]), jnp.where(plane_odd, at[3:4], at[4:5])
    rest = [at[k : k + 1] for k in range(5, nblocks)]
    for ref, rows in ((early_ref, [at[0:1], first, third]), (late_ref, [second, fourth, *rest])):
        lane = lax.broadcasted_iota(jnp.int32, (nfaces, ref.shape[1]), 1) % (ref.shape[1] // 2)
        for n, row in enumerate(rows):
            column = jnp.sum(jnp.where(eye, row, 0.0), axis=1, keepdims=True).astype(jnp.int32)
            ref[n * nfaces : (n + 1) * nfaces, :] = jnp.where(lane == column, 1.0, 0.0).astype(BF16)


def line_kernel(nplane, nlines, *refs):
    msgs, (low, upp, piv_t), outs, (r_scr, z_scr) = refs[:nplane], refs[nplane:-nplane-2], refs[-nplane-2:-2], refs[-2:]
    _, length, width = r_scr.shape
    me = lax.axis_index("plane")
    for k, msg in zip(far_first(nplane), msgs):
        _, source = partner(me, k, nplane)
        for m in range(nlines):
            for q in range(P_SIZE):
                r_scr[m, pl.ds(source * P_SIZE + q, 1), :] = msg[pl.ds(m * P_SIZE + q, 1), :]
    eye = lax.broadcasted_iota(jnp.int32, (width, width), 0) == lax.broadcasted_iota(jnp.int32, (width, width), 1)

    def column(row):
        return jnp.sum(jnp.where(eye, row, 0.0), axis=1, keepdims=True)

    rows = [[r_scr[m, pl.ds(j, 1), :] for m in range(nlines)] for j in range(length)]
    y_cols = [[None] * nlines for _ in range(length)]
    carry = [None] * nlines
    for j in range(length):
        for m in range(nlines):
            at = m * length + j
            if j == 0:
                carry[m] = rows[j][m]
            elif j % 2:
                carry[m] = column(rows[j][m]) - jnp.sum(low[at] * carry[m], axis=1, keepdims=True)
            else:
                carry[m] = rows[j][m] - jnp.sum(low[at] * carry[m], axis=0, keepdims=True)
            y_cols[j][m] = carry[m] if j % 2 else column(carry[m])
    after = [None] * nlines
    for j in reversed(range(length)):
        for m in range(nlines):
            at = m * length + j
            inner = y_cols[j][m]
            if j < length - 1:
                inner = inner - jnp.sum(upp[at] * after[m], axis=1, keepdims=True)
            after[m] = jnp.sum(piv_t[at] * inner, axis=0, keepdims=True)
            z_scr[m, pl.ds(j, 1), :] = after[m]
    for k in range(nplane):
        to, _ = partner(me, k, nplane)
        for m in range(nlines):
            for q in range(P_SIZE):
                outs[k][pl.ds(m * P_SIZE + q, 1), :] = z_scr[m, pl.ds(to * P_SIZE + q, 1), :]


def faces_kernel(nplane, choose, *refs):
    solved, mine_ref = refs[:nplane], refs[-1]
    table = split(jnp.concatenate([s[...] for s in solved], axis=0), 3).astype(BF16)
    mine_ref[...] = jnp.dot(choose[...].astype(BF16), table, preferred_element_type=F32)


def repeat_faces(faces, pick, copies):
    both = split(jnp.concatenate([f[...] for f in faces], axis=0), 2).astype(BF16)
    picked = jnp.dot(pick[...], both, preferred_element_type=F32)
    return jnp.concatenate([picked] * copies, axis=1)


def add_products(work, x_scr, acc_scr, parts, width):
    nfaces, area = acc_scr.shape
    chunk = x_scr.shape[1]
    copies, count = chunk // width, area // chunk
    lane = lax.broadcasted_iota(jnp.int32, (1, 128), 1)
    seg = [jnp.broadcast_to(jnp.where(lane % copies == r, 1.0, 0.0), (width, 128)) for r in range(copies)]
    seg = jnp.concatenate(seg, axis=0).astype(BF16)
    total = jnp.zeros((nfaces, 128), F32)
    done = 0
    for n, (places, fetch) in enumerate(work):
        if fetch is not None:
            fetch.wait()
        last = n == len(work) - 1
        for half in ((0, count // 2), (count // 2, count)):
            for v in range(0, chunk, 128):
                rows = range(done * nfaces, (done + len(places)) * nfaces, nfaces)
                xs = [x_scr[row : row + nfaces, v : v + 128] for row in rows]
                for c in range(*half):
                    at = c * chunk + v
                    value = acc_scr[:, at : at + 128] if n else None
                    for (ref, column), x in zip(places, xs):
                        term = ref[:, column + at : column + at + 128] * x
                        value = term if value is None else value + term
                    if not last:
                        acc_scr[:, at : at + 128] = value
                        continue
                    high = value.astype(BF16)
                    row = 2 * c * nfaces
                    parts[row : row + nfaces, v : v + 128] = high
                    parts[row + nfaces : row + 2 * nfaces, v : v + 128] = (value - high.astype(F32)).astype(BF16)
            if last:
                base = 2 * half[0] * nfaces
                sums = jnp.dot(parts[base : 2 * half[1] * nfaces, :], seg, preferred_element_type=F32)
                for c in range(*half):
                    at = 2 * c * nfaces - base
                    pair = sums[at : at + nfaces] + sums[at + nfaces : at + 2 * nfaces]
                    total = total + jnp.where(lane // copies == c, pair, 0.0)
        done += len(places)
    return total[:, :width]


def early_kernel(nblocks, blocks, pick, *refs):
    faces, (sum_ref, held, buf, x_scr, acc_scr, parts, sems) = refs[:3], refs[3:]
    width = faces[0].shape[1]
    area = width * width
    early, late = early_blocks()

    def fetch(k, count, dst, column, n):
        start = pl.multiple_of(k * area, 128) if not isinstance(k, int) else k * area
        return pltpu.make_async_copy(
            blocks.at[:, pl.ds(start, count * area)], dst.at[:, pl.ds(column, count * area)], sems.at[n]
        )

    mine = [fetch(k, 1, buf, n * area, n) for n, k in enumerate((0, *early))]
    kept = [fetch(k, 1, held, n * area, 3 + n) for n, k in enumerate(late)]
    kept.append(fetch(5, nblocks - 5, held, 2 * area, 5))
    for copy in mine + kept:
        copy.start()
    x_scr[...] = repeat_faces(faces, pick, x_scr.shape[1] // width)
    work = [([(buf, n * area)], copy) for n, copy in enumerate(mine)]
    sum_ref[...] = add_products(work, x_scr, acc_scr, parts, width)
    for copy in kept:
        copy.wait()


def late_kernel(nplane, last, *refs):
    (slot, held, pick, early_sum), faces, refs = refs[:4], refs[4:9], refs[9:]
    nold = ITERS if last else 1
    olds, refs = refs[:nold], refs[nold:]
    next_ref, outs, (x_scr, acc_scr, parts, slot_scr, slot_sem) = refs[0], refs[1:-5], refs[-5:]
    nfaces, width = faces[0].shape
    area = width * width
    if not last:
        slots = pltpu.make_async_copy(slot, slot_scr, slot_sem)
        slots.start()
    x_scr[...] = repeat_faces(faces, pick, x_scr.shape[1] // width)
    work = [([(held, column) for column in range(0, held.shape[1], area)], None)]
    u_next = early_sum[...] + add_products(work, x_scr, acc_scr, parts, width) - SHIFT * olds[-1][...]
    next_ref[...] = u_next
    if last:
        gram_ref = outs[0]
        lane = lax.broadcasted_iota(jnp.int32, gram_ref.shape, 1)
        basis = [old[...] for old in olds] + [u_next]
        gram, at = jnp.zeros(gram_ref.shape, F32), 0
        for i in range(ITERS + 1):
            for j in range(i, ITERS + 1):
                value = jnp.sum(jnp.sum(basis[i] * basis[j], axis=0, keepdims=True), axis=1, keepdims=True)
                gram, at = jnp.where(lane == at, value, gram), at + 1
        gram_ref[...] = gram
    else:
        per = nfaces // nplane
        me = lax.axis_index("plane")
        slots.wait()
        for k in range(nplane):
            to, _ = partner(me, k, nplane)
            for i in range(per):
                outs[k][pl.ds(i, 1), :] = next_ref[pl.ds(slot_scr[0, to * per + i], 1), :]


def finish_kernel(gram_ref, *refs):
    us, zs = refs[: ITERS + 1], refs[ITERS + 1 : 2 * ITERS + 1]
    sol_ref, res_ref, ok_ref = refs[2 * ITERS + 1 :]
    width = sol_ref.shape[1]
    rows = jnp.sum(gram_ref[...], axis=0, keepdims=True)
    lane = lax.broadcasted_iota(jnp.int32, rows.shape, 1)
    gram, at = {}, 0
    for i in range(ITERS + 1):
        for j in range(i, ITERS + 1):
            value = jnp.sum(jnp.where(lane == at, rows, 0.0), axis=1, keepdims=True)
            gram[i, j] = gram[j, i] = jnp.broadcast_to(value, rows.shape)
            at += 1
    largest = functools.reduce(jnp.maximum, [jnp.abs(g) for g in gram.values()])
    ok = largest < 1e30
    beta = jnp.sqrt(gram[0, 0] + EPS)
    basis = [[1.0 / beta]]
    hmat = {}
    for step in range(ITERS):
        own = basis[step]
        wvec = [SHIFT * own[0]] + [own[i] + SHIFT * own[i + 1] for i in range(step)] + [own[step]]
        images = [sum(gram[i, j] * wvec[j] for j in range(step + 2)) for i in range(step + 1)]
        for i in range(step + 1):
            hmat[i, step] = sum(basis[i][m] * images[m] for m in range(i + 1))
        for i in range(step + 1):
            for m in range(i + 1):
                wvec[m] = wvec[m] - hmat[i, step] * basis[i][m]
        terms = [wvec[i] * wvec[j] * gram[i, j] for i in range(step + 2) for j in range(step + 2)]
        square = jnp.maximum(sum(terms), 0.0)
        ok = ok & (square + EPS >= 2e-3 * sum(jnp.abs(term) for term in terms))
        hmat[step + 1, step] = jnp.sqrt(square + EPS)
        scale = 1.0 / hmat[step + 1, step]
        basis.append([w * scale for w in wvec])
    normal = {
        (i, j): sum(hmat[m, i] * hmat[m, j] for m in range(j + 2) if (m, i) in hmat and (m, j) in hmat)
        for i in range(ITERS)
        for j in range(i + 1)
    }
    factor, inverse = {}, []
    for j in range(ITERS):
        diag = jnp.sqrt(normal[j, j] - sum(factor[j, m] * factor[j, m] for m in range(j)))
        inverse.append(1.0 / diag)
        for i in range(j + 1, ITERS):
            factor[i, j] = (normal[i, j] - sum(factor[i, m] * factor[j, m] for m in range(j))) * inverse[j]
    forward = []
    for i in range(ITERS):
        forward.append((beta * hmat[0, i] - sum(factor[i, m] * forward[m] for m in range(i))) * inverse[i])
    coef = [None] * ITERS
    for i in reversed(range(ITERS)):
        coef[i] = (forward[i] - sum(factor[m, i] * coef[m] for m in range(i + 1, ITERS))) * inverse[i]
    mix = [sum(coef[s] * basis[s][m] for s in range(m, ITERS))[:, :width] for m in range(ITERS)]
    sol_ref[...] = sum(mix[m] * zs[m][...] for m in range(ITERS))
    image = sum(mix[m] * (us[m + 1][...] + SHIFT * us[m][...]) for m in range(ITERS))
    res_ref[...] = us[0][...] - image
    ok = ok & (functools.reduce(jnp.maximum, [jnp.abs(c) for c in coef]) < 1e30)
    ok_ref[...] = jnp.where(ok, 1.0, 0.0)


def call(kernel, args, outs, spaces=None, scratch=(), flops=0, pinned=True, ready=True, kind=F32):
    spaces = [pltpu.VMEM] * len(args) if spaces is None else spaces
    if ready:
        args = [pltpu.with_memory_space_constraint(x, s) if s is pltpu.VMEM else x for x, s in zip(args, spaces)]
    size = sum(x.dtype.itemsize * math.prod(x.shape) for x in args)
    return pl.pallas_call(
        kernel,
        out_shape=[pltpu.VMEM(shape, kind) if pinned else jax.ShapeDtypeStruct(shape, kind) for shape in outs],
        in_specs=[pl.BlockSpec(memory_space=s) for s in spaces],
        out_specs=[pl.BlockSpec(memory_space=pltpu.VMEM) for _ in outs],
        scratch_shapes=scratch,
        compiler_params=pltpu.CompilerParams(vmem_limit_bytes=VMEM_LIMIT),
        cost_estimate=pl.CostEstimate(flops=flops, bytes_accessed=size, transcendentals=0),
    )(*args)


def add_up(x):
    count = lax.axis_size("span") * lax.axis_size("plane")
    rows = jnp.broadcast_to(x, (count, x.shape[1]))
    return lax.all_to_all(rows, ("span", "plane"), split_axis=0, concat_axis=0, tiled=True)


def pairings(size):
    if size % 2:
        return [(i, (i + 1) % size) for i in range(size)], [(i, (i - 1) % size) for i in range(size)]
    return [(i, i ^ 1) for i in range(size)], [(i, (i + 1 if i % 2 else i - 1) % size) for i in range(size)]


def on_device(rhs, blocks, columns, line_slot, line_lower, line_upper, pivot_inv):
    width, nfaces = rhs.shape
    nblocks = columns.shape[0]
    nspan, nplane = lax.axis_size("span"), lax.axis_size("plane")
    owned = nfaces // P_SIZE // nplane
    length = P_SIZE * nplane
    per = owned * P_SIZE
    area = width * width
    shape = (nfaces, width)
    span_pairs, span_others = pairings(nspan)
    plane_pairs, plane_others = pairings(nplane)

    u_first, choose, *send = call(
        functools.partial(start_kernel, nplane),
        [line_slot, rhs.T],
        [shape, (nfaces, 3 * nfaces)] + [(per, width)] * nplane,
        [pltpu.SMEM, pltpu.VMEM],
        ready=False,
    )
    us = [u_first]
    zs = []
    picks = None
    for step in range(ITERS):
        factors = call(
            functools.partial(square_kernel, length),
            [line_lower, line_upper, pivot_inv, us[-1]],
            [(nfaces * width, width)] * 3,
            [pl.ANY] * 4,
            [pltpu.VMEM((nfaces, area), F32)] * 3 + [pltpu.SemaphoreType.DMA((3,))],
            flops=nfaces * area,
        )
        factors = [x.reshape(nfaces, width, width) for x in factors]
        got = [exchange(send[k], "plane", k) if k else send[0] for k in far_first(nplane)]
        solved = call(
            functools.partial(line_kernel, nplane, owned),
            [*got, *factors],
            [(per, width)] * nplane,
            scratch=[pltpu.VMEM((owned, length, width), F32)] * 2,
            flops=6 * nfaces * area,
        )
        if step == 0:
            picks = call(
                functools.partial(pick_kernel, nspan, nplane),
                [lax.optimization_barrier((columns, solved[0]))[0]],
                [(3 * nfaces, 6 * nfaces), ((nblocks - 3) * nfaces, 10 * nfaces)],
                ready=False,
                kind=BF16,
            )
        pieces = [exchange(solved[k], "plane", k) if k else solved[0] for k in far_first(nplane)]
        args = [choose, *pieces, *(picks if step == 0 else ())]
        spaces = [pltpu.VMEM] * (nplane + 1) + [pl.ANY] * (len(args) - nplane - 1)
        (mine,) = call(functools.partial(faces_kernel, nplane), args, [shape], spaces)
        zs.append(mine)
        other = lax.ppermute(mine, "span", span_others)
        near = [mine, lax.ppermute(mine, "span", span_pairs), lax.ppermute(mine, "plane", plane_pairs)]
        far = [other, lax.ppermute(mine, "plane", plane_others)]
        chunk = math.lcm(width, 128)

        def scratch(count):
            return [
                pltpu.VMEM((count * nfaces, chunk), F32),
                pltpu.VMEM((nfaces, area), F32),
                pltpu.VMEM((2 * nfaces * area // chunk, chunk), BF16),
            ]

        early_sum, held = call(
            functools.partial(early_kernel, nblocks),
            [blocks, picks[0], *near],
            [shape, (nfaces, (nblocks - 3) * area)],
            [pl.ANY] + [pltpu.VMEM] * 4,
            [pltpu.VMEM((nfaces, 3 * area), F32)] + scratch(3) + [pltpu.SemaphoreType.DMA((6,))],
            flops=6 * nfaces * area,
        )
        last = step == ITERS - 1
        args = [line_slot, held, picks[1], early_sum, *near, *far, *(us if last else us[-1:])]
        out = call(
            functools.partial(late_kernel, nplane, last),
            args,
            [shape] + ([(1, 128)] if last else [(per, width)] * nplane),
            [pl.ANY] + [pltpu.VMEM] * (len(args) - 1),
            scratch(nblocks - 3) + [pltpu.SMEM(line_slot.shape, jnp.int32), pltpu.SemaphoreType.DMA],
            flops=2 * nblocks * nfaces * area,
        )
        us.append(out[0])
        send = out[1:]
    gram = add_up(send[0])
    sol, res, ok = call(finish_kernel, [gram, *us, *zs], [shape, shape, (1, 128)], pinned=False)
    given = (rhs, blocks, columns, line_slot, line_lower, line_upper, pivot_inv)
    _, sol, res = lax.while_loop(
        lambda state: state[0], lambda _: (jnp.array(False), *step_by_step(*given)), (ok[0, 0] < 0.5, sol.T, res.T)
    )
    return sol, res


def solution(mesh):
    both = ("span", "plane")
    return jax.shard_map(
        on_device,
        mesh=mesh,
        in_specs=(
            P(None, both),
            P(both, None),
            P(None, both),
            P(both, None),
            P(both, None),
            P(both, None),
            P(both, None),
        ),
        out_specs=(P(None, both), P(None, both)),
        check_vma=False,
    )
```

```python
import functools
import math

import jax
import jax.numpy as jnp
import numpy as np
from jax import lax
from jax.experimental import pallas as pl
from jax.experimental.pallas import tpu as pltpu
from jax.sharding import PartitionSpec as P

ITERS = 3
P_SIZE = 2
SHIFT = 2.0
EPS = 1e-6
VMEM_LIMIT = 16 * 1024 * 1024
HIGH = lax.Precision.HIGHEST
F32, BF16 = jnp.float32, jnp.bfloat16


def with_halo(x, sides, width, wrap):
    for axis, dim in sides:
        size, length = (lax.axis_size(axis), x.shape[dim])
        up = [(i, (i + 1) % size) for i in range(size if wrap else size - 1)]
        down = [(j, i) for i, j in up]
        last = lax.slice_in_dim(x, length - width, length, axis=dim)
        first = lax.slice_in_dim(x, 0, width, axis=dim)
        before = lax.ppermute(last, axis, up)
        after = lax.ppermute(first, axis, down)
        x = jnp.concatenate([before, x, after], axis=dim)
    return x


def small_solve(factor, target):
    extent = target.shape[0]
    forward_vals = []
    for row in range(extent):
        running = target[row]
        for inner in range(row):
            running = running - factor[row, inner] * forward_vals[inner]
        forward_vals.append(running / factor[row, row])
    backward_vals = [None] * extent
    for row in reversed(range(extent)):
        running = forward_vals[row]
        for inner in range(row + 1, extent):
            running = running - factor[inner, row] * backward_vals[inner]
        backward_vals[row] = running / factor[row, row]
    return jnp.stack(backward_vals)


def to_sequence(factor_rows, nlines, length, width):
    return jnp.swapaxes(factor_rows.reshape(nlines, length, width, width), 0, 1)


def line_solve(rhs_lines, lseq, useq, pseq):
    rseq = jnp.moveaxis(rhs_lines, 2, 0)

    def forward(prev, items):
        right, low = items
        cur = right - jnp.einsum("mab,bm->am", low, prev, precision=HIGH)
        return (cur, cur)

    start = jnp.zeros(rseq.shape[1:], F32)
    _, yseq = lax.scan(forward, start, (rseq, lseq))

    def backward(nxt, items):
        yval, upp, piv = items
        inner = yval - jnp.einsum("mab,bm->am", upp, nxt, precision=HIGH)
        cur = jnp.einsum("mab,bm->am", piv, inner, precision=HIGH)
        return (cur, cur)

    _, zseq = lax.scan(backward, start, (yseq, useq, pseq), reverse=True)
    return jnp.moveaxis(zseq, 0, 2)


def table_positions(columns, nfaces, my_span, my_plane, nspan, nplane):
    device_of = columns // nfaces
    span_of = device_of // nplane
    plane_of = device_of % nplane
    dspan = (span_of - my_span + 1 + nspan) % nspan - 1
    dplane = plane_of - my_plane
    selector = jnp.where(
        dspan == -1,
        1,
        jnp.where(dspan == 1, 2, jnp.where(dplane == -1, 3, jnp.where(dplane == 1, 4, 0))),
    )
    return selector * nfaces + columns % nfaces


def step_by_step(rhs, blocks, columns, line_slot, line_lower, line_upper, pivot_inv):
    width, nfaces = rhs.shape
    nblocks = columns.shape[0]
    nplane = lax.axis_size("plane")
    position = table_positions(
        columns, nfaces, lax.axis_index("span"), lax.axis_index("plane"), lax.axis_size("span"), nplane
    )
    slot = line_slot[0]
    lines_group = nfaces // P_SIZE
    owned = lines_group // nplane
    length = P_SIZE * nplane
    lower = to_sequence(line_lower, owned, length, width)
    upper = to_sequence(line_upper, owned, length, width)
    pivot = to_sequence(pivot_inv, owned, length, width)
    shaped_blocks = blocks.reshape(nfaces, nblocks, width, width)

    def apply_a(vec):
        shaped = vec.reshape(width, 1, 1, nfaces)
        span_side = with_halo(shaped, (("span", 1),), 1, True)
        plane_side = with_halo(shaped, (("plane", 2),), 1, False)
        below = plane_side[:, 0, 0]
        above = plane_side[:, 0, 2]
        table = jnp.concatenate([vec, span_side[:, 0, 0], span_side[:, 2, 0], below, above], axis=1)
        return jnp.einsum("ikab,bki->ai", shaped_blocks, table[:, position], precision=HIGH)

    def apply_m(vec):
        pieces = vec[:, slot].reshape(width, lines_group, P_SIZE)
        whole = lax.all_to_all(pieces, "plane", split_axis=1, concat_axis=2, tiled=True)
        solved = line_solve(whole, lower, upper, pivot)
        back = lax.all_to_all(solved, "plane", split_axis=2, concat_axis=1, tiled=True)
        return jnp.zeros_like(vec).at[:, slot].set(back.reshape(width, nfaces))

    beta = jnp.sqrt(lax.psum(jnp.sum(rhs * rhs), ("span", "plane")) + EPS)
    basis = [rhs / beta]
    hcols = []
    for step in range(ITERS):
        wvec = apply_a(apply_m(basis[step]))
        stacked = jnp.stack(basis)
        hvals = lax.psum(jnp.einsum("jai,ai->j", stacked, wvec, precision=HIGH), ("span", "plane"))
        wvec = wvec - jnp.einsum("j,jai->ai", hvals, stacked, precision=HIGH)
        hnext = jnp.sqrt(lax.psum(jnp.sum(wvec * wvec), ("span", "plane")) + EPS)
        basis.append(wvec / hnext)
        hcols.append(jnp.concatenate([hvals, hnext[None], jnp.zeros((ITERS - step - 1,), F32)]))
    hmat = jnp.stack(hcols, axis=1)
    factor = jnp.linalg.cholesky(jnp.dot(hmat.T, hmat, precision=HIGH))
    coef = small_solve(factor, beta * hmat[0])
    update = jnp.einsum("j,jai->ai", coef, jnp.stack(basis[:ITERS]), precision=HIGH)
    solution = apply_m(update)
    return solution, rhs - apply_a(solution)


def partner(me, k, size):
    if size & (size - 1) == 0:
        return me ^ k, me ^ k
    return (me + k) % size, (me + size - k) % size


def far_first(size):
    return list(reversed(range(size)))


def exchange(x, axis, k):
    size = lax.axis_size(axis)
    return lax.ppermute(x, axis, [(i, partner(i, k, size)[0]) for i in range(size)])


def split(x, parts):
    out = []
    for _ in range(parts):
        out.append(x.astype(BF16).astype(F32))
        x = x - out[-1]
    return jnp.concatenate(out, axis=0)


def start_kernel(nplane, slot_ref, u_ref, copy_ref, choose_ref, *outs):
    nfaces = u_ref.shape[0]
    per = nfaces // nplane
    me = lax.axis_index("plane")
    for k in range(nplane):
        to, _ = partner(me, k, nplane)
        for i in range(per):
            outs[k][pl.ds(i, 1), :] = u_ref[pl.ds(slot_ref[0, to * per + i], 1), :]
    copy_ref[...] = u_ref[...]
    face = lax.broadcasted_iota(jnp.int32, choose_ref.shape, 0)
    piece = lax.broadcasted_iota(jnp.int32, choose_ref.shape, 1) % nfaces
    choose = jnp.zeros(choose_ref.shape, F32)
    for n, k in enumerate(far_first(nplane)):
        _, source = partner(me, k, nplane)
        for i in range(per):
            hit = (face == slot_ref[0, source * per + i]) & (piece == n * per + i)
            choose = jnp.where(hit, 1.0, choose)
    choose_ref[...] = choose


def to_squares(src, dst):
    nrows, width = src.shape[0], dst.shape[1]
    chunk = math.lcm(width, 128)
    for c in range(width * width // chunk):
        piece = src[:, c * chunk : (c + 1) * chunk]
        for r in range(chunk // width):
            a = c * (chunk // width) + r
            dst[pl.ds(a, nrows, stride=width), :] = piece[:, r * width : (r + 1) * width]


def turn_some(squares, length, parity):
    width = squares.shape[1]
    for at in range(squares.shape[0] // width):
        if at % length % 2 == parity and at % length:
            here = slice(at * width, (at + 1) * width)
            squares[here, :] = squares[here, :].T


def first_squares_kernel(length, low, piv, upp, _, low_out, piv_out, fold_out, low_scr, piv_scr, upp_scr, upp_sq, sems):
    width = low_out.shape[1]
    fetches = []
    for n, (src, scr) in enumerate(((low, low_scr), (piv, piv_scr), (upp, upp_scr))):
        fetches.append(pltpu.make_async_copy(src, scr, sems.at[n]))
        fetches[-1].start()
    for fetch, scr, dst in zip(fetches, (low_scr, piv_scr, upp_scr), (low_out, piv_out, upp_sq)):
        fetch.wait()
        to_squares(scr, dst)
    for at in range(low.shape[0]):
        here = slice(at * width, (at + 1) * width)
        if at % length == length - 1:
            fold_out[here, :] = jnp.zeros((width, width), F32)
            continue
        (ph, pl_), (uh, ul) = [
            (x.astype(BF16), (x - x.astype(BF16).astype(F32)).astype(BF16)) for x in (piv_out[here, :], upp_sq[here, :])
        ]
        fold = sum(jnp.dot(x, y, preferred_element_type=F32) for x, y in ((pl_, uh), (ph, ul), (ph, uh)))
        fold_out[here, :] = fold.T if at % length % 2 else fold
    turn_some(low_out, length, 0)
    turn_some(piv_out, length, 1)


def next_squares_kernel(length, low, piv, fold, _, low_out, piv_out, fold_out, low_scr, piv_scr, sems):
    fetches = []
    for n, (src, scr) in enumerate(((low, low_scr), (piv, piv_scr), (fold, fold_out))):
        fetches.append(pltpu.make_async_copy(src, scr, sems.at[n]))
        fetches[-1].start()
    for fetch, scr, dst, parity in zip(fetches, (low_scr, piv_scr), (low_out, piv_out), (0, 1)):
        fetch.wait()
        to_squares(scr, dst)
        turn_some(dst, length, parity)
    fetches[2].wait()


def store_kernel(x, _, out, sem):
    copy = pltpu.make_async_copy(x, out, sem)
    copy.start()
    copy.wait()


def parities():
    return [1 if lax.axis_size(a) % 2 else lax.axis_index(a) % 2 for a in ("span", "plane")]


def early_blocks():
    span_odd, plane_odd = parities()
    return (1 + span_odd, 3 + plane_odd), (2 - span_odd, 4 - plane_odd)


def pick_kernel(nspan, nplane, columns_ref, early_ref, late_ref):
    nblocks, nfaces = columns_ref.shape
    span, plane = lax.axis_index("span"), lax.axis_index("plane")
    position = table_positions(columns_ref[...], nfaces, span, plane, nspan, nplane)
    selector, face = position // nfaces, position % nfaces
    span_odd, plane_odd = [parity == 1 for parity in parities()]
    of_span = jnp.where((selector == 1) == span_odd, 1, 3)
    of_plane = jnp.where((selector == 3) == plane_odd, 2, 4)
    group = jnp.where(selector == 0, 0, jnp.where(selector <= 2, of_span, of_plane))
    at = (group * nfaces + face).astype(F32)
    eye = lax.broadcasted_iota(jnp.int32, (nfaces, nfaces), 0) == lax.broadcasted_iota(jnp.int32, (nfaces, nfaces), 1)
    first, second = jnp.where(span_odd, at[2:3], at[1:2]), jnp.where(span_odd, at[1:2], at[2:3])
    third, fourth = jnp.where(plane_odd, at[4:5], at[3:4]), jnp.where(plane_odd, at[3:4], at[4:5])
    rest = [at[k : k + 1] for k in range(5, nblocks)]
    for ref, rows in ((early_ref, [at[0:1], first, third]), (late_ref, [second, fourth, *rest])):
        lane = lax.broadcasted_iota(jnp.int32, (nfaces, ref.shape[1]), 1) % (ref.shape[1] // 2)
        for n, row in enumerate(rows):
            column = jnp.sum(jnp.where(eye, row, 0.0), axis=1, keepdims=True).astype(jnp.int32)
            ref[n * nfaces : (n + 1) * nfaces, :] = jnp.where(lane == column, 1.0, 0.0).astype(BF16)


def line_kernel(nplane, nlines, *refs):
    msgs, (low, piv, fold), outs, (r_scr, z_scr) = refs[:nplane], refs[nplane:-nplane-2], refs[-nplane-2:-2], refs[-2:]
    _, length, width = r_scr.shape
    me = lax.axis_index("plane")
    for k, msg in zip(far_first(nplane), msgs):
        _, source = partner(me, k, nplane)
        for m in range(nlines):
            for q in range(P_SIZE):
                r_scr[m, pl.ds(source * P_SIZE + q, 1), :] = msg[pl.ds(m * P_SIZE + q, 1), :]
    eye = lax.broadcasted_iota(jnp.int32, (width, width), 0) == lax.broadcasted_iota(jnp.int32, (width, width), 1)

    def column(row):
        return jnp.sum(jnp.where(eye, row, 0.0), axis=1, keepdims=True)

    rows = [[r_scr[m, pl.ds(j, 1), :] for m in range(nlines)] for j in range(length)]
    scaled = [[None] * nlines for _ in range(length)]
    carry = [None] * nlines
    for j in range(length):
        for m in range(nlines):
            at = m * length + j
            if j == 0:
                carry[m] = rows[j][m]
            elif j % 2:
                carry[m] = column(rows[j][m]) - jnp.sum(low[at] * carry[m], axis=1, keepdims=True)
            else:
                carry[m] = rows[j][m] - jnp.sum(low[at] * carry[m], axis=0, keepdims=True)
            scaled[j][m] = jnp.sum(piv[at] * carry[m], axis=0 if j % 2 else 1, keepdims=True)
    after = [None] * nlines
    for j in reversed(range(length)):
        for m in range(nlines):
            at = m * length + j
            value = scaled[j][m]
            if j < length - 1:
                value = value - jnp.sum(fold[at] * after[m], axis=0 if j % 2 else 1, keepdims=True)
            after[m] = value
            row = value if j % 2 else jnp.sum(jnp.where(eye, value, 0.0), axis=0, keepdims=True)
            z_scr[m, pl.ds(j, 1), :] = row
    for k in range(nplane):
        to, _ = partner(me, k, nplane)
        for m in range(nlines):
            for q in range(P_SIZE):
                outs[k][pl.ds(m * P_SIZE + q, 1), :] = z_scr[m, pl.ds(to * P_SIZE + q, 1), :]


def faces_kernel(nplane, choose, *refs):
    solved, mine_ref = refs[:nplane], refs[-1]
    table = split(jnp.concatenate([s[...] for s in solved], axis=0), 3).astype(BF16)
    mine_ref[...] = jnp.dot(choose[...].astype(BF16), table, preferred_element_type=F32)


def repeat_faces(faces, pick, copies):
    both = split(jnp.concatenate([f[...] for f in faces], axis=0), 2).astype(BF16)
    picked = jnp.dot(pick[...], both, preferred_element_type=F32)
    return jnp.concatenate([picked] * copies, axis=1)


def add_products(work, x_scr, acc_scr, parts, width):
    nfaces, area = acc_scr.shape
    chunk = x_scr.shape[1]
    copies, count = chunk // width, area // chunk
    lane = lax.broadcasted_iota(jnp.int32, (1, 128), 1)
    seg = [jnp.broadcast_to(jnp.where(lane % copies == r, 1.0, 0.0), (width, 128)) for r in range(copies)]
    seg = jnp.concatenate(seg, axis=0).astype(BF16)
    total = jnp.zeros((nfaces, 128), F32)
    done = 0
    for n, (places, fetch) in enumerate(work):
        if fetch is not None:
            fetch.wait()
        last = n == len(work) - 1
        for half in ((0, count // 2), (count // 2, count)):
            for v in range(0, chunk, 128):
                rows = range(done * nfaces, (done + len(places)) * nfaces, nfaces)
                xs = [x_scr[row : row + nfaces, v : v + 128] for row in rows]
                for c in range(*half):
                    at = c * chunk + v
                    value = acc_scr[:, at : at + 128] if n else None
                    for (ref, column), x in zip(places, xs):
                        term = ref[:, column + at : column + at + 128] * x
                        value = term if value is None else value + term
                    if not last:
                        acc_scr[:, at : at + 128] = value
                        continue
                    high = value.astype(BF16)
                    row = 2 * c * nfaces
                    parts[row : row + nfaces, v : v + 128] = high
                    parts[row + nfaces : row + 2 * nfaces, v : v + 128] = (value - high.astype(F32)).astype(BF16)
            if last:
                base = 2 * half[0] * nfaces
                sums = jnp.dot(parts[base : 2 * half[1] * nfaces, :], seg, preferred_element_type=F32)
                for c in range(*half):
                    at = 2 * c * nfaces - base
                    pair = sums[at : at + nfaces] + sums[at + nfaces : at + 2 * nfaces]
                    total = total + jnp.where(lane // copies == c, pair, 0.0)
        done += len(places)
    return total[:, :width]


def early_kernel(nblocks, blocks, pick, *refs):
    faces, (sum_ref, held, buf, x_scr, acc_scr, parts, sems) = refs[:3], refs[3:]
    width = faces[0].shape[1]
    area = width * width
    early, late = early_blocks()

    def fetch(k, count, dst, column, n):
        start = pl.multiple_of(k * area, 128) if not isinstance(k, int) else k * area
        return pltpu.make_async_copy(
            blocks.at[:, pl.ds(start, count * area)], dst.at[:, pl.ds(column, count * area)], sems.at[n]
        )

    mine = [fetch(k, 1, buf, n * area, n) for n, k in enumerate((0, *early))]
    kept = [fetch(k, 1, held, n * area, 3 + n) for n, k in enumerate(late)]
    kept.append(fetch(5, nblocks - 5, held, 2 * area, 5))
    for copy in mine + kept:
        copy.start()
    x_scr[...] = repeat_faces(faces, pick, x_scr.shape[1] // width)
    work = [([(buf, n * area)], copy) for n, copy in enumerate(mine)]
    sum_ref[...] = add_products(work, x_scr, acc_scr, parts, width)
    for copy in kept:
        copy.wait()


def late_kernel(nplane, last, *refs):
    (slot, held, pick, early_sum), faces, refs = refs[:4], refs[4:9], refs[9:]
    nold = ITERS if last else 1
    olds, refs = refs[:nold], refs[nold:]
    next_ref, outs, (x_scr, acc_scr, parts, slot_scr, slot_sem) = refs[0], refs[1:-5], refs[-5:]
    nfaces, width = faces[0].shape
    area = width * width
    if not last:
        slots = pltpu.make_async_copy(slot, slot_scr, slot_sem)
        slots.start()
    x_scr[...] = repeat_faces(faces, pick, x_scr.shape[1] // width)
    work = [([(held, column) for column in range(0, held.shape[1], area)], None)]
    u_next = early_sum[...] + add_products(work, x_scr, acc_scr, parts, width) - SHIFT * olds[-1][...]
    next_ref[...] = u_next
    if last:
        gram_ref = outs[0]
        lane = lax.broadcasted_iota(jnp.int32, gram_ref.shape, 1)
        basis = [old[...] for old in olds] + [u_next]
        gram, at = jnp.zeros(gram_ref.shape, F32), 0
        for i in range(ITERS + 1):
            for j in range(i, ITERS + 1):
                value = jnp.sum(jnp.sum(basis[i] * basis[j], axis=0, keepdims=True), axis=1, keepdims=True)
                gram, at = jnp.where(lane == at, value, gram), at + 1
        gram_ref[...] = gram
    else:
        per = nfaces // nplane
        me = lax.axis_index("plane")
        slots.wait()
        for k in range(nplane):
            to, _ = partner(me, k, nplane)
            for i in range(per):
                outs[k][pl.ds(i, 1), :] = next_ref[pl.ds(slot_scr[0, to * per + i], 1), :]


def finish_kernel(gram_ref, *refs):
    us, zs = refs[: ITERS + 1], refs[ITERS + 1 : 2 * ITERS + 1]
    sol_ref, res_ref, ok_ref = refs[2 * ITERS + 1 :]
    width = sol_ref.shape[1]
    rows = jnp.sum(gram_ref[...], axis=0, keepdims=True)
    lane = lax.broadcasted_iota(jnp.int32, rows.shape, 1)
    gram, at = {}, 0
    for i in range(ITERS + 1):
        for j in range(i, ITERS + 1):
            value = jnp.sum(jnp.where(lane == at, rows, 0.0), axis=1, keepdims=True)
            gram[i, j] = gram[j, i] = jnp.broadcast_to(value, rows.shape)
            at += 1
    largest = functools.reduce(jnp.maximum, [jnp.abs(g) for g in gram.values()])
    ok = largest < 1e30
    beta = jnp.sqrt(gram[0, 0] + EPS)
    basis = [[1.0 / beta]]
    hmat = {}
    for step in range(ITERS):
        own = basis[step]
        wvec = [SHIFT * own[0]] + [own[i] + SHIFT * own[i + 1] for i in range(step)] + [own[step]]
        images = [sum(gram[i, j] * wvec[j] for j in range(step + 2)) for i in range(step + 1)]
        for i in range(step + 1):
            hmat[i, step] = sum(basis[i][m] * images[m] for m in range(i + 1))
        for i in range(step + 1):
            for m in range(i + 1):
                wvec[m] = wvec[m] - hmat[i, step] * basis[i][m]
        terms = [wvec[i] * wvec[j] * gram[i, j] for i in range(step + 2) for j in range(step + 2)]
        square = jnp.maximum(sum(terms), 0.0)
        ok = ok & (square + EPS >= 2e-3 * sum(jnp.abs(term) for term in terms))
        hmat[step + 1, step] = jnp.sqrt(square + EPS)
        scale = 1.0 / hmat[step + 1, step]
        basis.append([w * scale for w in wvec])
    normal = {
        (i, j): sum(hmat[m, i] * hmat[m, j] for m in range(j + 2) if (m, i) in hmat and (m, j) in hmat)
        for i in range(ITERS)
        for j in range(i + 1)
    }
    factor, inverse = {}, []
    for j in range(ITERS):
        diag = jnp.sqrt(normal[j, j] - sum(factor[j, m] * factor[j, m] for m in range(j)))
        inverse.append(1.0 / diag)
        for i in range(j + 1, ITERS):
            factor[i, j] = (normal[i, j] - sum(factor[i, m] * factor[j, m] for m in range(j))) * inverse[j]
    forward = []
    for i in range(ITERS):
        forward.append((beta * hmat[0, i] - sum(factor[i, m] * forward[m] for m in range(i))) * inverse[i])
    coef = [None] * ITERS
    for i in reversed(range(ITERS)):
        coef[i] = (forward[i] - sum(factor[m, i] * coef[m] for m in range(i + 1, ITERS))) * inverse[i]
    mix = [sum(coef[s] * basis[s][m] for s in range(m, ITERS))[:, :width] for m in range(ITERS)]
    sol_ref[...] = sum(mix[m] * zs[m][...] for m in range(ITERS))
    image = sum(mix[m] * (us[m + 1][...] + SHIFT * us[m][...]) for m in range(ITERS))
    res_ref[...] = us[0][...] - image
    ok = ok & (functools.reduce(jnp.maximum, [jnp.abs(c) for c in coef]) < 1e30)
    ok_ref[...] = jnp.where(ok, 1.0, 0.0)


def call(kernel, args, outs, spaces=None, scratch=(), flops=0, pinned=True, ready=True, kind=F32):
    spaces = [pltpu.VMEM] * len(args) if spaces is None else spaces
    if ready:
        args = [pltpu.with_memory_space_constraint(x, s) if s is pltpu.VMEM else x for x, s in zip(args, spaces)]
    size = sum(x.dtype.itemsize * math.prod(x.shape) for x in args)
    return pl.pallas_call(
        kernel,
        out_shape=[pltpu.VMEM(shape, kind) if pinned else jax.ShapeDtypeStruct(shape, kind) for shape in outs],
        in_specs=[pl.BlockSpec(memory_space=s) for s in spaces],
        out_specs=[pl.BlockSpec(memory_space=pltpu.VMEM) for _ in outs],
        scratch_shapes=scratch,
        compiler_params=pltpu.CompilerParams(vmem_limit_bytes=VMEM_LIMIT),
        cost_estimate=pl.CostEstimate(flops=flops, bytes_accessed=size, transcendentals=0),
    )(*args)


def add_up(x):
    count = lax.axis_size("span") * lax.axis_size("plane")
    rows = jnp.broadcast_to(x, (count, x.shape[1]))
    return lax.all_to_all(rows, ("span", "plane"), split_axis=0, concat_axis=0, tiled=True)


def pairings(size):
    if size % 2:
        return [(i, (i + 1) % size) for i in range(size)], [(i, (i - 1) % size) for i in range(size)]
    return [(i, i ^ 1) for i in range(size)], [(i, (i + 1 if i % 2 else i - 1) % size) for i in range(size)]


def on_device(rhs, blocks, columns, line_slot, line_lower, line_upper, pivot_inv):
    width, nfaces = rhs.shape
    nblocks = columns.shape[0]
    nspan, nplane = lax.axis_size("span"), lax.axis_size("plane")
    owned = nfaces // P_SIZE // nplane
    length = P_SIZE * nplane
    per = owned * P_SIZE
    area = width * width
    shape = (nfaces, width)
    span_pairs, span_others = pairings(nspan)
    plane_pairs, plane_others = pairings(nplane)

    u_first, choose, *send = call(
        functools.partial(start_kernel, nplane),
        [line_slot, rhs.T],
        [shape, (nfaces, 3 * nfaces)] + [(per, width)] * nplane,
        [pltpu.SMEM, pltpu.VMEM],
        ready=False,
    )
    us = [u_first]
    zs = []
    picks = None
    for step in range(ITERS):
        flat = pltpu.VMEM((nfaces, area), F32)
        squares = [(nfaces * width, width)] * 3
        if step == 0:
            factors = call(
                functools.partial(first_squares_kernel, length),
                [line_lower, pivot_inv, line_upper, us[-1]],
                squares,
                [pl.ANY] * 4,
                [flat] * 3 + [pltpu.VMEM(squares[0], F32), pltpu.SemaphoreType.DMA((3,))],
                flops=nfaces * area * width,
            )
        else:
            factors = call(
                functools.partial(next_squares_kernel, length),
                [line_lower, pivot_inv, fold, us[-1]],
                squares,
                [pl.ANY] * 4,
                [flat] * 2 + [pltpu.SemaphoreType.DMA((3,))],
                flops=nfaces * area,
            )
        shaped = [x.reshape(nfaces, width, width) for x in factors]
        got = [exchange(send[k], "plane", k) if k else send[0] for k in far_first(nplane)]
        solved = call(
            functools.partial(line_kernel, nplane, owned),
            [*got, *shaped],
            [(per, width)] * nplane,
            scratch=[pltpu.VMEM((owned, length, width), F32)] * 2,
            flops=6 * nfaces * area,
        )
        if step == 0:
            fold = pl.pallas_call(
                store_kernel,
                out_shape=pltpu.HBM(squares[0], F32),
                in_specs=[pl.BlockSpec(memory_space=pl.ANY)] * 2,
                out_specs=pl.BlockSpec(memory_space=pl.ANY),
                scratch_shapes=[pltpu.SemaphoreType.DMA],
                cost_estimate=pl.CostEstimate(flops=0, bytes_accessed=4 * nfaces * area, transcendentals=0),
            )(pltpu.with_memory_space_constraint(factors[2], pltpu.VMEM), solved[0])
            picks = call(
                functools.partial(pick_kernel, nspan, nplane),
                [lax.optimization_barrier((columns, solved[0]))[0]],
                [(3 * nfaces, 6 * nfaces), ((nblocks - 3) * nfaces, 10 * nfaces)],
                ready=False,
                kind=BF16,
            )
        pieces = [exchange(solved[k], "plane", k) if k else solved[0] for k in far_first(nplane)]
        args = [choose, *pieces, *((*picks, fold) if step == 0 else ())]
        spaces = [pltpu.VMEM] * (nplane + 1) + [pl.ANY] * (len(args) - nplane - 1)
        (mine,) = call(functools.partial(faces_kernel, nplane), args, [shape], spaces)
        zs.append(mine)
        other = lax.ppermute(mine, "span", span_others)
        near = [mine, lax.ppermute(mine, "span", span_pairs), lax.ppermute(mine, "plane", plane_pairs)]
        far = [other, lax.ppermute(mine, "plane", plane_others)]
        chunk = math.lcm(width, 128)

        def scratch(count):
            return [
                pltpu.VMEM((count * nfaces, chunk), F32),
                pltpu.VMEM((nfaces, area), F32),
                pltpu.VMEM((2 * nfaces * area // chunk, chunk), BF16),
            ]

        early_sum, held = call(
            functools.partial(early_kernel, nblocks),
            [blocks, picks[0], *near],
            [shape, (nfaces, (nblocks - 3) * area)],
            [pl.ANY] + [pltpu.VMEM] * 4,
            [pltpu.VMEM((nfaces, 3 * area), F32)] + scratch(3) + [pltpu.SemaphoreType.DMA((6,))],
            flops=6 * nfaces * area,
        )
        last = step == ITERS - 1
        args = [line_slot, held, picks[1], early_sum, *near, *far, *(us if last else us[-1:])]
        out = call(
            functools.partial(late_kernel, nplane, last),
            args,
            [shape] + ([(1, 128)] if last else [(per, width)] * nplane),
            [pl.ANY] + [pltpu.VMEM] * (len(args) - 1),
            scratch(nblocks - 3) + [pltpu.SMEM(line_slot.shape, jnp.int32), pltpu.SemaphoreType.DMA],
            flops=2 * nblocks * nfaces * area,
        )
        us.append(out[0])
        send = out[1:]
    gram = add_up(send[0])
    sol, res, ok = call(finish_kernel, [gram, *us, *zs], [shape, shape, (1, 128)], pinned=False)
    given = (rhs, blocks, columns, line_slot, line_lower, line_upper, pivot_inv)
    _, sol, res = lax.while_loop(
        lambda state: state[0], lambda _: (jnp.array(False), *step_by_step(*given)), (ok[0, 0] < 0.5, sol.T, res.T)
    )
    return sol, res


def solution(mesh):
    both = ("span", "plane")
    return jax.shard_map(
        on_device,
        mesh=mesh,
        in_specs=(
            P(None, both),
            P(both, None),
            P(None, both),
            P(both, None),
            P(both, None),
            P(both, None),
            P(both, None),
        ),
        out_specs=(P(None, both), P(None, both)),
        check_vma=False,
    )
```

```python
import functools
import math

import jax
import jax.numpy as jnp
import numpy as np
from jax import lax
from jax.experimental import pallas as pl
from jax.experimental.pallas import tpu as pltpu
from jax.sharding import PartitionSpec as P

ITERS = 3
P_SIZE = 2
SHIFT = 2.0
EPS = 1e-6
VMEM_LIMIT = 16 * 1024 * 1024
HIGH = lax.Precision.HIGHEST
F32, BF16 = jnp.float32, jnp.bfloat16


def with_halo(x, sides, width, wrap):
    for axis, dim in sides:
        size, length = (lax.axis_size(axis), x.shape[dim])
        up = [(i, (i + 1) % size) for i in range(size if wrap else size - 1)]
        down = [(j, i) for i, j in up]
        last = lax.slice_in_dim(x, length - width, length, axis=dim)
        first = lax.slice_in_dim(x, 0, width, axis=dim)
        before = lax.ppermute(last, axis, up)
        after = lax.ppermute(first, axis, down)
        x = jnp.concatenate([before, x, after], axis=dim)
    return x


def small_solve(factor, target):
    extent = target.shape[0]
    forward_vals = []
    for row in range(extent):
        running = target[row]
        for inner in range(row):
            running = running - factor[row, inner] * forward_vals[inner]
        forward_vals.append(running / factor[row, row])
    backward_vals = [None] * extent
    for row in reversed(range(extent)):
        running = forward_vals[row]
        for inner in range(row + 1, extent):
            running = running - factor[inner, row] * backward_vals[inner]
        backward_vals[row] = running / factor[row, row]
    return jnp.stack(backward_vals)


def to_sequence(factor_rows, nlines, length, width):
    return jnp.swapaxes(factor_rows.reshape(nlines, length, width, width), 0, 1)


def line_solve(rhs_lines, lseq, useq, pseq):
    rseq = jnp.moveaxis(rhs_lines, 2, 0)

    def forward(prev, items):
        right, low = items
        cur = right - jnp.einsum("mab,bm->am", low, prev, precision=HIGH)
        return (cur, cur)

    start = jnp.zeros(rseq.shape[1:], F32)
    _, yseq = lax.scan(forward, start, (rseq, lseq))

    def backward(nxt, items):
        yval, upp, piv = items
        inner = yval - jnp.einsum("mab,bm->am", upp, nxt, precision=HIGH)
        cur = jnp.einsum("mab,bm->am", piv, inner, precision=HIGH)
        return (cur, cur)

    _, zseq = lax.scan(backward, start, (yseq, useq, pseq), reverse=True)
    return jnp.moveaxis(zseq, 0, 2)


def table_positions(columns, nfaces, my_span, my_plane, nspan, nplane):
    device_of = columns // nfaces
    span_of = device_of // nplane
    plane_of = device_of % nplane
    dspan = (span_of - my_span + 1 + nspan) % nspan - 1
    dplane = plane_of - my_plane
    selector = jnp.where(
        dspan == -1,
        1,
        jnp.where(dspan == 1, 2, jnp.where(dplane == -1, 3, jnp.where(dplane == 1, 4, 0))),
    )
    return selector * nfaces + columns % nfaces


def step_by_step(rhs, blocks, columns, line_slot, line_lower, line_upper, pivot_inv):
    width, nfaces = rhs.shape
    nblocks = columns.shape[0]
    nplane = lax.axis_size("plane")
    position = table_positions(
        columns, nfaces, lax.axis_index("span"), lax.axis_index("plane"), lax.axis_size("span"), nplane
    )
    slot = line_slot[0]
    lines_group = nfaces // P_SIZE
    owned = lines_group // nplane
    length = P_SIZE * nplane
    lower = to_sequence(line_lower, owned, length, width)
    upper = to_sequence(line_upper, owned, length, width)
    pivot = to_sequence(pivot_inv, owned, length, width)
    shaped_blocks = blocks.reshape(nfaces, nblocks, width, width)

    def apply_a(vec):
        shaped = vec.reshape(width, 1, 1, nfaces)
        span_side = with_halo(shaped, (("span", 1),), 1, True)
        plane_side = with_halo(shaped, (("plane", 2),), 1, False)
        below = plane_side[:, 0, 0]
        above = plane_side[:, 0, 2]
        table = jnp.concatenate([vec, span_side[:, 0, 0], span_side[:, 2, 0], below, above], axis=1)
        return jnp.einsum("ikab,bki->ai", shaped_blocks, table[:, position], precision=HIGH)

    def apply_m(vec):
        pieces = vec[:, slot].reshape(width, lines_group, P_SIZE)
        whole = lax.all_to_all(pieces, "plane", split_axis=1, concat_axis=2, tiled=True)
        solved = line_solve(whole, lower, upper, pivot)
        back = lax.all_to_all(solved, "plane", split_axis=2, concat_axis=1, tiled=True)
        return jnp.zeros_like(vec).at[:, slot].set(back.reshape(width, nfaces))

    beta = jnp.sqrt(lax.psum(jnp.sum(rhs * rhs), ("span", "plane")) + EPS)
    basis = [rhs / beta]
    hcols = []
    for step in range(ITERS):
        wvec = apply_a(apply_m(basis[step]))
        stacked = jnp.stack(basis)
        hvals = lax.psum(jnp.einsum("jai,ai->j", stacked, wvec, precision=HIGH), ("span", "plane"))
        wvec = wvec - jnp.einsum("j,jai->ai", hvals, stacked, precision=HIGH)
        hnext = jnp.sqrt(lax.psum(jnp.sum(wvec * wvec), ("span", "plane")) + EPS)
        basis.append(wvec / hnext)
        hcols.append(jnp.concatenate([hvals, hnext[None], jnp.zeros((ITERS - step - 1,), F32)]))
    hmat = jnp.stack(hcols, axis=1)
    factor = jnp.linalg.cholesky(jnp.dot(hmat.T, hmat, precision=HIGH))
    coef = small_solve(factor, beta * hmat[0])
    update = jnp.einsum("j,jai->ai", coef, jnp.stack(basis[:ITERS]), precision=HIGH)
    solution = apply_m(update)
    return solution, rhs - apply_a(solution)


def partner(me, k, size):
    if size & (size - 1) == 0:
        return me ^ k, me ^ k
    return (me + k) % size, (me + size - k) % size


def far_first(size):
    return list(reversed(range(size)))


def exchange(x, axis, k):
    size = lax.axis_size(axis)
    return lax.ppermute(x, axis, [(i, partner(i, k, size)[0]) for i in range(size)])


def split(x, parts):
    out = []
    for _ in range(parts):
        out.append(x.astype(BF16).astype(F32))
        x = x - out[-1]
    return jnp.concatenate(out, axis=0)


def start_kernel(nplane, slot_ref, u_ref, copy_ref, choose_ref, *outs):
    nfaces = u_ref.shape[0]
    per = nfaces // nplane
    me = lax.axis_index("plane")
    for k in range(nplane):
        to, _ = partner(me, k, nplane)
        for i in range(per):
            outs[k][pl.ds(i, 1), :] = u_ref[pl.ds(slot_ref[0, to * per + i], 1), :]
    copy_ref[...] = u_ref[...]
    face = lax.broadcasted_iota(jnp.int32, choose_ref.shape, 0)
    piece = lax.broadcasted_iota(jnp.int32, choose_ref.shape, 1) % nfaces
    choose = jnp.zeros(choose_ref.shape, F32)
    for n, k in enumerate(far_first(nplane)):
        _, source = partner(me, k, nplane)
        for i in range(per):
            hit = (face == slot_ref[0, source * per + i]) & (piece == n * per + i)
            choose = jnp.where(hit, 1.0, choose)
    choose_ref[...] = choose


def to_squares(src, dst):
    nrows, width = src.shape[0], dst.shape[1]
    chunk = math.lcm(width, 128)
    for c in range(width * width // chunk):
        piece = src[:, c * chunk : (c + 1) * chunk]
        for r in range(chunk // width):
            a = c * (chunk // width) + r
            dst[pl.ds(a, nrows, stride=width), :] = piece[:, r * width : (r + 1) * width]


def turn_some(squares, length, parity):
    width = squares.shape[1]
    for at in range(squares.shape[0] // width):
        if at % length % 2 == parity and at % length:
            here = slice(at * width, (at + 1) * width)
            squares[here, :] = squares[here, :].T


def first_squares_kernel(length, low, piv, upp, _, low_out, piv_out, fold_out, low_scr, piv_scr, upp_scr, upp_sq, sems):
    width = low_out.shape[1]
    fetches = []
    for n, (src, scr) in enumerate(((low, low_scr), (piv, piv_scr), (upp, upp_scr))):
        fetches.append(pltpu.make_async_copy(src, scr, sems.at[n]))
        fetches[-1].start()
    for fetch, scr, dst in zip(fetches, (low_scr, piv_scr, upp_scr), (low_out, piv_out, upp_sq)):
        fetch.wait()
        to_squares(scr, dst)
    for at in range(low.shape[0]):
        here = slice(at * width, (at + 1) * width)
        if at % length == length - 1:
            fold_out[here, :] = jnp.zeros((width, width), F32)
            continue
        (ph, pl_), (uh, ul) = [
            (x.astype(BF16), (x - x.astype(BF16).astype(F32)).astype(BF16)) for x in (piv_out[here, :], upp_sq[here, :])
        ]
        fold = sum(jnp.dot(x, y, preferred_element_type=F32) for x, y in ((pl_, uh), (ph, ul), (ph, uh)))
        fold_out[here, :] = fold.T if at % length % 2 else fold
    turn_some(low_out, length, 0)
    turn_some(piv_out, length, 1)


def next_squares_kernel(length, low, piv, fold, _, low_out, piv_out, fold_out, low_scr, piv_scr, sems):
    fetches = []
    for n, (src, scr) in enumerate(((low, low_scr), (piv, piv_scr), (fold, fold_out))):
        fetches.append(pltpu.make_async_copy(src, scr, sems.at[n]))
        fetches[-1].start()
    for fetch, scr, dst, parity in zip(fetches, (low_scr, piv_scr), (low_out, piv_out), (0, 1)):
        fetch.wait()
        to_squares(scr, dst)
        turn_some(dst, length, parity)
    fetches[2].wait()


def parities():
    return [1 if lax.axis_size(a) % 2 else lax.axis_index(a) % 2 for a in ("span", "plane")]


def early_blocks():
    span_odd, plane_odd = parities()
    return (1 + span_odd, 3 + plane_odd), (2 - span_odd, 4 - plane_odd)


def pick_kernel(nspan, nplane, columns_ref, fold_ref, early_ref, late_ref, store_ref, sem):
    store = pltpu.make_async_copy(fold_ref, store_ref, sem)
    store.start()
    nblocks, nfaces = columns_ref.shape
    span, plane = lax.axis_index("span"), lax.axis_index("plane")
    position = table_positions(columns_ref[...], nfaces, span, plane, nspan, nplane)
    selector, face = position // nfaces, position % nfaces
    span_odd, plane_odd = [parity == 1 for parity in parities()]
    of_span = jnp.where((selector == 1) == span_odd, 1, 3)
    of_plane = jnp.where((selector == 3) == plane_odd, 2, 4)
    group = jnp.where(selector == 0, 0, jnp.where(selector <= 2, of_span, of_plane))
    at = (group * nfaces + face).astype(F32)
    eye = lax.broadcasted_iota(jnp.int32, (nfaces, nfaces), 0) == lax.broadcasted_iota(jnp.int32, (nfaces, nfaces), 1)
    first, second = jnp.where(span_odd, at[2:3], at[1:2]), jnp.where(span_odd, at[1:2], at[2:3])
    third, fourth = jnp.where(plane_odd, at[4:5], at[3:4]), jnp.where(plane_odd, at[3:4], at[4:5])
    rest = [at[k : k + 1] for k in range(5, nblocks)]
    for ref, rows in ((early_ref, [at[0:1], first, third]), (late_ref, [second, fourth, *rest])):
        lane = lax.broadcasted_iota(jnp.int32, (nfaces, ref.shape[1]), 1) % (ref.shape[1] // 2)
        for n, row in enumerate(rows):
            column = jnp.sum(jnp.where(eye, row, 0.0), axis=1, keepdims=True).astype(jnp.int32)
            ref[n * nfaces : (n + 1) * nfaces, :] = jnp.where(lane == column, 1.0, 0.0).astype(BF16)
    store.wait()


def line_kernel(nplane, nlines, *refs):
    msgs, (low, piv, fold), outs, (r_scr, z_scr) = refs[:nplane], refs[nplane:-nplane-2], refs[-nplane-2:-2], refs[-2:]
    _, length, width = r_scr.shape
    me = lax.axis_index("plane")
    for k, msg in zip(far_first(nplane), msgs):
        _, source = partner(me, k, nplane)
        for m in range(nlines):
            for q in range(P_SIZE):
                r_scr[m, pl.ds(source * P_SIZE + q, 1), :] = msg[pl.ds(m * P_SIZE + q, 1), :]
    eye = lax.broadcasted_iota(jnp.int32, (width, width), 0) == lax.broadcasted_iota(jnp.int32, (width, width), 1)

    def column(row):
        return jnp.sum(jnp.where(eye, row, 0.0), axis=1, keepdims=True)

    rows = [[r_scr[m, pl.ds(j, 1), :] for m in range(nlines)] for j in range(length)]
    scaled = [[None] * nlines for _ in range(length)]
    carry = [None] * nlines
    for j in range(length):
        for m in range(nlines):
            at = m * length + j
            if j == 0:
                carry[m] = rows[j][m]
            elif j % 2:
                carry[m] = column(rows[j][m]) - jnp.sum(low[at] * carry[m], axis=1, keepdims=True)
            else:
                carry[m] = rows[j][m] - jnp.sum(low[at] * carry[m], axis=0, keepdims=True)
            scaled[j][m] = jnp.sum(piv[at] * carry[m], axis=0 if j % 2 else 1, keepdims=True)
    after = [None] * nlines
    for j in reversed(range(length)):
        for m in range(nlines):
            at = m * length + j
            value = scaled[j][m]
            if j < length - 1:
                value = value - jnp.sum(fold[at] * after[m], axis=0 if j % 2 else 1, keepdims=True)
            after[m] = value
            row = value if j % 2 else jnp.sum(jnp.where(eye, value, 0.0), axis=0, keepdims=True)
            z_scr[m, pl.ds(j, 1), :] = row
    for k in range(nplane):
        to, _ = partner(me, k, nplane)
        for m in range(nlines):
            for q in range(P_SIZE):
                outs[k][pl.ds(m * P_SIZE + q, 1), :] = z_scr[m, pl.ds(to * P_SIZE + q, 1), :]


def faces_kernel(nplane, choose, *refs):
    solved, mine_ref = refs[:nplane], refs[-1]
    table = split(jnp.concatenate([s[...] for s in solved], axis=0), 3).astype(BF16)
    mine_ref[...] = jnp.dot(choose[...].astype(BF16), table, preferred_element_type=F32)


def repeat_faces(faces, pick, copies):
    both = split(jnp.concatenate([f[...] for f in faces], axis=0), 2).astype(BF16)
    picked = jnp.dot(pick[...], both, preferred_element_type=F32)
    return jnp.concatenate([picked] * copies, axis=1)


def add_products(work, x_scr, acc_scr, parts, width):
    nfaces, area = acc_scr.shape
    chunk = x_scr.shape[1]
    copies, count = chunk // width, area // chunk
    lane = lax.broadcasted_iota(jnp.int32, (1, 128), 1)
    seg = [jnp.broadcast_to(jnp.where(lane % copies == r, 1.0, 0.0), (width, 128)) for r in range(copies)]
    seg = jnp.concatenate(seg, axis=0).astype(BF16)
    total = jnp.zeros((nfaces, 128), F32)
    done = 0
    for n, (places, fetch) in enumerate(work):
        if fetch is not None:
            fetch.wait()
        last = n == len(work) - 1
        for half in ((0, count // 2), (count // 2, count)):
            for v in range(0, chunk, 128):
                rows = range(done * nfaces, (done + len(places)) * nfaces, nfaces)
                xs = [x_scr[row : row + nfaces, v : v + 128] for row in rows]
                for c in range(*half):
                    at = c * chunk + v
                    value = acc_scr[:, at : at + 128] if n else None
                    for (ref, column), x in zip(places, xs):
                        term = ref[:, column + at : column + at + 128] * x
                        value = term if value is None else value + term
                    if not last:
                        acc_scr[:, at : at + 128] = value
                        continue
                    high = value.astype(BF16)
                    row = 2 * c * nfaces
                    parts[row : row + nfaces, v : v + 128] = high
                    parts[row + nfaces : row + 2 * nfaces, v : v + 128] = (value - high.astype(F32)).astype(BF16)
            if last:
                base = 2 * half[0] * nfaces
                sums = jnp.dot(parts[base : 2 * half[1] * nfaces, :], seg, preferred_element_type=F32)
                for c in range(*half):
                    at = 2 * c * nfaces - base
                    pair = sums[at : at + nfaces] + sums[at + nfaces : at + 2 * nfaces]
                    total = total + jnp.where(lane // copies == c, pair, 0.0)
        done += len(places)
    return total[:, :width]


def early_kernel(nblocks, blocks, pick, *refs):
    faces, (sum_ref, held, buf, x_scr, acc_scr, parts, sems) = refs[:3], refs[3:]
    width = faces[0].shape[1]
    area = width * width
    early, late = early_blocks()

    def fetch(k, count, dst, column, n):
        start = pl.multiple_of(k * area, 128) if not isinstance(k, int) else k * area
        return pltpu.make_async_copy(
            blocks.at[:, pl.ds(start, count * area)], dst.at[:, pl.ds(column, count * area)], sems.at[n]
        )

    mine = [fetch(k, 1, buf, n * area, n) for n, k in enumerate((0, *early))]
    kept = [fetch(k, 1, held, n * area, 3 + n) for n, k in enumerate(late)]
    kept.append(fetch(5, nblocks - 5, held, 2 * area, 5))
    for copy in mine + kept:
        copy.start()
    x_scr[...] = repeat_faces(faces, pick, x_scr.shape[1] // width)
    work = [([(buf, n * area)], copy) for n, copy in enumerate(mine)]
    sum_ref[...] = add_products(work, x_scr, acc_scr, parts, width)
    for copy in kept:
        copy.wait()


def late_kernel(nplane, last, *refs):
    (slot, held, pick, early_sum), faces, refs = refs[:4], refs[4:9], refs[9:]
    nold = ITERS if last else 1
    olds, refs = refs[:nold], refs[nold:]
    next_ref, outs, (x_scr, acc_scr, parts, slot_scr, slot_sem) = refs[0], refs[1:-5], refs[-5:]
    nfaces, width = faces[0].shape
    area = width * width
    if not last:
        slots = pltpu.make_async_copy(slot, slot_scr, slot_sem)
        slots.start()
    x_scr[...] = repeat_faces(faces, pick, x_scr.shape[1] // width)
    work = [([(held, column) for column in range(0, held.shape[1], area)], None)]
    u_next = early_sum[...] + add_products(work, x_scr, acc_scr, parts, width) - SHIFT * olds[-1][...]
    next_ref[...] = u_next
    if last:
        gram_ref = outs[0]
        lane = lax.broadcasted_iota(jnp.int32, gram_ref.shape, 1)
        basis = [old[...] for old in olds] + [u_next]
        gram, at = jnp.zeros(gram_ref.shape, F32), 0
        for i in range(ITERS + 1):
            for j in range(i, ITERS + 1):
                value = jnp.sum(jnp.sum(basis[i] * basis[j], axis=0, keepdims=True), axis=1, keepdims=True)
                gram, at = jnp.where(lane == at, value, gram), at + 1
        gram_ref[...] = gram
    else:
        per = nfaces // nplane
        me = lax.axis_index("plane")
        slots.wait()
        for k in range(nplane):
            to, _ = partner(me, k, nplane)
            for i in range(per):
                outs[k][pl.ds(i, 1), :] = next_ref[pl.ds(slot_scr[0, to * per + i], 1), :]


def finish_kernel(gram_ref, *refs):
    us, zs = refs[: ITERS + 1], refs[ITERS + 1 : 2 * ITERS + 1]
    sol_ref, res_ref, ok_ref = refs[2 * ITERS + 1 :]
    width = sol_ref.shape[1]
    rows = jnp.sum(gram_ref[...], axis=0, keepdims=True)
    lane = lax.broadcasted_iota(jnp.int32, rows.shape, 1)
    gram, at = {}, 0
    for i in range(ITERS + 1):
        for j in range(i, ITERS + 1):
            value = jnp.sum(jnp.where(lane == at, rows, 0.0), axis=1, keepdims=True)
            gram[i, j] = gram[j, i] = jnp.broadcast_to(value, rows.shape)
            at += 1
    largest = functools.reduce(jnp.maximum, [jnp.abs(g) for g in gram.values()])
    ok = largest < 1e30
    beta = jnp.sqrt(gram[0, 0] + EPS)
    basis = [[1.0 / beta]]
    hmat = {}
    for step in range(ITERS):
        own = basis[step]
        wvec = [SHIFT * own[0]] + [own[i] + SHIFT * own[i + 1] for i in range(step)] + [own[step]]
        images = [sum(gram[i, j] * wvec[j] for j in range(step + 2)) for i in range(step + 1)]
        for i in range(step + 1):
            hmat[i, step] = sum(basis[i][m] * images[m] for m in range(i + 1))
        for i in range(step + 1):
            for m in range(i + 1):
                wvec[m] = wvec[m] - hmat[i, step] * basis[i][m]
        terms = [wvec[i] * wvec[j] * gram[i, j] for i in range(step + 2) for j in range(step + 2)]
        square = jnp.maximum(sum(terms), 0.0)
        ok = ok & (square + EPS >= 2e-3 * sum(jnp.abs(term) for term in terms))
        hmat[step + 1, step] = jnp.sqrt(square + EPS)
        scale = 1.0 / hmat[step + 1, step]
        basis.append([w * scale for w in wvec])
    normal = {
        (i, j): sum(hmat[m, i] * hmat[m, j] for m in range(j + 2) if (m, i) in hmat and (m, j) in hmat)
        for i in range(ITERS)
        for j in range(i + 1)
    }
    factor, inverse = {}, []
    for j in range(ITERS):
        diag = jnp.sqrt(normal[j, j] - sum(factor[j, m] * factor[j, m] for m in range(j)))
        inverse.append(1.0 / diag)
        for i in range(j + 1, ITERS):
            factor[i, j] = (normal[i, j] - sum(factor[i, m] * factor[j, m] for m in range(j))) * inverse[j]
    forward = []
    for i in range(ITERS):
        forward.append((beta * hmat[0, i] - sum(factor[i, m] * forward[m] for m in range(i))) * inverse[i])
    coef = [None] * ITERS
    for i in reversed(range(ITERS)):
        coef[i] = (forward[i] - sum(factor[m, i] * coef[m] for m in range(i + 1, ITERS))) * inverse[i]
    mix = [sum(coef[s] * basis[s][m] for s in range(m, ITERS))[:, :width] for m in range(ITERS)]
    sol_ref[...] = sum(mix[m] * zs[m][...] for m in range(ITERS))
    image = sum(mix[m] * (us[m + 1][...] + SHIFT * us[m][...]) for m in range(ITERS))
    res_ref[...] = us[0][...] - image
    ok = ok & (functools.reduce(jnp.maximum, [jnp.abs(c) for c in coef]) < 1e30)
    ok_ref[...] = jnp.where(ok, 1.0, 0.0)


def call(kernel, args, outs, spaces=None, scratch=(), flops=0, pinned=True, ready=True):
    spaces = [pltpu.VMEM] * len(args) if spaces is None else spaces
    if ready:
        args = [pltpu.with_memory_space_constraint(x, s) if s is pltpu.VMEM else x for x, s in zip(args, spaces)]
    size = sum(x.dtype.itemsize * math.prod(x.shape) for x in args)
    return pl.pallas_call(
        kernel,
        out_shape=[pltpu.VMEM(shape, F32) if pinned else jax.ShapeDtypeStruct(shape, F32) for shape in outs],
        in_specs=[pl.BlockSpec(memory_space=s) for s in spaces],
        out_specs=[pl.BlockSpec(memory_space=pltpu.VMEM) for _ in outs],
        scratch_shapes=scratch,
        compiler_params=pltpu.CompilerParams(vmem_limit_bytes=VMEM_LIMIT),
        cost_estimate=pl.CostEstimate(flops=flops, bytes_accessed=size, transcendentals=0),
    )(*args)


def add_up(x):
    count = lax.axis_size("span") * lax.axis_size("plane")
    rows = jnp.broadcast_to(x, (count, x.shape[1]))
    return lax.all_to_all(rows, ("span", "plane"), split_axis=0, concat_axis=0, tiled=True)


def pairings(size):
    if size % 2:
        return [(i, (i + 1) % size) for i in range(size)], [(i, (i - 1) % size) for i in range(size)]
    return [(i, i ^ 1) for i in range(size)], [(i, (i + 1 if i % 2 else i - 1) % size) for i in range(size)]


def on_device(rhs, blocks, columns, line_slot, line_lower, line_upper, pivot_inv):
    width, nfaces = rhs.shape
    nblocks = columns.shape[0]
    nspan, nplane = lax.axis_size("span"), lax.axis_size("plane")
    owned = nfaces // P_SIZE // nplane
    length = P_SIZE * nplane
    per = owned * P_SIZE
    area = width * width
    shape = (nfaces, width)
    span_pairs, span_others = pairings(nspan)
    plane_pairs, plane_others = pairings(nplane)

    u_first, choose, *send = call(
        functools.partial(start_kernel, nplane),
        [line_slot, rhs.T],
        [shape, (nfaces, 3 * nfaces)] + [(per, width)] * nplane,
        [pltpu.SMEM, pltpu.VMEM],
        ready=False,
    )
    us = [u_first]
    zs = []
    picks = None
    for step in range(ITERS):
        flat = pltpu.VMEM((nfaces, area), F32)
        squares = [(nfaces * width, width)] * 3
        if step == 0:
            factors = call(
                functools.partial(first_squares_kernel, length),
                [line_lower, pivot_inv, line_upper, us[-1]],
                squares,
                [pl.ANY] * 4,
                [flat] * 3 + [pltpu.VMEM(squares[0], F32), pltpu.SemaphoreType.DMA((3,))],
                flops=nfaces * area * width,
            )
        else:
            factors = call(
                functools.partial(next_squares_kernel, length),
                [line_lower, pivot_inv, fold, us[-1]],
                squares,
                [pl.ANY] * 4,
                [flat] * 2 + [pltpu.SemaphoreType.DMA((3,))],
                flops=nfaces * area,
            )
        shaped = [x.reshape(nfaces, width, width) for x in factors]
        got = [exchange(send[k], "plane", k) if k else send[0] for k in far_first(nplane)]
        solved = call(
            functools.partial(line_kernel, nplane, owned),
            [*got, *shaped],
            [(per, width)] * nplane,
            scratch=[pltpu.VMEM((owned, length, width), F32)] * 2,
            flops=6 * nfaces * area,
        )
        if step == 0:
            *picks, fold = pl.pallas_call(
                functools.partial(pick_kernel, nspan, nplane),
                out_shape=[
                    pltpu.VMEM((3 * nfaces, 6 * nfaces), BF16),
                    pltpu.VMEM(((nblocks - 3) * nfaces, 10 * nfaces), BF16),
                    pltpu.HBM(squares[0], F32),
                ],
                in_specs=[pl.BlockSpec(memory_space=pltpu.VMEM)] * 2,
                out_specs=[pl.BlockSpec(memory_space=pltpu.VMEM)] * 2 + [pl.BlockSpec(memory_space=pl.ANY)],
                scratch_shapes=[pltpu.SemaphoreType.DMA],
                compiler_params=pltpu.CompilerParams(vmem_limit_bytes=VMEM_LIMIT),
                cost_estimate=pl.CostEstimate(flops=0, bytes_accessed=4 * nfaces * area, transcendentals=0),
            )(
                lax.optimization_barrier((columns, solved[0]))[0],
                pltpu.with_memory_space_constraint(factors[2], pltpu.VMEM),
            )
        pieces = [exchange(solved[k], "plane", k) if k else solved[0] for k in far_first(nplane)]
        args = [choose, *pieces, *(picks if step == 0 else ())]
        spaces = [pltpu.VMEM] * (nplane + 1) + [pl.ANY] * (len(args) - nplane - 1)
        (mine,) = call(functools.partial(faces_kernel, nplane), args, [shape], spaces)
        zs.append(mine)
        other = lax.ppermute(mine, "span", span_others)
        near = [mine, lax.ppermute(mine, "span", span_pairs), lax.ppermute(mine, "plane", plane_pairs)]
        far = [other, lax.ppermute(mine, "plane", plane_others)]
        chunk = math.lcm(width, 128)

        def scratch(count):
            return [
                pltpu.VMEM((count * nfaces, chunk), F32),
                pltpu.VMEM((nfaces, area), F32),
                pltpu.VMEM((2 * nfaces * area // chunk, chunk), BF16),
            ]

        early_sum, held = call(
            functools.partial(early_kernel, nblocks),
            [blocks, picks[0], *near],
            [shape, (nfaces, (nblocks - 3) * area)],
            [pl.ANY] + [pltpu.VMEM] * 4,
            [pltpu.VMEM((nfaces, 3 * area), F32)] + scratch(3) + [pltpu.SemaphoreType.DMA((6,))],
            flops=6 * nfaces * area,
        )
        last = step == ITERS - 1
        args = [line_slot, held, picks[1], early_sum, *near, *far, *(us if last else us[-1:])]
        out = call(
            functools.partial(late_kernel, nplane, last),
            args,
            [shape] + ([(1, 128)] if last else [(per, width)] * nplane),
            [pl.ANY] + [pltpu.VMEM] * (len(args) - 1),
            scratch(nblocks - 3) + [pltpu.SMEM(line_slot.shape, jnp.int32), pltpu.SemaphoreType.DMA],
            flops=2 * nblocks * nfaces * area,
        )
        us.append(out[0])
        send = out[1:]
    gram = add_up(send[0])
    sol, res, ok = call(finish_kernel, [gram, *us, *zs], [shape, shape, (1, 128)], pinned=False)
    given = (rhs, blocks, columns, line_slot, line_lower, line_upper, pivot_inv)
    _, sol, res = lax.while_loop(
        lambda state: state[0], lambda _: (jnp.array(False), *step_by_step(*given)), (ok[0, 0] < 0.5, sol.T, res.T)
    )
    return sol, res


def solution(mesh):
    both = ("span", "plane")
    return jax.shard_map(
        on_device,
        mesh=mesh,
        in_specs=(
            P(None, both),
            P(both, None),
            P(None, both),
            P(both, None),
            P(both, None),
            P(both, None),
            P(both, None),
        ),
        out_specs=(P(None, both), P(None, both)),
        check_vma=False,
    )
```

```python
import functools
import math

import jax
import jax.numpy as jnp
import numpy as np
from jax import lax
from jax.experimental import pallas as pl
from jax.experimental.pallas import tpu as pltpu
from jax.sharding import PartitionSpec as P

ITERS = 3
P_SIZE = 2
SHIFT = 2.0
EPS = 1e-6
VMEM_LIMIT = 16 * 1024 * 1024
HIGH = lax.Precision.HIGHEST
F32, BF16 = jnp.float32, jnp.bfloat16


def with_halo(x, sides, width, wrap):
    for axis, dim in sides:
        size, length = (lax.axis_size(axis), x.shape[dim])
        up = [(i, (i + 1) % size) for i in range(size if wrap else size - 1)]
        down = [(j, i) for i, j in up]
        last = lax.slice_in_dim(x, length - width, length, axis=dim)
        first = lax.slice_in_dim(x, 0, width, axis=dim)
        before = lax.ppermute(last, axis, up)
        after = lax.ppermute(first, axis, down)
        x = jnp.concatenate([before, x, after], axis=dim)
    return x


def small_solve(factor, target):
    extent = target.shape[0]
    forward_vals = []
    for row in range(extent):
        running = target[row]
        for inner in range(row):
            running = running - factor[row, inner] * forward_vals[inner]
        forward_vals.append(running / factor[row, row])
    backward_vals = [None] * extent
    for row in reversed(range(extent)):
        running = forward_vals[row]
        for inner in range(row + 1, extent):
            running = running - factor[inner, row] * backward_vals[inner]
        backward_vals[row] = running / factor[row, row]
    return jnp.stack(backward_vals)


def to_sequence(factor_rows, nlines, length, width):
    return jnp.swapaxes(factor_rows.reshape(nlines, length, width, width), 0, 1)


def line_solve(rhs_lines, lseq, useq, pseq):
    rseq = jnp.moveaxis(rhs_lines, 2, 0)

    def forward(prev, items):
        right, low = items
        cur = right - jnp.einsum("mab,bm->am", low, prev, precision=HIGH)
        return (cur, cur)

    start = jnp.zeros(rseq.shape[1:], F32)
    _, yseq = lax.scan(forward, start, (rseq, lseq))

    def backward(nxt, items):
        yval, upp, piv = items
        inner = yval - jnp.einsum("mab,bm->am", upp, nxt, precision=HIGH)
        cur = jnp.einsum("mab,bm->am", piv, inner, precision=HIGH)
        return (cur, cur)

    _, zseq = lax.scan(backward, start, (yseq, useq, pseq), reverse=True)
    return jnp.moveaxis(zseq, 0, 2)


def table_positions(columns, nfaces, my_span, my_plane, nspan, nplane):
    device_of = columns // nfaces
    span_of = device_of // nplane
    plane_of = device_of % nplane
    dspan = (span_of - my_span + 1 + nspan) % nspan - 1
    dplane = plane_of - my_plane
    selector = jnp.where(
        dspan == -1,
        1,
        jnp.where(dspan == 1, 2, jnp.where(dplane == -1, 3, jnp.where(dplane == 1, 4, 0))),
    )
    return selector * nfaces + columns % nfaces


def step_by_step(rhs, blocks, columns, line_slot, line_lower, line_upper, pivot_inv):
    width, nfaces = rhs.shape
    nblocks = columns.shape[0]
    nplane = lax.axis_size("plane")
    position = table_positions(
        columns, nfaces, lax.axis_index("span"), lax.axis_index("plane"), lax.axis_size("span"), nplane
    )
    slot = line_slot[0]
    lines_group = nfaces // P_SIZE
    owned = lines_group // nplane
    length = P_SIZE * nplane
    lower = to_sequence(line_lower, owned, length, width)
    upper = to_sequence(line_upper, owned, length, width)
    pivot = to_sequence(pivot_inv, owned, length, width)
    shaped_blocks = blocks.reshape(nfaces, nblocks, width, width)

    def apply_a(vec):
        shaped = vec.reshape(width, 1, 1, nfaces)
        span_side = with_halo(shaped, (("span", 1),), 1, True)
        plane_side = with_halo(shaped, (("plane", 2),), 1, False)
        below = plane_side[:, 0, 0]
        above = plane_side[:, 0, 2]
        table = jnp.concatenate([vec, span_side[:, 0, 0], span_side[:, 2, 0], below, above], axis=1)
        return jnp.einsum("ikab,bki->ai", shaped_blocks, table[:, position], precision=HIGH)

    def apply_m(vec):
        pieces = vec[:, slot].reshape(width, lines_group, P_SIZE)
        whole = lax.all_to_all(pieces, "plane", split_axis=1, concat_axis=2, tiled=True)
        solved = line_solve(whole, lower, upper, pivot)
        back = lax.all_to_all(solved, "plane", split_axis=2, concat_axis=1, tiled=True)
        return jnp.zeros_like(vec).at[:, slot].set(back.reshape(width, nfaces))

    beta = jnp.sqrt(lax.psum(jnp.sum(rhs * rhs), ("span", "plane")) + EPS)
    basis = [rhs / beta]
    hcols = []
    for step in range(ITERS):
        wvec = apply_a(apply_m(basis[step]))
        stacked = jnp.stack(basis)
        hvals = lax.psum(jnp.einsum("jai,ai->j", stacked, wvec, precision=HIGH), ("span", "plane"))
        wvec = wvec - jnp.einsum("j,jai->ai", hvals, stacked, precision=HIGH)
        hnext = jnp.sqrt(lax.psum(jnp.sum(wvec * wvec), ("span", "plane")) + EPS)
        basis.append(wvec / hnext)
        hcols.append(jnp.concatenate([hvals, hnext[None], jnp.zeros((ITERS - step - 1,), F32)]))
    hmat = jnp.stack(hcols, axis=1)
    factor = jnp.linalg.cholesky(jnp.dot(hmat.T, hmat, precision=HIGH))
    coef = small_solve(factor, beta * hmat[0])
    update = jnp.einsum("j,jai->ai", coef, jnp.stack(basis[:ITERS]), precision=HIGH)
    solution = apply_m(update)
    return solution, rhs - apply_a(solution)


def partner(me, k, size):
    if size & (size - 1) == 0:
        return me ^ k, me ^ k
    return (me + k) % size, (me + size - k) % size


def far_first(size):
    return list(reversed(range(size)))


def exchange(x, axis, k):
    size = lax.axis_size(axis)
    return lax.ppermute(x, axis, [(i, partner(i, k, size)[0]) for i in range(size)])


def split(x, parts):
    out = []
    for _ in range(parts):
        out.append(x.astype(BF16).astype(F32))
        x = x - out[-1]
    return jnp.concatenate(out, axis=0)


def start_kernel(nplane, slot_ref, u_ref, copy_ref, choose_ref, *outs):
    nfaces = u_ref.shape[0]
    per = nfaces // nplane
    me = lax.axis_index("plane")
    for k in range(nplane):
        to, _ = partner(me, k, nplane)
        for i in range(per):
            outs[k][pl.ds(i, 1), :] = u_ref[pl.ds(slot_ref[0, to * per + i], 1), :]
    copy_ref[...] = u_ref[...]
    face = lax.broadcasted_iota(jnp.int32, choose_ref.shape, 0)
    piece = lax.broadcasted_iota(jnp.int32, choose_ref.shape, 1) % nfaces
    choose = jnp.zeros(choose_ref.shape, F32)
    for n, k in enumerate(far_first(nplane)):
        _, source = partner(me, k, nplane)
        for i in range(per):
            hit = (face == slot_ref[0, source * per + i]) & (piece == n * per + i)
            choose = jnp.where(hit, 1.0, choose)
    choose_ref[...] = choose


def to_squares(src, dst):
    nrows, width = src.shape[0], dst.shape[1]
    chunk = math.lcm(width, 128)
    for c in range(width * width // chunk):
        piece = src[:, c * chunk : (c + 1) * chunk]
        for r in range(chunk // width):
            a = c * (chunk // width) + r
            dst[pl.ds(a, nrows, stride=width), :] = piece[:, r * width : (r + 1) * width]


def turn_some(squares, length, parity):
    width = squares.shape[1]
    for at in range(squares.shape[0] // width):
        if at % length % 2 == parity and at % length:
            here = slice(at * width, (at + 1) * width)
            squares[here, :] = squares[here, :].T


def first_squares_kernel(length, low, piv, upp, _, low_out, piv_out, fold_out, low_scr, piv_scr, upp_scr, upp_sq, sems):
    width = low_out.shape[1]
    fetches = []
    for n, (src, scr) in enumerate(((low, low_scr), (piv, piv_scr), (upp, upp_scr))):
        fetches.append(pltpu.make_async_copy(src, scr, sems.at[n]))
        fetches[-1].start()
    for fetch, scr, dst in zip(fetches, (low_scr, piv_scr, upp_scr), (low_out, piv_out, upp_sq)):
        fetch.wait()
        to_squares(scr, dst)
    for at in range(low.shape[0]):
        here = slice(at * width, (at + 1) * width)
        if at % length == length - 1:
            fold_out[here, :] = jnp.zeros((width, width), F32)
            continue
        (ph, pl_), (uh, ul) = [
            (x.astype(BF16), (x - x.astype(BF16).astype(F32)).astype(BF16)) for x in (piv_out[here, :], upp_sq[here, :])
        ]
        fold = sum(jnp.dot(x, y, preferred_element_type=F32) for x, y in ((pl_, uh), (ph, ul), (ph, uh)))
        fold_out[here, :] = fold.T if at % length % 2 else fold
    turn_some(low_out, length, 0)
    turn_some(piv_out, length, 1)


def next_squares_kernel(length, low, piv, fold, _, low_out, piv_out, fold_out, low_scr, piv_scr, sems):
    fetches = []
    for n, (src, scr) in enumerate(((low, low_scr), (piv, piv_scr), (fold, fold_out))):
        fetches.append(pltpu.make_async_copy(src, scr, sems.at[n]))
        fetches[-1].start()
    for fetch, scr, dst, parity in zip(fetches, (low_scr, piv_scr), (low_out, piv_out), (0, 1)):
        fetch.wait()
        to_squares(scr, dst)
        turn_some(dst, length, parity)
    fetches[2].wait()


def parities():
    return [1 if lax.axis_size(a) % 2 else lax.axis_index(a) % 2 for a in ("span", "plane")]


def early_blocks():
    span_odd, plane_odd = parities()
    return (1 + span_odd, 3 + plane_odd), (2 - span_odd, 4 - plane_odd)


def pick_kernel(nspan, nplane, width, columns_ref, fold_ref, early_ref, late_ref, seg_ref, store_ref, sem):
    store = pltpu.make_async_copy(fold_ref, store_ref, sem)
    store.start()
    copies = seg_ref.shape[0] // width
    lane = lax.broadcasted_iota(jnp.int32, (width, 128), 1) % copies
    for r in range(copies):
        seg_ref[r * width : (r + 1) * width, :] = jnp.where(lane == r, 1.0, 0.0).astype(BF16)
    nblocks, nfaces = columns_ref.shape
    span, plane = lax.axis_index("span"), lax.axis_index("plane")
    position = table_positions(columns_ref[...], nfaces, span, plane, nspan, nplane)
    selector, face = position // nfaces, position % nfaces
    span_odd, plane_odd = [parity == 1 for parity in parities()]
    of_span = jnp.where((selector == 1) == span_odd, 1, 3)
    of_plane = jnp.where((selector == 3) == plane_odd, 2, 4)
    group = jnp.where(selector == 0, 0, jnp.where(selector <= 2, of_span, of_plane))
    at = (group * nfaces + face).astype(F32)
    eye = lax.broadcasted_iota(jnp.int32, (nfaces, nfaces), 0) == lax.broadcasted_iota(jnp.int32, (nfaces, nfaces), 1)
    first, second = jnp.where(span_odd, at[2:3], at[1:2]), jnp.where(span_odd, at[1:2], at[2:3])
    third, fourth = jnp.where(plane_odd, at[4:5], at[3:4]), jnp.where(plane_odd, at[3:4], at[4:5])
    rest = [at[k : k + 1] for k in range(5, nblocks)]
    for ref, rows in ((early_ref, [at[0:1], first, third]), (late_ref, [second, fourth, *rest])):
        lane = lax.broadcasted_iota(jnp.int32, (nfaces, ref.shape[1]), 1) % (ref.shape[1] // 3)
        for n, row in enumerate(rows):
            column = jnp.sum(jnp.where(eye, row, 0.0), axis=1, keepdims=True).astype(jnp.int32)
            ref[n * nfaces : (n + 1) * nfaces, :] = jnp.where(lane == column, 1.0, 0.0).astype(BF16)
    store.wait()


def line_kernel(nplane, nlines, *refs):
    msgs, (low, piv, fold), outs, (r_scr, z_scr) = refs[:nplane], refs[nplane:-nplane-2], refs[-nplane-2:-2], refs[-2:]
    _, length, width = r_scr.shape
    me = lax.axis_index("plane")
    for k, msg in zip(far_first(nplane), msgs):
        _, source = partner(me, k, nplane)
        for m in range(nlines):
            for q in range(P_SIZE):
                r_scr[m, pl.ds(source * P_SIZE + q, 1), :] = msg[pl.ds(m * P_SIZE + q, 1), :]
    eye = lax.broadcasted_iota(jnp.int32, (width, width), 0) == lax.broadcasted_iota(jnp.int32, (width, width), 1)

    def column(row):
        return jnp.sum(jnp.where(eye, row, 0.0), axis=1, keepdims=True)

    rows = [[r_scr[m, pl.ds(j, 1), :] for m in range(nlines)] for j in range(length)]
    scaled = [[None] * nlines for _ in range(length)]
    carry = [None] * nlines
    for j in range(length):
        for m in range(nlines):
            at = m * length + j
            if j == 0:
                carry[m] = rows[j][m]
            elif j % 2:
                carry[m] = column(rows[j][m]) - jnp.sum(low[at] * carry[m], axis=1, keepdims=True)
            else:
                carry[m] = rows[j][m] - jnp.sum(low[at] * carry[m], axis=0, keepdims=True)
            scaled[j][m] = jnp.sum(piv[at] * carry[m], axis=0 if j % 2 else 1, keepdims=True)
    after = [None] * nlines
    for j in reversed(range(length)):
        for m in range(nlines):
            at = m * length + j
            value = scaled[j][m]
            if j < length - 1:
                value = value - jnp.sum(fold[at] * after[m], axis=0 if j % 2 else 1, keepdims=True)
            after[m] = value
            row = value if j % 2 else jnp.sum(jnp.where(eye, value, 0.0), axis=0, keepdims=True)
            z_scr[m, pl.ds(j, 1), :] = row
    for k in range(nplane):
        to, _ = partner(me, k, nplane)
        for m in range(nlines):
            for q in range(P_SIZE):
                outs[k][pl.ds(m * P_SIZE + q, 1), :] = z_scr[m, pl.ds(to * P_SIZE + q, 1), :]


def faces_kernel(nplane, choose, *refs):
    solved, mine_ref = refs[:nplane], refs[-1]
    table = split(jnp.concatenate([s[...] for s in solved], axis=0), 3).astype(BF16)
    mine_ref[...] = jnp.dot(choose[...].astype(BF16), table, preferred_element_type=F32)


def repeat_faces(faces, pick, copies):
    table = split(jnp.concatenate([f[...] for f in faces], axis=0), 3).astype(BF16)
    picked = jnp.dot(pick[...], table, preferred_element_type=F32)
    return jnp.concatenate([picked] * copies, axis=1)


def add_products(work, x_scr, acc_scr, parts, seg, width):
    nfaces, area = acc_scr.shape
    chunk = x_scr.shape[1]
    copies, count = chunk // width, area // chunk
    lane = lax.broadcasted_iota(jnp.int32, (1, 128), 1)
    total = jnp.zeros((nfaces, 128), F32)
    done = 0
    for n, (places, fetch) in enumerate(work):
        if fetch is not None:
            fetch.wait()
        last = n == len(work) - 1
        for half in ((0, count // 2), (count // 2, count)):
            for v in range(0, chunk, 128):
                rows = range(done * nfaces, (done + len(places)) * nfaces, nfaces)
                xs = [x_scr[row : row + nfaces, v : v + 128] for row in rows]
                for c in range(*half):
                    at = c * chunk + v
                    value = acc_scr[:, at : at + 128] if n else None
                    for (ref, column), x in zip(places, xs):
                        term = ref[:, column + at : column + at + 128] * x
                        value = term if value is None else value + term
                    if not last:
                        acc_scr[:, at : at + 128] = value
                        continue
                    for n_part in range(3):
                        part = value.astype(BF16)
                        row = (3 * c + n_part) * nfaces
                        parts[row : row + nfaces, v : v + 128] = part
                        value = value - part.astype(F32)
            if last:
                base = 3 * half[0] * nfaces
                sums = jnp.dot(parts[base : 3 * half[1] * nfaces, :], seg[...], preferred_element_type=F32)
                for c in range(*half):
                    high, middle, low = [
                        sums[at : at + nfaces] for at in range(3 * c * nfaces - base, 3 * (c + 1) * nfaces - base, nfaces)
                    ]
                    total = total + jnp.where(lane // copies == c, high + (middle + low), 0.0)
        done += len(places)
    return total[:, :width]


def early_kernel(nblocks, blocks, pick, seg, *refs):
    faces, (sum_ref, held, buf, x_scr, acc_scr, parts, sems) = refs[:3], refs[3:]
    width = faces[0].shape[1]
    area = width * width
    early, late = early_blocks()

    def fetch(k, count, dst, column, n):
        start = pl.multiple_of(k * area, 128) if not isinstance(k, int) else k * area
        return pltpu.make_async_copy(
            blocks.at[:, pl.ds(start, count * area)], dst.at[:, pl.ds(column, count * area)], sems.at[n]
        )

    mine = [fetch(k, 1, buf, n * area, n) for n, k in enumerate((0, *early))]
    kept = [fetch(k, 1, held, n * area, 3 + n) for n, k in enumerate(late)]
    kept.append(fetch(5, nblocks - 5, held, 2 * area, 5))
    for copy in mine + kept:
        copy.start()
    x_scr[...] = repeat_faces(faces, pick, x_scr.shape[1] // width)
    work = [([(buf, n * area)], copy) for n, copy in enumerate(mine)]
    sum_ref[...] = add_products(work, x_scr, acc_scr, parts, seg, width)
    for copy in kept:
        copy.wait()


def late_kernel(nplane, last, *refs):
    (slot, held, pick, seg, early_sum), faces, refs = refs[:5], refs[5:10], refs[10:]
    nold = ITERS if last else 1
    olds, refs = refs[:nold], refs[nold:]
    next_ref, outs, (x_scr, acc_scr, parts, slot_scr, slot_sem) = refs[0], refs[1:-5], refs[-5:]
    nfaces, width = faces[0].shape
    area = width * width
    if not last:
        slots = pltpu.make_async_copy(slot, slot_scr, slot_sem)
        slots.start()
    x_scr[...] = repeat_faces(faces, pick, x_scr.shape[1] // width)
    work = [([(held, column) for column in range(0, held.shape[1], area)], None)]
    u_next = early_sum[...] + add_products(work, x_scr, acc_scr, parts, seg, width) - SHIFT * olds[-1][...]
    next_ref[...] = u_next
    if last:
        gram_ref = outs[0]
        lane = lax.broadcasted_iota(jnp.int32, gram_ref.shape, 1)
        basis = [old[...] for old in olds] + [u_next]
        gram, at = jnp.zeros(gram_ref.shape, F32), 0
        for i in range(ITERS + 1):
            for j in range(i, ITERS + 1):
                value = jnp.sum(jnp.sum(basis[i] * basis[j], axis=0, keepdims=True), axis=1, keepdims=True)
                gram, at = jnp.where(lane == at, value, gram), at + 1
        gram_ref[...] = gram
    else:
        per = nfaces // nplane
        me = lax.axis_index("plane")
        slots.wait()
        for k in range(nplane):
            to, _ = partner(me, k, nplane)
            for i in range(per):
                outs[k][pl.ds(i, 1), :] = next_ref[pl.ds(slot_scr[0, to * per + i], 1), :]


def finish_kernel(gram_ref, *refs):
    us, zs = refs[: ITERS + 1], refs[ITERS + 1 : 2 * ITERS + 1]
    sol_ref, res_ref, ok_ref = refs[2 * ITERS + 1 :]
    width = sol_ref.shape[1]
    rows = jnp.sum(gram_ref[...], axis=0, keepdims=True)
    lane = lax.broadcasted_iota(jnp.int32, rows.shape, 1)
    gram, at = {}, 0
    for i in range(ITERS + 1):
        for j in range(i, ITERS + 1):
            value = jnp.sum(jnp.where(lane == at, rows, 0.0), axis=1, keepdims=True)
            gram[i, j] = gram[j, i] = jnp.broadcast_to(value, rows.shape)
            at += 1
    largest = functools.reduce(jnp.maximum, [jnp.abs(g) for g in gram.values()])
    ok = largest < 1e30
    beta = jnp.sqrt(gram[0, 0] + EPS)
    basis = [[1.0 / beta]]
    hmat = {}
    for step in range(ITERS):
        own = basis[step]
        wvec = [SHIFT * own[0]] + [own[i] + SHIFT * own[i + 1] for i in range(step)] + [own[step]]
        images = [sum(gram[i, j] * wvec[j] for j in range(step + 2)) for i in range(step + 1)]
        for i in range(step + 1):
            hmat[i, step] = sum(basis[i][m] * images[m] for m in range(i + 1))
        for i in range(step + 1):
            for m in range(i + 1):
                wvec[m] = wvec[m] - hmat[i, step] * basis[i][m]
        terms = [wvec[i] * wvec[j] * gram[i, j] for i in range(step + 2) for j in range(step + 2)]
        square = jnp.maximum(sum(terms), 0.0)
        ok = ok & (square + EPS >= 2e-3 * sum(jnp.abs(term) for term in terms))
        hmat[step + 1, step] = jnp.sqrt(square + EPS)
        scale = 1.0 / hmat[step + 1, step]
        basis.append([w * scale for w in wvec])
    normal = {
        (i, j): sum(hmat[m, i] * hmat[m, j] for m in range(j + 2) if (m, i) in hmat and (m, j) in hmat)
        for i in range(ITERS)
        for j in range(i + 1)
    }
    factor, inverse = {}, []
    for j in range(ITERS):
        diag = jnp.sqrt(normal[j, j] - sum(factor[j, m] * factor[j, m] for m in range(j)))
        inverse.append(1.0 / diag)
        for i in range(j + 1, ITERS):
            factor[i, j] = (normal[i, j] - sum(factor[i, m] * factor[j, m] for m in range(j))) * inverse[j]
    forward = []
    for i in range(ITERS):
        forward.append((beta * hmat[0, i] - sum(factor[i, m] * forward[m] for m in range(i))) * inverse[i])
    coef = [None] * ITERS
    for i in reversed(range(ITERS)):
        coef[i] = (forward[i] - sum(factor[m, i] * coef[m] for m in range(i + 1, ITERS))) * inverse[i]
    mix = [sum(coef[s] * basis[s][m] for s in range(m, ITERS))[:, :width] for m in range(ITERS)]
    sol_ref[...] = sum(mix[m] * zs[m][...] for m in range(ITERS))
    image = sum(mix[m] * (us[m + 1][...] + SHIFT * us[m][...]) for m in range(ITERS))
    res_ref[...] = us[0][...] - image
    ok = ok & (functools.reduce(jnp.maximum, [jnp.abs(c) for c in coef]) < 1e30)
    ok_ref[...] = jnp.where(ok, 1.0, 0.0)


def call(kernel, args, outs, spaces=None, scratch=(), flops=0, pinned=True, ready=True):
    spaces = [pltpu.VMEM] * len(args) if spaces is None else spaces
    if ready:
        args = [pltpu.with_memory_space_constraint(x, s) if s is pltpu.VMEM else x for x, s in zip(args, spaces)]
    size = sum(x.dtype.itemsize * math.prod(x.shape) for x in args)
    return pl.pallas_call(
        kernel,
        out_shape=[pltpu.VMEM(shape, F32) if pinned else jax.ShapeDtypeStruct(shape, F32) for shape in outs],
        in_specs=[pl.BlockSpec(memory_space=s) for s in spaces],
        out_specs=[pl.BlockSpec(memory_space=pltpu.VMEM) for _ in outs],
        scratch_shapes=scratch,
        compiler_params=pltpu.CompilerParams(vmem_limit_bytes=VMEM_LIMIT),
        cost_estimate=pl.CostEstimate(flops=flops, bytes_accessed=size, transcendentals=0),
    )(*args)


def add_up(x):
    count = lax.axis_size("span") * lax.axis_size("plane")
    rows = jnp.broadcast_to(x, (count, x.shape[1]))
    return lax.all_to_all(rows, ("span", "plane"), split_axis=0, concat_axis=0, tiled=True)


def pairings(size):
    if size % 2:
        return [(i, (i + 1) % size) for i in range(size)], [(i, (i - 1) % size) for i in range(size)]
    return [(i, i ^ 1) for i in range(size)], [(i, (i + 1 if i % 2 else i - 1) % size) for i in range(size)]


def on_device(rhs, blocks, columns, line_slot, line_lower, line_upper, pivot_inv):
    width, nfaces = rhs.shape
    nblocks = columns.shape[0]
    nspan, nplane = lax.axis_size("span"), lax.axis_size("plane")
    owned = nfaces // P_SIZE // nplane
    length = P_SIZE * nplane
    per = owned * P_SIZE
    area = width * width
    shape = (nfaces, width)
    span_pairs, span_others = pairings(nspan)
    plane_pairs, plane_others = pairings(nplane)

    u_first, choose, *send = call(
        functools.partial(start_kernel, nplane),
        [line_slot, rhs.T],
        [shape, (nfaces, 3 * nfaces)] + [(per, width)] * nplane,
        [pltpu.SMEM, pltpu.VMEM],
        ready=False,
    )
    us = [u_first]
    zs = []
    picks = None
    for step in range(ITERS):
        flat = pltpu.VMEM((nfaces, area), F32)
        squares = [(nfaces * width, width)] * 3
        if step == 0:
            factors = call(
                functools.partial(first_squares_kernel, length),
                [line_lower, pivot_inv, line_upper, us[-1]],
                squares,
                [pl.ANY] * 4,
                [flat] * 3 + [pltpu.VMEM(squares[0], F32), pltpu.SemaphoreType.DMA((3,))],
                flops=nfaces * area * width,
            )
        else:
            factors = call(
                functools.partial(next_squares_kernel, length),
                [line_lower, pivot_inv, fold, us[-1]],
                squares,
                [pl.ANY] * 4,
                [flat] * 2 + [pltpu.SemaphoreType.DMA((3,))],
                flops=nfaces * area,
            )
        shaped = [x.reshape(nfaces, width, width) for x in factors]
        got = [exchange(send[k], "plane", k) if k else send[0] for k in far_first(nplane)]
        solved = call(
            functools.partial(line_kernel, nplane, owned),
            [*got, *shaped],
            [(per, width)] * nplane,
            scratch=[pltpu.VMEM((owned, length, width), F32)] * 2,
            flops=6 * nfaces * area,
        )
        if step == 0:
            *picks, fold = pl.pallas_call(
                functools.partial(pick_kernel, nspan, nplane, width),
                out_shape=[
                    pltpu.VMEM((3 * nfaces, 9 * nfaces), BF16),
                    pltpu.VMEM(((nblocks - 3) * nfaces, 15 * nfaces), BF16),
                    pltpu.VMEM((math.lcm(width, 128), 128), BF16),
                    pltpu.HBM(squares[0], F32),
                ],
                in_specs=[pl.BlockSpec(memory_space=pltpu.VMEM)] * 2,
                out_specs=[pl.BlockSpec(memory_space=pltpu.VMEM)] * 3 + [pl.BlockSpec(memory_space=pl.ANY)],
                scratch_shapes=[pltpu.SemaphoreType.DMA],
                compiler_params=pltpu.CompilerParams(vmem_limit_bytes=VMEM_LIMIT),
                cost_estimate=pl.CostEstimate(flops=0, bytes_accessed=4 * nfaces * area, transcendentals=0),
            )(
                lax.optimization_barrier((columns, solved[0]))[0],
                pltpu.with_memory_space_constraint(factors[2], pltpu.VMEM),
            )
        pieces = [exchange(solved[k], "plane", k) if k else solved[0] for k in far_first(nplane)]
        args = [choose, *pieces, *(picks if step == 0 else ())]
        spaces = [pltpu.VMEM] * (nplane + 1) + [pl.ANY] * (len(args) - nplane - 1)
        (mine,) = call(functools.partial(faces_kernel, nplane), args, [shape], spaces)
        zs.append(mine)
        other = lax.ppermute(mine, "span", span_others)
        near = [mine, lax.ppermute(mine, "span", span_pairs), lax.ppermute(mine, "plane", plane_pairs)]
        far = [other, lax.ppermute(mine, "plane", plane_others)]
        chunk = math.lcm(width, 128)

        def scratch(count):
            return [
                pltpu.VMEM((count * nfaces, chunk), F32),
                pltpu.VMEM((nfaces, area), F32),
                pltpu.VMEM((3 * nfaces * area // chunk, chunk), BF16),
            ]

        early_sum, held = call(
            functools.partial(early_kernel, nblocks),
            [blocks, picks[0], picks[2], *near],
            [shape, (nfaces, (nblocks - 3) * area)],
            [pl.ANY] + [pltpu.VMEM] * 5,
            [pltpu.VMEM((nfaces, 3 * area), F32)] + scratch(3) + [pltpu.SemaphoreType.DMA((6,))],
            flops=6 * nfaces * area,
        )
        last = step == ITERS - 1
        args = [line_slot, held, picks[1], picks[2], early_sum, *near, *far, *(us if last else us[-1:])]
        out = call(
            functools.partial(late_kernel, nplane, last),
            args,
            [shape] + ([(1, 128)] if last else [(per, width)] * nplane),
            [pl.ANY] + [pltpu.VMEM] * (len(args) - 1),
            scratch(nblocks - 3) + [pltpu.SMEM(line_slot.shape, jnp.int32), pltpu.SemaphoreType.DMA],
            flops=2 * nblocks * nfaces * area,
        )
        us.append(out[0])
        send = out[1:]
    gram = add_up(send[0])
    sol, res, ok = call(finish_kernel, [gram, *us, *zs], [shape, shape, (1, 128)], pinned=False)
    given = (rhs, blocks, columns, line_slot, line_lower, line_upper, pivot_inv)
    _, sol, res = lax.while_loop(
        lambda state: state[0], lambda _: (jnp.array(False), *step_by_step(*given)), (ok[0, 0] < 0.5, sol.T, res.T)
    )
    return sol, res


def solution(mesh):
    both = ("span", "plane")
    return jax.shard_map(
        on_device,
        mesh=mesh,
        in_specs=(
            P(None, both),
            P(both, None),
            P(None, both),
            P(both, None),
            P(both, None),
            P(both, None),
            P(both, None),
        ),
        out_specs=(P(None, both), P(None, both)),
        check_vma=False,
    )
```

```python
import functools
import math

import jax
import jax.numpy as jnp
import numpy as np
from jax import lax
from jax.experimental import pallas as pl
from jax.experimental.pallas import tpu as pltpu
from jax.sharding import PartitionSpec as P

ITERS = 3
P_SIZE = 2
SHIFT = 2.0
EPS = 1e-6
VMEM_LIMIT = 16 * 1024 * 1024
HIGH = lax.Precision.HIGHEST
F32, BF16 = jnp.float32, jnp.bfloat16


def with_halo(x, sides, width, wrap):
    for axis, dim in sides:
        size, length = (lax.axis_size(axis), x.shape[dim])
        up = [(i, (i + 1) % size) for i in range(size if wrap else size - 1)]
        down = [(j, i) for i, j in up]
        last = lax.slice_in_dim(x, length - width, length, axis=dim)
        first = lax.slice_in_dim(x, 0, width, axis=dim)
        before = lax.ppermute(last, axis, up)
        after = lax.ppermute(first, axis, down)
        x = jnp.concatenate([before, x, after], axis=dim)
    return x


def small_solve(factor, target):
    extent = target.shape[0]
    forward_vals = []
    for row in range(extent):
        running = target[row]
        for inner in range(row):
            running = running - factor[row, inner] * forward_vals[inner]
        forward_vals.append(running / factor[row, row])
    backward_vals = [None] * extent
    for row in reversed(range(extent)):
        running = forward_vals[row]
        for inner in range(row + 1, extent):
            running = running - factor[inner, row] * backward_vals[inner]
        backward_vals[row] = running / factor[row, row]
    return jnp.stack(backward_vals)


def to_sequence(factor_rows, nlines, length, width):
    return jnp.swapaxes(factor_rows.reshape(nlines, length, width, width), 0, 1)


def line_solve(rhs_lines, lseq, useq, pseq):
    rseq = jnp.moveaxis(rhs_lines, 2, 0)

    def forward(prev, items):
        right, low = items
        cur = right - jnp.einsum("mab,bm->am", low, prev, precision=HIGH)
        return (cur, cur)

    start = jnp.zeros(rseq.shape[1:], F32)
    _, yseq = lax.scan(forward, start, (rseq, lseq))

    def backward(nxt, items):
        yval, upp, piv = items
        inner = yval - jnp.einsum("mab,bm->am", upp, nxt, precision=HIGH)
        cur = jnp.einsum("mab,bm->am", piv, inner, precision=HIGH)
        return (cur, cur)

    _, zseq = lax.scan(backward, start, (yseq, useq, pseq), reverse=True)
    return jnp.moveaxis(zseq, 0, 2)


def table_positions(columns, nfaces, my_span, my_plane, nspan, nplane):
    device_of = columns // nfaces
    span_of = device_of // nplane
    plane_of = device_of % nplane
    dspan = (span_of - my_span + 1 + nspan) % nspan - 1
    dplane = plane_of - my_plane
    selector = jnp.where(
        dspan == -1,
        1,
        jnp.where(dspan == 1, 2, jnp.where(dplane == -1, 3, jnp.where(dplane == 1, 4, 0))),
    )
    return selector * nfaces + columns % nfaces


def step_by_step(rhs, blocks, columns, line_slot, line_lower, line_upper, pivot_inv):
    width, nfaces = rhs.shape
    nblocks = columns.shape[0]
    nplane = lax.axis_size("plane")
    position = table_positions(
        columns, nfaces, lax.axis_index("span"), lax.axis_index("plane"), lax.axis_size("span"), nplane
    )
    slot = line_slot[0]
    lines_group = nfaces // P_SIZE
    owned = lines_group // nplane
    length = P_SIZE * nplane
    lower = to_sequence(line_lower, owned, length, width)
    upper = to_sequence(line_upper, owned, length, width)
    pivot = to_sequence(pivot_inv, owned, length, width)
    shaped_blocks = blocks.reshape(nfaces, nblocks, width, width)

    def apply_a(vec):
        shaped = vec.reshape(width, 1, 1, nfaces)
        span_side = with_halo(shaped, (("span", 1),), 1, True)
        plane_side = with_halo(shaped, (("plane", 2),), 1, False)
        below = plane_side[:, 0, 0]
        above = plane_side[:, 0, 2]
        table = jnp.concatenate([vec, span_side[:, 0, 0], span_side[:, 2, 0], below, above], axis=1)
        return jnp.einsum("ikab,bki->ai", shaped_blocks, table[:, position], precision=HIGH)

    def apply_m(vec):
        pieces = vec[:, slot].reshape(width, lines_group, P_SIZE)
        whole = lax.all_to_all(pieces, "plane", split_axis=1, concat_axis=2, tiled=True)
        solved = line_solve(whole, lower, upper, pivot)
        back = lax.all_to_all(solved, "plane", split_axis=2, concat_axis=1, tiled=True)
        return jnp.zeros_like(vec).at[:, slot].set(back.reshape(width, nfaces))

    beta = jnp.sqrt(lax.psum(jnp.sum(rhs * rhs), ("span", "plane")) + EPS)
    basis = [rhs / beta]
    hcols = []
    for step in range(ITERS):
        wvec = apply_a(apply_m(basis[step]))
        stacked = jnp.stack(basis)
        hvals = lax.psum(jnp.einsum("jai,ai->j", stacked, wvec, precision=HIGH), ("span", "plane"))
        wvec = wvec - jnp.einsum("j,jai->ai", hvals, stacked, precision=HIGH)
        hnext = jnp.sqrt(lax.psum(jnp.sum(wvec * wvec), ("span", "plane")) + EPS)
        basis.append(wvec / hnext)
        hcols.append(jnp.concatenate([hvals, hnext[None], jnp.zeros((ITERS - step - 1,), F32)]))
    hmat = jnp.stack(hcols, axis=1)
    factor = jnp.linalg.cholesky(jnp.dot(hmat.T, hmat, precision=HIGH))
    coef = small_solve(factor, beta * hmat[0])
    update = jnp.einsum("j,jai->ai", coef, jnp.stack(basis[:ITERS]), precision=HIGH)
    solution = apply_m(update)
    return solution, rhs - apply_a(solution)


def partner(me, k, size):
    if size & (size - 1) == 0:
        return me ^ k, me ^ k
    return (me + k) % size, (me + size - k) % size


def far_first(size):
    return list(reversed(range(size)))


def exchange(x, axis, k):
    size = lax.axis_size(axis)
    return lax.ppermute(x, axis, [(i, partner(i, k, size)[0]) for i in range(size)])


def split(x, parts):
    out = []
    for _ in range(parts):
        out.append(x.astype(BF16).astype(F32))
        x = x - out[-1]
    return jnp.concatenate(out, axis=0)


def start_kernel(nplane, slot_ref, u_ref, copy_ref, choose_ref, *outs):
    nfaces = u_ref.shape[0]
    per = nfaces // nplane
    me = lax.axis_index("plane")
    for k in range(nplane):
        to, _ = partner(me, k, nplane)
        for i in range(per):
            outs[k][pl.ds(i, 1), :] = u_ref[pl.ds(slot_ref[0, to * per + i], 1), :]
    copy_ref[...] = u_ref[...]
    face = lax.broadcasted_iota(jnp.int32, choose_ref.shape, 0)
    piece = lax.broadcasted_iota(jnp.int32, choose_ref.shape, 1) % nfaces
    choose = jnp.zeros(choose_ref.shape, F32)
    for n, k in enumerate(far_first(nplane)):
        _, source = partner(me, k, nplane)
        for i in range(per):
            hit = (face == slot_ref[0, source * per + i]) & (piece == n * per + i)
            choose = jnp.where(hit, 1.0, choose)
    choose_ref[...] = choose


def to_squares(src, dst):
    nrows, width = src.shape[0], dst.shape[1]
    chunk = math.lcm(width, 128)
    for c in range(width * width // chunk):
        piece = src[:, c * chunk : (c + 1) * chunk]
        for r in range(chunk // width):
            a = c * (chunk // width) + r
            dst[pl.ds(a, nrows, stride=width), :] = piece[:, r * width : (r + 1) * width]


def turn_some(squares, length, parity):
    width = squares.shape[1]
    for at in range(squares.shape[0] // width):
        if at % length % 2 == parity and at % length:
            here = slice(at * width, (at + 1) * width)
            squares[here, :] = squares[here, :].T


def first_squares_kernel(length, low, piv, upp, _, low_out, piv_out, fold_out, low_scr, piv_scr, upp_scr, upp_sq, sems):
    width = low_out.shape[1]
    fetches = []
    for n, (src, scr) in enumerate(((low, low_scr), (piv, piv_scr), (upp, upp_scr))):
        fetches.append(pltpu.make_async_copy(src, scr, sems.at[n]))
        fetches[-1].start()
    for fetch, scr, dst in zip(fetches, (low_scr, piv_scr, upp_scr), (low_out, piv_out, upp_sq)):
        fetch.wait()
        to_squares(scr, dst)
    for at in range(low.shape[0]):
        here = slice(at * width, (at + 1) * width)
        if at % length == length - 1:
            fold_out[here, :] = jnp.zeros((width, width), F32)
            continue
        (ph, pl_), (uh, ul) = [
            (x.astype(BF16), (x - x.astype(BF16).astype(F32)).astype(BF16)) for x in (piv_out[here, :], upp_sq[here, :])
        ]
        fold = sum(jnp.dot(x, y, preferred_element_type=F32) for x, y in ((pl_, uh), (ph, ul), (ph, uh)))
        fold_out[here, :] = fold.T if at % length % 2 else fold
    turn_some(low_out, length, 0)
    turn_some(piv_out, length, 1)


def next_squares_kernel(length, low, piv, fold, _, low_out, piv_out, fold_out, low_scr, piv_scr, sems):
    fetches = []
    for n, (src, scr) in enumerate(((low, low_scr), (piv, piv_scr), (fold, fold_out))):
        fetches.append(pltpu.make_async_copy(src, scr, sems.at[n]))
        fetches[-1].start()
    for fetch, scr, dst, parity in zip(fetches, (low_scr, piv_scr), (low_out, piv_out), (0, 1)):
        fetch.wait()
        to_squares(scr, dst)
        turn_some(dst, length, parity)
    fetches[2].wait()


def parities():
    return [1 if lax.axis_size(a) % 2 else lax.axis_index(a) % 2 for a in ("span", "plane")]


def early_blocks():
    span_odd, plane_odd = parities()
    return (1 + span_odd, 3 + plane_odd), (2 - span_odd, 4 - plane_odd)


def pick_kernel(nspan, nplane, width, columns_ref, fold_ref, early_ref, late_ref, seg_ref, store_ref, sem):
    store = pltpu.make_async_copy(fold_ref, store_ref, sem)
    store.start()
    copies = seg_ref.shape[0] // width
    lane = lax.broadcasted_iota(jnp.int32, (width, 128), 1) % copies
    for r in range(copies):
        seg_ref[r * width : (r + 1) * width, :] = jnp.where(lane == r, 1.0, 0.0).astype(BF16)
    nblocks, nfaces = columns_ref.shape
    span, plane = lax.axis_index("span"), lax.axis_index("plane")
    position = table_positions(columns_ref[...], nfaces, span, plane, nspan, nplane)
    selector, face = position // nfaces, position % nfaces
    span_odd, plane_odd = [parity == 1 for parity in parities()]
    of_span = jnp.where((selector == 1) == span_odd, 1, 3)
    of_plane = jnp.where((selector == 3) == plane_odd, 2, 4)
    group = jnp.where(selector == 0, 0, jnp.where(selector <= 2, of_span, of_plane))
    at = (group * nfaces + face).astype(F32)
    eye = lax.broadcasted_iota(jnp.int32, (nfaces, nfaces), 0) == lax.broadcasted_iota(jnp.int32, (nfaces, nfaces), 1)
    first, second = jnp.where(span_odd, at[2:3], at[1:2]), jnp.where(span_odd, at[1:2], at[2:3])
    third, fourth = jnp.where(plane_odd, at[4:5], at[3:4]), jnp.where(plane_odd, at[3:4], at[4:5])
    rest = [at[k : k + 1] for k in range(5, nblocks)]
    for ref, rows in ((early_ref, [at[0:1], first, third]), (late_ref, [second, fourth, *rest])):
        lane = lax.broadcasted_iota(jnp.int32, (nfaces, ref.shape[1]), 1) % (ref.shape[1] // 3)
        for n, row in enumerate(rows):
            column = jnp.sum(jnp.where(eye, row, 0.0), axis=1, keepdims=True).astype(jnp.int32)
            ref[n * nfaces : (n + 1) * nfaces, :] = jnp.where(lane == column, 1.0, 0.0).astype(BF16)
    store.wait()


def line_kernel(nplane, nlines, *refs):
    msgs, (low, piv, fold), outs, (r_scr, z_scr) = refs[:nplane], refs[nplane:-nplane-2], refs[-nplane-2:-2], refs[-2:]
    _, length, width = r_scr.shape
    me = lax.axis_index("plane")
    for k, msg in zip(far_first(nplane), msgs):
        _, source = partner(me, k, nplane)
        for m in range(nlines):
            for q in range(P_SIZE):
                r_scr[m, pl.ds(source * P_SIZE + q, 1), :] = msg[pl.ds(m * P_SIZE + q, 1), :]
    eye = lax.broadcasted_iota(jnp.int32, (width, width), 0) == lax.broadcasted_iota(jnp.int32, (width, width), 1)

    def column(row):
        return jnp.sum(jnp.where(eye, row, 0.0), axis=1, keepdims=True)

    rows = [[r_scr[m, pl.ds(j, 1), :] for m in range(nlines)] for j in range(length)]
    scaled = [[None] * nlines for _ in range(length)]
    carry = [None] * nlines
    for j in range(length):
        for m in range(nlines):
            at = m * length + j
            if j == 0:
                carry[m] = rows[j][m]
            elif j % 2:
                carry[m] = column(rows[j][m]) - jnp.sum(low[at] * carry[m], axis=1, keepdims=True)
            else:
                carry[m] = rows[j][m] - jnp.sum(low[at] * carry[m], axis=0, keepdims=True)
            scaled[j][m] = jnp.sum(piv[at] * carry[m], axis=0 if j % 2 else 1, keepdims=True)
    after = [None] * nlines
    for j in reversed(range(length)):
        for m in range(nlines):
            at = m * length + j
            value = scaled[j][m]
            if j < length - 1:
                value = value - jnp.sum(fold[at] * after[m], axis=0 if j % 2 else 1, keepdims=True)
            after[m] = value
            row = value if j % 2 else jnp.sum(jnp.where(eye, value, 0.0), axis=0, keepdims=True)
            z_scr[m, pl.ds(j, 1), :] = row
    for k in range(nplane):
        to, _ = partner(me, k, nplane)
        for m in range(nlines):
            for q in range(P_SIZE):
                outs[k][pl.ds(m * P_SIZE + q, 1), :] = z_scr[m, pl.ds(to * P_SIZE + q, 1), :]


def faces_kernel(nplane, choose, *refs):
    solved, mine_ref = refs[:nplane], refs[-1]
    table = split(jnp.concatenate([s[...] for s in solved], axis=0), 3).astype(BF16)
    mine_ref[...] = jnp.dot(choose[...].astype(BF16), table, preferred_element_type=F32)


def repeat_faces(faces, pick, copies):
    table = split(jnp.concatenate([f[...] for f in faces], axis=0), 3).astype(BF16)
    picked = jnp.dot(pick[...], table, preferred_element_type=F32)
    return jnp.concatenate([picked] * copies, axis=1)


def add_products(work, x_scr, acc_scr, parts, seg, width):
    nfaces, area = acc_scr.shape
    chunk = x_scr.shape[1]
    copies, count = chunk // width, area // chunk
    lane = lax.broadcasted_iota(jnp.int32, (1, 128), 1)
    total = jnp.zeros((nfaces, 128), F32)
    done = 0
    for n, (places, fetch) in enumerate(work):
        if fetch is not None:
            fetch.wait()
        last = n == len(work) - 1
        for half in ((0, count // 2), (count // 2, count)):
            for v in range(0, chunk, 128):
                rows = range(done * nfaces, (done + len(places)) * nfaces, nfaces)
                xs = [x_scr[row : row + nfaces, v : v + 128] for row in rows]
                for c in range(*half):
                    at = c * chunk + v
                    value = acc_scr[:, at : at + 128] if n else None
                    for (ref, column), x in zip(places, xs):
                        term = ref[:, column + at : column + at + 128] * x
                        value = term if value is None else value + term
                    if not last:
                        acc_scr[:, at : at + 128] = value
                        continue
                    for n_part in range(3):
                        part = value.astype(BF16)
                        row = (3 * c + n_part) * nfaces
                        parts[row : row + nfaces, v : v + 128] = part
                        value = value - part.astype(F32)
            if last:
                base = 3 * half[0] * nfaces
                sums = jnp.dot(parts[base : 3 * half[1] * nfaces, :], seg[...], preferred_element_type=F32)
                for c in range(*half):
                    high, middle, low = [
                        sums[at : at + nfaces] for at in range(3 * c * nfaces - base, 3 * (c + 1) * nfaces - base, nfaces)
                    ]
                    total = total + jnp.where(lane // copies == c, high + (middle + low), 0.0)
        done += len(places)
    return total[:, :width]


def early_kernel(nblocks, blocks, pick, seg, *refs):
    faces, (sum_ref, held, buf, x_scr, acc_scr, parts, sems) = refs[:3], refs[3:]
    width = faces[0].shape[1]
    area = width * width
    early, late = early_blocks()

    def fetch(k, count, dst, column, n):
        start = pl.multiple_of(k * area, 128) if not isinstance(k, int) else k * area
        return pltpu.make_async_copy(
            blocks.at[:, pl.ds(start, count * area)], dst.at[:, pl.ds(column, count * area)], sems.at[n]
        )

    mine = [fetch(k, 1, buf, n * area, n) for n, k in enumerate((0, *early))]
    kept = [fetch(k, 1, held, n * area, 3 + n) for n, k in enumerate(late)]
    kept.append(fetch(5, nblocks - 5, held, 2 * area, 5))
    for copy in mine + kept:
        copy.start()
    x_scr[...] = repeat_faces(faces, pick, x_scr.shape[1] // width)
    work = [([(buf, n * area)], copy) for n, copy in enumerate(mine)]
    sum_ref[...] = add_products(work, x_scr, acc_scr, parts, seg, width)
    for copy in kept:
        copy.wait()


def early_again_kernel(pick, seg, first, *refs):
    faces, (sum_ref, x_scr, acc_scr, parts) = refs[:3], refs[3:]
    width = faces[0].shape[1]
    x_scr[...] = repeat_faces(faces, pick, x_scr.shape[1] // width)
    work = [([(first, column) for column in range(0, first.shape[1], width * width)], None)]
    sum_ref[...] = add_products(work, x_scr, acc_scr, parts, seg, width)


def late_kernel(nplane, last, *refs):
    (slot, held, pick, seg, early_sum), faces, refs = refs[:5], refs[5:10], refs[10:]
    nold = ITERS if last else 1
    olds, refs = refs[:nold], refs[nold:]
    next_ref, outs, (x_scr, acc_scr, parts, slot_scr, slot_sem) = refs[0], refs[1:-5], refs[-5:]
    nfaces, width = faces[0].shape
    area = width * width
    if not last:
        slots = pltpu.make_async_copy(slot, slot_scr, slot_sem)
        slots.start()
    x_scr[...] = repeat_faces(faces, pick, x_scr.shape[1] // width)
    work = [([(held, column) for column in range(0, held.shape[1], area)], None)]
    u_next = early_sum[...] + add_products(work, x_scr, acc_scr, parts, seg, width) - SHIFT * olds[-1][...]
    next_ref[...] = u_next
    if last:
        gram_ref = outs[0]
        lane = lax.broadcasted_iota(jnp.int32, gram_ref.shape, 1)
        basis = [old[...] for old in olds] + [u_next]
        gram, at = jnp.zeros(gram_ref.shape, F32), 0
        for i in range(ITERS + 1):
            for j in range(i, ITERS + 1):
                value = jnp.sum(jnp.sum(basis[i] * basis[j], axis=0, keepdims=True), axis=1, keepdims=True)
                gram, at = jnp.where(lane == at, value, gram), at + 1
        gram_ref[...] = gram
    else:
        per = nfaces // nplane
        me = lax.axis_index("plane")
        slots.wait()
        for k in range(nplane):
            to, _ = partner(me, k, nplane)
            for i in range(per):
                outs[k][pl.ds(i, 1), :] = next_ref[pl.ds(slot_scr[0, to * per + i], 1), :]


def finish_kernel(gram_ref, *refs):
    us, zs = refs[: ITERS + 1], refs[ITERS + 1 : 2 * ITERS + 1]
    sol_ref, res_ref, ok_ref = refs[2 * ITERS + 1 :]
    width = sol_ref.shape[1]
    rows = jnp.sum(gram_ref[...], axis=0, keepdims=True)
    lane = lax.broadcasted_iota(jnp.int32, rows.shape, 1)
    gram, at = {}, 0
    for i in range(ITERS + 1):
        for j in range(i, ITERS + 1):
            value = jnp.sum(jnp.where(lane == at, rows, 0.0), axis=1, keepdims=True)
            gram[i, j] = gram[j, i] = jnp.broadcast_to(value, rows.shape)
            at += 1
    largest = functools.reduce(jnp.maximum, [jnp.abs(g) for g in gram.values()])
    ok = largest < 1e30
    beta = jnp.sqrt(gram[0, 0] + EPS)
    basis = [[1.0 / beta]]
    hmat = {}
    for step in range(ITERS):
        own = basis[step]
        wvec = [SHIFT * own[0]] + [own[i] + SHIFT * own[i + 1] for i in range(step)] + [own[step]]
        images = [sum(gram[i, j] * wvec[j] for j in range(step + 2)) for i in range(step + 1)]
        for i in range(step + 1):
            hmat[i, step] = sum(basis[i][m] * images[m] for m in range(i + 1))
        for i in range(step + 1):
            for m in range(i + 1):
                wvec[m] = wvec[m] - hmat[i, step] * basis[i][m]
        terms = [wvec[i] * wvec[j] * gram[i, j] for i in range(step + 2) for j in range(step + 2)]
        square = jnp.maximum(sum(terms), 0.0)
        ok = ok & (square + EPS >= 2e-3 * sum(jnp.abs(term) for term in terms))
        hmat[step + 1, step] = jnp.sqrt(square + EPS)
        scale = 1.0 / hmat[step + 1, step]
        basis.append([w * scale for w in wvec])
    normal = {
        (i, j): sum(hmat[m, i] * hmat[m, j] for m in range(j + 2) if (m, i) in hmat and (m, j) in hmat)
        for i in range(ITERS)
        for j in range(i + 1)
    }
    factor, inverse = {}, []
    for j in range(ITERS):
        diag = jnp.sqrt(normal[j, j] - sum(factor[j, m] * factor[j, m] for m in range(j)))
        inverse.append(1.0 / diag)
        for i in range(j + 1, ITERS):
            factor[i, j] = (normal[i, j] - sum(factor[i, m] * factor[j, m] for m in range(j))) * inverse[j]
    forward = []
    for i in range(ITERS):
        forward.append((beta * hmat[0, i] - sum(factor[i, m] * forward[m] for m in range(i))) * inverse[i])
    coef = [None] * ITERS
    for i in reversed(range(ITERS)):
        coef[i] = (forward[i] - sum(factor[m, i] * coef[m] for m in range(i + 1, ITERS))) * inverse[i]
    mix = [sum(coef[s] * basis[s][m] for s in range(m, ITERS))[:, :width] for m in range(ITERS)]
    sol_ref[...] = sum(mix[m] * zs[m][...] for m in range(ITERS))
    image = sum(mix[m] * (us[m + 1][...] + SHIFT * us[m][...]) for m in range(ITERS))
    res_ref[...] = us[0][...] - image
    ok = ok & (functools.reduce(jnp.maximum, [jnp.abs(c) for c in coef]) < 1e30)
    ok_ref[...] = jnp.where(ok, 1.0, 0.0)


def call(kernel, args, outs, spaces=None, scratch=(), flops=0, pinned=True, ready=True):
    spaces = [pltpu.VMEM] * len(args) if spaces is None else spaces
    if ready:
        args = [pltpu.with_memory_space_constraint(x, s) if s is pltpu.VMEM else x for x, s in zip(args, spaces)]
    size = sum(x.dtype.itemsize * math.prod(x.shape) for x in args)
    return pl.pallas_call(
        kernel,
        out_shape=[pltpu.VMEM(shape, F32) if pinned else jax.ShapeDtypeStruct(shape, F32) for shape in outs],
        in_specs=[pl.BlockSpec(memory_space=s) for s in spaces],
        out_specs=[pl.BlockSpec(memory_space=pltpu.VMEM) for _ in outs],
        scratch_shapes=scratch,
        compiler_params=pltpu.CompilerParams(vmem_limit_bytes=VMEM_LIMIT),
        cost_estimate=pl.CostEstimate(flops=flops, bytes_accessed=size, transcendentals=0),
    )(*args)


def add_up(x):
    count = lax.axis_size("span") * lax.axis_size("plane")
    rows = jnp.broadcast_to(x, (count, x.shape[1]))
    return lax.all_to_all(rows, ("span", "plane"), split_axis=0, concat_axis=0, tiled=True)


def pairings(size):
    if size % 2:
        return [(i, (i + 1) % size) for i in range(size)], [(i, (i - 1) % size) for i in range(size)]
    return [(i, i ^ 1) for i in range(size)], [(i, (i + 1 if i % 2 else i - 1) % size) for i in range(size)]


def on_device(rhs, blocks, columns, line_slot, line_lower, line_upper, pivot_inv):
    width, nfaces = rhs.shape
    nblocks = columns.shape[0]
    nspan, nplane = lax.axis_size("span"), lax.axis_size("plane")
    owned = nfaces // P_SIZE // nplane
    length = P_SIZE * nplane
    per = owned * P_SIZE
    area = width * width
    shape = (nfaces, width)
    span_pairs, span_others = pairings(nspan)
    plane_pairs, plane_others = pairings(nplane)

    u_first, choose, *send = call(
        functools.partial(start_kernel, nplane),
        [line_slot, rhs.T],
        [shape, (nfaces, 3 * nfaces)] + [(per, width)] * nplane,
        [pltpu.SMEM, pltpu.VMEM],
        ready=False,
    )
    us = [u_first]
    zs = []
    picks = held = first = None
    for step in range(ITERS):
        flat = pltpu.VMEM((nfaces, area), F32)
        squares = [(nfaces * width, width)] * 3
        if step == 0:
            factors = call(
                functools.partial(first_squares_kernel, length),
                [line_lower, pivot_inv, line_upper, us[-1]],
                squares,
                [pl.ANY] * 4,
                [flat] * 3 + [pltpu.VMEM(squares[0], F32), pltpu.SemaphoreType.DMA((3,))],
                flops=nfaces * area * width,
            )
        else:
            factors = call(
                functools.partial(next_squares_kernel, length),
                [line_lower, pivot_inv, fold, us[-1]],
                squares,
                [pl.ANY] * 4,
                [flat] * 2 + [pltpu.SemaphoreType.DMA((3,))],
                flops=nfaces * area,
            )
        shaped = [x.reshape(nfaces, width, width) for x in factors]
        got = [exchange(send[k], "plane", k) if k else send[0] for k in far_first(nplane)]
        solved = call(
            functools.partial(line_kernel, nplane, owned),
            [*got, *shaped],
            [(per, width)] * nplane,
            scratch=[pltpu.VMEM((owned, length, width), F32)] * 2,
            flops=6 * nfaces * area,
        )
        if step == 0:
            *picks, fold = pl.pallas_call(
                functools.partial(pick_kernel, nspan, nplane, width),
                out_shape=[
                    pltpu.VMEM((3 * nfaces, 9 * nfaces), BF16),
                    pltpu.VMEM(((nblocks - 3) * nfaces, 15 * nfaces), BF16),
                    pltpu.VMEM((math.lcm(width, 128), 128), BF16),
                    pltpu.HBM(squares[0], F32),
                ],
                in_specs=[pl.BlockSpec(memory_space=pltpu.VMEM)] * 2,
                out_specs=[pl.BlockSpec(memory_space=pltpu.VMEM)] * 3 + [pl.BlockSpec(memory_space=pl.ANY)],
                scratch_shapes=[pltpu.SemaphoreType.DMA],
                compiler_params=pltpu.CompilerParams(vmem_limit_bytes=VMEM_LIMIT),
                cost_estimate=pl.CostEstimate(flops=0, bytes_accessed=4 * nfaces * area, transcendentals=0),
            )(
                lax.optimization_barrier((columns, solved[0]))[0],
                pltpu.with_memory_space_constraint(factors[2], pltpu.VMEM),
            )
        pieces = [exchange(solved[k], "plane", k) if k else solved[0] for k in far_first(nplane)]
        args = [choose, *pieces, *(picks if step == 0 else ())]
        spaces = [pltpu.VMEM] * (nplane + 1) + [pl.ANY] * (len(args) - nplane - 1)
        (mine,) = call(functools.partial(faces_kernel, nplane), args, [shape], spaces)
        zs.append(mine)
        other = lax.ppermute(mine, "span", span_others)
        near = [mine, lax.ppermute(mine, "span", span_pairs), lax.ppermute(mine, "plane", plane_pairs)]
        far = [other, lax.ppermute(mine, "plane", plane_others)]
        chunk = math.lcm(width, 128)

        def scratch(count):
            return [
                pltpu.VMEM((count * nfaces, chunk), F32),
                pltpu.VMEM((nfaces, area), F32),
                pltpu.VMEM((3 * nfaces * area // chunk, chunk), BF16),
            ]

        if step == 0:
            early_sum, held, first = call(
                functools.partial(early_kernel, nblocks),
                [blocks, picks[0], picks[2], *near],
                [shape, (nfaces, (nblocks - 3) * area), (nfaces, 3 * area)],
                [pl.ANY] + [pltpu.VMEM] * 5,
                scratch(3) + [pltpu.SemaphoreType.DMA((6,))],
                flops=6 * nfaces * area,
            )
        else:
            (early_sum,) = call(
                early_again_kernel, [picks[0], picks[2], first, *near], [shape], scratch=scratch(3), flops=6 * nfaces * area
            )
        last = step == ITERS - 1
        args = [line_slot, held, picks[1], picks[2], early_sum, *near, *far, *(us if last else us[-1:])]
        out = call(
            functools.partial(late_kernel, nplane, last),
            args,
            [shape] + ([(1, 128)] if last else [(per, width)] * nplane),
            [pl.ANY] + [pltpu.VMEM] * (len(args) - 1),
            scratch(nblocks - 3) + [pltpu.SMEM(line_slot.shape, jnp.int32), pltpu.SemaphoreType.DMA],
            flops=2 * nblocks * nfaces * area,
        )
        us.append(out[0])
        send = out[1:]
    gram = add_up(send[0])
    sol, res, ok = call(finish_kernel, [gram, *us, *zs], [shape, shape, (1, 128)], pinned=False)
    given = (rhs, blocks, columns, line_slot, line_lower, line_upper, pivot_inv)
    _, sol, res = lax.while_loop(
        lambda state: state[0], lambda _: (jnp.array(False), *step_by_step(*given)), (ok[0, 0] < 0.5, sol.T, res.T)
    )
    return sol, res


def solution(mesh):
    both = ("span", "plane")
    return jax.shard_map(
        on_device,
        mesh=mesh,
        in_specs=(
            P(None, both),
            P(both, None),
            P(None, both),
            P(both, None),
            P(both, None),
            P(both, None),
            P(both, None),
        ),
        out_specs=(P(None, both), P(None, both)),
        check_vma=False,
    )
```

```python
import functools
import math

import jax
import jax.numpy as jnp
import numpy as np
from jax import lax
from jax.experimental import pallas as pl
from jax.experimental.pallas import tpu as pltpu
from jax.sharding import PartitionSpec as P

ITERS = 3
P_SIZE = 2
SHIFT = 2.0
EPS = 1e-6
VMEM_LIMIT = 16 * 1024 * 1024
HIGH = lax.Precision.HIGHEST
F32, BF16 = jnp.float32, jnp.bfloat16


def with_halo(x, sides, width, wrap):
    for axis, dim in sides:
        size, length = (lax.axis_size(axis), x.shape[dim])
        up = [(i, (i + 1) % size) for i in range(size if wrap else size - 1)]
        down = [(j, i) for i, j in up]
        last = lax.slice_in_dim(x, length - width, length, axis=dim)
        first = lax.slice_in_dim(x, 0, width, axis=dim)
        before = lax.ppermute(last, axis, up)
        after = lax.ppermute(first, axis, down)
        x = jnp.concatenate([before, x, after], axis=dim)
    return x


def small_solve(factor, target):
    extent = target.shape[0]
    forward_vals = []
    for row in range(extent):
        running = target[row]
        for inner in range(row):
            running = running - factor[row, inner] * forward_vals[inner]
        forward_vals.append(running / factor[row, row])
    backward_vals = [None] * extent
    for row in reversed(range(extent)):
        running = forward_vals[row]
        for inner in range(row + 1, extent):
            running = running - factor[inner, row] * backward_vals[inner]
        backward_vals[row] = running / factor[row, row]
    return jnp.stack(backward_vals)


def to_sequence(factor_rows, nlines, length, width):
    return jnp.swapaxes(factor_rows.reshape(nlines, length, width, width), 0, 1)


def line_solve(rhs_lines, lseq, useq, pseq):
    rseq = jnp.moveaxis(rhs_lines, 2, 0)

    def forward(prev, items):
        right, low = items
        cur = right - jnp.einsum("mab,bm->am", low, prev, precision=HIGH)
        return (cur, cur)

    start = jnp.zeros(rseq.shape[1:], F32)
    _, yseq = lax.scan(forward, start, (rseq, lseq))

    def backward(nxt, items):
        yval, upp, piv = items
        inner = yval - jnp.einsum("mab,bm->am", upp, nxt, precision=HIGH)
        cur = jnp.einsum("mab,bm->am", piv, inner, precision=HIGH)
        return (cur, cur)

    _, zseq = lax.scan(backward, start, (yseq, useq, pseq), reverse=True)
    return jnp.moveaxis(zseq, 0, 2)


def table_positions(columns, nfaces, my_span, my_plane, nspan, nplane):
    device_of = columns // nfaces
    span_of = device_of // nplane
    plane_of = device_of % nplane
    dspan = (span_of - my_span + 1 + nspan) % nspan - 1
    dplane = plane_of - my_plane
    selector = jnp.where(
        dspan == -1,
        1,
        jnp.where(dspan == 1, 2, jnp.where(dplane == -1, 3, jnp.where(dplane == 1, 4, 0))),
    )
    return selector * nfaces + columns % nfaces


def step_by_step(rhs, blocks, columns, line_slot, line_lower, line_upper, pivot_inv):
    width, nfaces = rhs.shape
    nblocks = columns.shape[0]
    nplane = lax.axis_size("plane")
    position = table_positions(
        columns, nfaces, lax.axis_index("span"), lax.axis_index("plane"), lax.axis_size("span"), nplane
    )
    slot = line_slot[0]
    lines_group = nfaces // P_SIZE
    owned = lines_group // nplane
    length = P_SIZE * nplane
    lower = to_sequence(line_lower, owned, length, width)
    upper = to_sequence(line_upper, owned, length, width)
    pivot = to_sequence(pivot_inv, owned, length, width)
    shaped_blocks = blocks.reshape(nfaces, nblocks, width, width)

    def apply_a(vec):
        shaped = vec.reshape(width, 1, 1, nfaces)
        span_side = with_halo(shaped, (("span", 1),), 1, True)
        plane_side = with_halo(shaped, (("plane", 2),), 1, False)
        below = plane_side[:, 0, 0]
        above = plane_side[:, 0, 2]
        table = jnp.concatenate([vec, span_side[:, 0, 0], span_side[:, 2, 0], below, above], axis=1)
        return jnp.einsum("ikab,bki->ai", shaped_blocks, table[:, position], precision=HIGH)

    def apply_m(vec):
        pieces = vec[:, slot].reshape(width, lines_group, P_SIZE)
        whole = lax.all_to_all(pieces, "plane", split_axis=1, concat_axis=2, tiled=True)
        solved = line_solve(whole, lower, upper, pivot)
        back = lax.all_to_all(solved, "plane", split_axis=2, concat_axis=1, tiled=True)
        return jnp.zeros_like(vec).at[:, slot].set(back.reshape(width, nfaces))

    beta = jnp.sqrt(lax.psum(jnp.sum(rhs * rhs), ("span", "plane")) + EPS)
    basis = [rhs / beta]
    hcols = []
    for step in range(ITERS):
        wvec = apply_a(apply_m(basis[step]))
        stacked = jnp.stack(basis)
        hvals = lax.psum(jnp.einsum("jai,ai->j", stacked, wvec, precision=HIGH), ("span", "plane"))
        wvec = wvec - jnp.einsum("j,jai->ai", hvals, stacked, precision=HIGH)
        hnext = jnp.sqrt(lax.psum(jnp.sum(wvec * wvec), ("span", "plane")) + EPS)
        basis.append(wvec / hnext)
        hcols.append(jnp.concatenate([hvals, hnext[None], jnp.zeros((ITERS - step - 1,), F32)]))
    hmat = jnp.stack(hcols, axis=1)
    factor = jnp.linalg.cholesky(jnp.dot(hmat.T, hmat, precision=HIGH))
    coef = small_solve(factor, beta * hmat[0])
    update = jnp.einsum("j,jai->ai", coef, jnp.stack(basis[:ITERS]), precision=HIGH)
    solution = apply_m(update)
    return solution, rhs - apply_a(solution)


def partner(me, k, size):
    if size & (size - 1) == 0:
        return me ^ k, me ^ k
    return (me + k) % size, (me + size - k) % size


def far_first(size):
    return list(reversed(range(size)))


def exchange(x, axis, k):
    size = lax.axis_size(axis)
    return lax.ppermute(x, axis, [(i, partner(i, k, size)[0]) for i in range(size)])


def split(x, parts):
    out = []
    for _ in range(parts):
        out.append(x.astype(BF16).astype(F32))
        x = x - out[-1]
    return jnp.concatenate(out, axis=0)


def start_kernel(nplane, slot_ref, u_ref, copy_ref, choose_ref, *outs):
    nfaces = u_ref.shape[0]
    per = nfaces // nplane
    me = lax.axis_index("plane")
    for k in range(nplane):
        to, _ = partner(me, k, nplane)
        for i in range(per):
            outs[k][pl.ds(i, 1), :] = u_ref[pl.ds(slot_ref[0, to * per + i], 1), :]
    copy_ref[...] = u_ref[...]
    face = lax.broadcasted_iota(jnp.int32, choose_ref.shape, 0)
    piece = lax.broadcasted_iota(jnp.int32, choose_ref.shape, 1) % nfaces
    choose = jnp.zeros(choose_ref.shape, F32)
    for n, k in enumerate(far_first(nplane)):
        _, source = partner(me, k, nplane)
        for i in range(per):
            hit = (face == slot_ref[0, source * per + i]) & (piece == n * per + i)
            choose = jnp.where(hit, 1.0, choose)
    choose_ref[...] = choose


def to_squares(src, dst):
    nrows, width = src.shape[0], dst.shape[1]
    chunk = math.lcm(width, 128)
    for c in range(width * width // chunk):
        piece = src[:, c * chunk : (c + 1) * chunk]
        for r in range(chunk // width):
            a = c * (chunk // width) + r
            dst[pl.ds(a, nrows, stride=width), :] = piece[:, r * width : (r + 1) * width]


def turn_some(squares, length, parity):
    width = squares.shape[1]
    for at in range(squares.shape[0] // width):
        if at % length % 2 == parity and at % length:
            here = slice(at * width, (at + 1) * width)
            squares[here, :] = squares[here, :].T


def first_squares_kernel(length, low, piv, upp, _, low_out, piv_out, fold_out, low_scr, piv_scr, upp_scr, upp_sq, sems):
    width = low_out.shape[1]
    fetches = []
    for n, (src, scr) in enumerate(((low, low_scr), (piv, piv_scr), (upp, upp_scr))):
        fetches.append(pltpu.make_async_copy(src, scr, sems.at[n]))
        fetches[-1].start()
    for fetch, scr, dst in zip(fetches, (low_scr, piv_scr, upp_scr), (low_out, piv_out, upp_sq)):
        fetch.wait()
        to_squares(scr, dst)
    for at in range(low.shape[0]):
        here = slice(at * width, (at + 1) * width)
        if at % length == length - 1:
            fold_out[here, :] = jnp.zeros((width, width), F32)
            continue
        (ph, pl_), (uh, ul) = [
            (x.astype(BF16), (x - x.astype(BF16).astype(F32)).astype(BF16)) for x in (piv_out[here, :], upp_sq[here, :])
        ]
        fold = sum(jnp.dot(x, y, preferred_element_type=F32) for x, y in ((pl_, uh), (ph, ul), (ph, uh)))
        fold_out[here, :] = fold.T if at % length % 2 else fold
    turn_some(low_out, length, 0)
    turn_some(piv_out, length, 1)


def next_squares_kernel(length, low, piv, fold, _, low_out, piv_out, fold_out, low_scr, piv_scr, sems):
    fetches = []
    for n, (src, scr) in enumerate(((low, low_scr), (piv, piv_scr), (fold, fold_out))):
        fetches.append(pltpu.make_async_copy(src, scr, sems.at[n]))
        fetches[-1].start()
    for fetch, scr, dst, parity in zip(fetches, (low_scr, piv_scr), (low_out, piv_out), (0, 1)):
        fetch.wait()
        to_squares(scr, dst)
        turn_some(dst, length, parity)
    fetches[2].wait()


def parities():
    return [1 if lax.axis_size(a) % 2 else lax.axis_index(a) % 2 for a in ("span", "plane")]


def pick_kernel(nspan, nplane, width, columns_ref, fold_ref, pick_ref, seg_ref, store_ref, sem):
    store = pltpu.make_async_copy(fold_ref, store_ref, sem)
    store.start()
    copies = seg_ref.shape[0] // width
    lane = lax.broadcasted_iota(jnp.int32, (width, 128), 1) % copies
    for r in range(copies):
        seg_ref[r * width : (r + 1) * width, :] = jnp.where(lane == r, 1.0, 0.0).astype(BF16)
    nblocks, nfaces = columns_ref.shape
    span, plane = lax.axis_index("span"), lax.axis_index("plane")
    position = table_positions(columns_ref[...], nfaces, span, plane, nspan, nplane)
    selector, face = position // nfaces, position % nfaces
    span_odd, plane_odd = [parity == 1 for parity in parities()]
    of_span = jnp.where((selector == 1) == span_odd, 1, 3)
    of_plane = jnp.where((selector == 3) == plane_odd, 2, 4)
    group = jnp.where(selector == 0, 0, jnp.where(selector <= 2, of_span, of_plane))
    at = (group * nfaces + face).astype(F32)
    eye = lax.broadcasted_iota(jnp.int32, (nfaces, nfaces), 0) == lax.broadcasted_iota(jnp.int32, (nfaces, nfaces), 1)
    lane = lax.broadcasted_iota(jnp.int32, (nfaces, pick_ref.shape[1]), 1) % (pick_ref.shape[1] // 3)
    for k in range(nblocks):
        column = jnp.sum(jnp.where(eye, at[k : k + 1], 0.0), axis=1, keepdims=True).astype(jnp.int32)
        pick_ref[k * nfaces : (k + 1) * nfaces, :] = jnp.where(lane == column, 1.0, 0.0).astype(BF16)
    store.wait()


def line_kernel(nplane, nlines, *refs):
    msgs, (low, piv, fold), outs, (r_scr, z_scr) = refs[:nplane], refs[nplane:-nplane-2], refs[-nplane-2:-2], refs[-2:]
    _, length, width = r_scr.shape
    me = lax.axis_index("plane")
    for k, msg in zip(far_first(nplane), msgs):
        _, source = partner(me, k, nplane)
        for m in range(nlines):
            for q in range(P_SIZE):
                r_scr[m, pl.ds(source * P_SIZE + q, 1), :] = msg[pl.ds(m * P_SIZE + q, 1), :]
    eye = lax.broadcasted_iota(jnp.int32, (width, width), 0) == lax.broadcasted_iota(jnp.int32, (width, width), 1)

    def column(row):
        return jnp.sum(jnp.where(eye, row, 0.0), axis=1, keepdims=True)

    rows = [[r_scr[m, pl.ds(j, 1), :] for m in range(nlines)] for j in range(length)]
    scaled = [[None] * nlines for _ in range(length)]
    carry = [None] * nlines
    for j in range(length):
        for m in range(nlines):
            at = m * length + j
            if j == 0:
                carry[m] = rows[j][m]
            elif j % 2:
                carry[m] = column(rows[j][m]) - jnp.sum(low[at] * carry[m], axis=1, keepdims=True)
            else:
                carry[m] = rows[j][m] - jnp.sum(low[at] * carry[m], axis=0, keepdims=True)
            scaled[j][m] = jnp.sum(piv[at] * carry[m], axis=0 if j % 2 else 1, keepdims=True)
    after = [None] * nlines
    for j in reversed(range(length)):
        for m in range(nlines):
            at = m * length + j
            value = scaled[j][m]
            if j < length - 1:
                value = value - jnp.sum(fold[at] * after[m], axis=0 if j % 2 else 1, keepdims=True)
            after[m] = value
            row = value if j % 2 else jnp.sum(jnp.where(eye, value, 0.0), axis=0, keepdims=True)
            z_scr[m, pl.ds(j, 1), :] = row
    for k in range(nplane):
        to, _ = partner(me, k, nplane)
        for m in range(nlines):
            for q in range(P_SIZE):
                outs[k][pl.ds(m * P_SIZE + q, 1), :] = z_scr[m, pl.ds(to * P_SIZE + q, 1), :]


def faces_kernel(nplane, choose, *refs):
    solved, mine_ref = refs[:nplane], refs[-1]
    table = split(jnp.concatenate([s[...] for s in solved], axis=0), 3).astype(BF16)
    mine_ref[...] = jnp.dot(choose[...].astype(BF16), table, preferred_element_type=F32)


def repeat_faces(faces, pick, copies):
    table = split(jnp.concatenate([f[...] for f in faces], axis=0), 3).astype(BF16)
    picked = jnp.dot(pick[...], table, preferred_element_type=F32)
    return jnp.concatenate([picked] * copies, axis=1)


def add_products(work, x_scr, acc_scr, parts, seg, width):
    nfaces, area = acc_scr.shape
    chunk = x_scr.shape[1]
    copies, count = chunk // width, area // chunk
    lane = lax.broadcasted_iota(jnp.int32, (1, 128), 1)
    total = jnp.zeros((nfaces, 128), F32)
    done = 0
    for n, (places, fetch) in enumerate(work):
        if fetch is not None:
            fetch.wait()
        last = n == len(work) - 1
        for half in ((0, count // 2), (count // 2, count)):
            for v in range(0, chunk, 128):
                rows = range(done * nfaces, (done + len(places)) * nfaces, nfaces)
                xs = [x_scr[row : row + nfaces, v : v + 128] for row in rows]
                for c in range(*half):
                    at = c * chunk + v
                    value = acc_scr[:, at : at + 128] if n else None
                    for (ref, column), x in zip(places, xs):
                        term = ref[:, column + at : column + at + 128] * x
                        value = term if value is None else value + term
                    if not last:
                        acc_scr[:, at : at + 128] = value
                        continue
                    for n_part in range(3):
                        part = value.astype(BF16)
                        row = (3 * c + n_part) * nfaces
                        parts[row : row + nfaces, v : v + 128] = part
                        value = value - part.astype(F32)
            if last:
                base = 3 * half[0] * nfaces
                sums = jnp.dot(parts[base : 3 * half[1] * nfaces, :], seg[...], preferred_element_type=F32)
                for c in range(*half):
                    high, middle, low = [
                        sums[at : at + nfaces] for at in range(3 * c * nfaces - base, 3 * (c + 1) * nfaces - base, nfaces)
                    ]
                    total = total + jnp.where(lane // copies == c, high + (middle + low), 0.0)
        done += len(places)
    return total[:, :width]


def hold_kernel(blocks, _, held, sem):
    fetch = pltpu.make_async_copy(blocks, held, sem)
    fetch.start()
    fetch.wait()


def late_kernel(nplane, last, *refs):
    (slot, other, plane_other, pair, plane_pair, held, pick, seg, mine), refs = refs[:9], refs[9:]
    faces = (mine, pair, plane_pair, other, plane_other)
    nold = ITERS if last else 1
    olds, refs = refs[:nold], refs[nold:]
    next_ref, outs, (x_scr, acc_scr, parts, slot_scr, slot_sem) = refs[0], refs[1:-5], refs[-5:]
    nfaces, width = faces[0].shape
    area = width * width
    if not last:
        slots = pltpu.make_async_copy(slot, slot_scr, slot_sem)
        slots.start()
    x_scr[...] = repeat_faces(faces, pick, x_scr.shape[1] // width)
    work = [([(held, column) for column in range(0, held.shape[1], area)], None)]
    u_next = add_products(work, x_scr, acc_scr, parts, seg, width) - SHIFT * olds[-1][...]
    next_ref[...] = u_next
    if last:
        gram_ref = outs[0]
        lane = lax.broadcasted_iota(jnp.int32, gram_ref.shape, 1)
        basis = [old[...] for old in olds] + [u_next]
        gram, at = jnp.zeros(gram_ref.shape, F32), 0
        for i in range(ITERS + 1):
            for j in range(i, ITERS + 1):
                value = jnp.sum(jnp.sum(basis[i] * basis[j], axis=0, keepdims=True), axis=1, keepdims=True)
                gram, at = jnp.where(lane == at, value, gram), at + 1
        gram_ref[...] = gram
    else:
        per = nfaces // nplane
        me = lax.axis_index("plane")
        slots.wait()
        for k in range(nplane):
            to, _ = partner(me, k, nplane)
            for i in range(per):
                outs[k][pl.ds(i, 1), :] = next_ref[pl.ds(slot_scr[0, to * per + i], 1), :]


def finish_kernel(gram_ref, *refs):
    us, zs = refs[: ITERS + 1], refs[ITERS + 1 : 2 * ITERS + 1]
    sol_ref, res_ref, ok_ref = refs[2 * ITERS + 1 :]
    width = sol_ref.shape[1]
    rows = jnp.sum(gram_ref[...], axis=0, keepdims=True)
    lane = lax.broadcasted_iota(jnp.int32, rows.shape, 1)
    gram, at = {}, 0
    for i in range(ITERS + 1):
        for j in range(i, ITERS + 1):
            value = jnp.sum(jnp.where(lane == at, rows, 0.0), axis=1, keepdims=True)
            gram[i, j] = gram[j, i] = jnp.broadcast_to(value, rows.shape)
            at += 1
    largest = functools.reduce(jnp.maximum, [jnp.abs(g) for g in gram.values()])
    ok = largest < 1e30
    beta = jnp.sqrt(gram[0, 0] + EPS)
    basis = [[1.0 / beta]]
    hmat = {}
    for step in range(ITERS):
        own = basis[step]
        wvec = [SHIFT * own[0]] + [own[i] + SHIFT * own[i + 1] for i in range(step)] + [own[step]]
        images = [sum(gram[i, j] * wvec[j] for j in range(step + 2)) for i in range(step + 1)]
        for i in range(step + 1):
            hmat[i, step] = sum(basis[i][m] * images[m] for m in range(i + 1))
        for i in range(step + 1):
            for m in range(i + 1):
                wvec[m] = wvec[m] - hmat[i, step] * basis[i][m]
        terms = [wvec[i] * wvec[j] * gram[i, j] for i in range(step + 2) for j in range(step + 2)]
        square = jnp.maximum(sum(terms), 0.0)
        ok = ok & (square + EPS >= 2e-3 * sum(jnp.abs(term) for term in terms))
        hmat[step + 1, step] = jnp.sqrt(square + EPS)
        scale = 1.0 / hmat[step + 1, step]
        basis.append([w * scale for w in wvec])
    normal = {
        (i, j): sum(hmat[m, i] * hmat[m, j] for m in range(j + 2) if (m, i) in hmat and (m, j) in hmat)
        for i in range(ITERS)
        for j in range(i + 1)
    }
    factor, inverse = {}, []
    for j in range(ITERS):
        diag = jnp.sqrt(normal[j, j] - sum(factor[j, m] * factor[j, m] for m in range(j)))
        inverse.append(1.0 / diag)
        for i in range(j + 1, ITERS):
            factor[i, j] = (normal[i, j] - sum(factor[i, m] * factor[j, m] for m in range(j))) * inverse[j]
    forward = []
    for i in range(ITERS):
        forward.append((beta * hmat[0, i] - sum(factor[i, m] * forward[m] for m in range(i))) * inverse[i])
    coef = [None] * ITERS
    for i in reversed(range(ITERS)):
        coef[i] = (forward[i] - sum(factor[m, i] * coef[m] for m in range(i + 1, ITERS))) * inverse[i]
    mix = [sum(coef[s] * basis[s][m] for s in range(m, ITERS))[:, :width] for m in range(ITERS)]
    sol_ref[...] = sum(mix[m] * zs[m][...] for m in range(ITERS))
    image = sum(mix[m] * (us[m + 1][...] + SHIFT * us[m][...]) for m in range(ITERS))
    res_ref[...] = us[0][...] - image
    ok = ok & (functools.reduce(jnp.maximum, [jnp.abs(c) for c in coef]) < 1e30)
    ok_ref[...] = jnp.where(ok, 1.0, 0.0)


def call(kernel, args, outs, spaces=None, scratch=(), flops=0, pinned=True, ready=True):
    spaces = [pltpu.VMEM] * len(args) if spaces is None else spaces
    if ready:
        args = [pltpu.with_memory_space_constraint(x, s) if s is pltpu.VMEM else x for x, s in zip(args, spaces)]
    size = sum(x.dtype.itemsize * math.prod(x.shape) for x in args)
    return pl.pallas_call(
        kernel,
        out_shape=[pltpu.VMEM(shape, F32) if pinned else jax.ShapeDtypeStruct(shape, F32) for shape in outs],
        in_specs=[pl.BlockSpec(memory_space=s) for s in spaces],
        out_specs=[pl.BlockSpec(memory_space=pltpu.VMEM) for _ in outs],
        scratch_shapes=scratch,
        compiler_params=pltpu.CompilerParams(vmem_limit_bytes=VMEM_LIMIT),
        cost_estimate=pl.CostEstimate(flops=flops, bytes_accessed=size, transcendentals=0),
    )(*args)


def add_up(x):
    count = lax.axis_size("span") * lax.axis_size("plane")
    rows = jnp.broadcast_to(x, (count, x.shape[1]))
    return lax.all_to_all(rows, ("span", "plane"), split_axis=0, concat_axis=0, tiled=True)


def pairings(size):
    if size % 2:
        return [(i, (i + 1) % size) for i in range(size)], [(i, (i - 1) % size) for i in range(size)]
    return [(i, i ^ 1) for i in range(size)], [(i, (i + 1 if i % 2 else i - 1) % size) for i in range(size)]


def on_device(rhs, blocks, columns, line_slot, line_lower, line_upper, pivot_inv):
    width, nfaces = rhs.shape
    nblocks = columns.shape[0]
    nspan, nplane = lax.axis_size("span"), lax.axis_size("plane")
    owned = nfaces // P_SIZE // nplane
    length = P_SIZE * nplane
    per = owned * P_SIZE
    area = width * width
    shape = (nfaces, width)
    span_pairs, span_others = pairings(nspan)
    plane_pairs, plane_others = pairings(nplane)

    u_first, choose, *send = call(
        functools.partial(start_kernel, nplane),
        [line_slot, rhs.T],
        [shape, (nfaces, 3 * nfaces)] + [(per, width)] * nplane,
        [pltpu.SMEM, pltpu.VMEM],
        ready=False,
    )
    us = [u_first]
    zs = []
    picks = held = None
    for step in range(ITERS):
        flat = pltpu.VMEM((nfaces, area), F32)
        squares = [(nfaces * width, width)] * 3
        if step == 0:
            factors = call(
                functools.partial(first_squares_kernel, length),
                [line_lower, pivot_inv, line_upper, us[-1]],
                squares,
                [pl.ANY] * 4,
                [flat] * 3 + [pltpu.VMEM(squares[0], F32), pltpu.SemaphoreType.DMA((3,))],
                flops=nfaces * area * width,
            )
        else:
            factors = call(
                functools.partial(next_squares_kernel, length),
                [line_lower, pivot_inv, fold, us[-1]],
                squares,
                [pl.ANY] * 4,
                [flat] * 2 + [pltpu.SemaphoreType.DMA((3,))],
                flops=nfaces * area,
            )
        shaped = [x.reshape(nfaces, width, width) for x in factors]
        got = [exchange(send[k], "plane", k) if k else send[0] for k in far_first(nplane)]
        solved = call(
            functools.partial(line_kernel, nplane, owned),
            [*got, *shaped],
            [(per, width)] * nplane,
            scratch=[pltpu.VMEM((owned, length, width), F32)] * 2,
            flops=6 * nfaces * area,
        )
        if step == 0:
            *picks, fold = pl.pallas_call(
                functools.partial(pick_kernel, nspan, nplane, width),
                out_shape=[
                    pltpu.VMEM((nblocks * nfaces, 15 * nfaces), BF16),
                    pltpu.VMEM((math.lcm(width, 128), 128), BF16),
                    pltpu.HBM(squares[0], F32),
                ],
                in_specs=[pl.BlockSpec(memory_space=pltpu.VMEM)] * 2,
                out_specs=[pl.BlockSpec(memory_space=pltpu.VMEM)] * 2 + [pl.BlockSpec(memory_space=pl.ANY)],
                scratch_shapes=[pltpu.SemaphoreType.DMA],
                compiler_params=pltpu.CompilerParams(vmem_limit_bytes=VMEM_LIMIT),
                cost_estimate=pl.CostEstimate(flops=0, bytes_accessed=4 * nfaces * area, transcendentals=0),
            )(
                lax.optimization_barrier((columns, solved[0]))[0],
                pltpu.with_memory_space_constraint(factors[2], pltpu.VMEM),
            )
        pieces = [exchange(solved[k], "plane", k) if k else solved[0] for k in far_first(nplane)]
        args = [choose, *pieces, *(picks if step == 0 else ())]
        spaces = [pltpu.VMEM] * (nplane + 1) + [pl.ANY] * (len(args) - nplane - 1)
        (mine,) = call(functools.partial(faces_kernel, nplane), args, [shape], spaces)
        zs.append(mine)
        other = lax.ppermute(mine, "span", span_others)
        pair = lax.ppermute(mine, "span", span_pairs)
        plane_pair = lax.ppermute(mine, "plane", plane_pairs)
        plane_other = lax.ppermute(mine, "plane", plane_others)
        chunk = math.lcm(width, 128)

        def scratch(count):
            return [
                pltpu.VMEM((count * nfaces, chunk), F32),
                pltpu.VMEM((nfaces, area), F32),
                pltpu.VMEM((3 * nfaces * area // chunk, chunk), BF16),
            ]

        if step == 0:
            (held,) = call(hold_kernel, [blocks, mine], [blocks.shape], [pl.ANY] * 2, [pltpu.SemaphoreType.DMA])
        last = step == ITERS - 1
        args = [line_slot, other, plane_other, pair, plane_pair, held, *picks, mine, *(us if last else us[-1:])]
        out = call(
            functools.partial(late_kernel, nplane, last),
            args,
            [shape] + ([(1, 128)] if last else [(per, width)] * nplane),
            [pl.ANY] + [pltpu.VMEM] * (len(args) - 1),
            scratch(nblocks) + [pltpu.SMEM(line_slot.shape, jnp.int32), pltpu.SemaphoreType.DMA],
            flops=2 * nblocks * nfaces * area,
        )
        us.append(out[0])
        send = out[1:]
    gram = add_up(send[0])
    sol, res, ok = call(finish_kernel, [gram, *us, *zs], [shape, shape, (1, 128)], pinned=False)
    given = (rhs, blocks, columns, line_slot, line_lower, line_upper, pivot_inv)
    _, sol, res = lax.while_loop(
        lambda state: state[0], lambda _: (jnp.array(False), *step_by_step(*given)), (ok[0, 0] < 0.5, sol.T, res.T)
    )
    return sol, res


def solution(mesh):
    both = ("span", "plane")
    return jax.shard_map(
        on_device,
        mesh=mesh,
        in_specs=(
            P(None, both),
            P(both, None),
            P(None, both),
            P(both, None),
            P(both, None),
            P(both, None),
            P(both, None),
        ),
        out_specs=(P(None, both), P(None, both)),
        check_vma=False,
    )
```

```python
import functools
import math

import jax
import jax.numpy as jnp
import numpy as np
from jax import lax
from jax.experimental import pallas as pl
from jax.experimental.pallas import tpu as pltpu
from jax.sharding import PartitionSpec as P

ITERS = 3
P_SIZE = 2
SHIFT = 2.0
EPS = 1e-6
VMEM_LIMIT = 16 * 1024 * 1024
HIGH = lax.Precision.HIGHEST
F32, BF16 = jnp.float32, jnp.bfloat16


def with_halo(x, sides, width, wrap):
    for axis, dim in sides:
        size, length = (lax.axis_size(axis), x.shape[dim])
        up = [(i, (i + 1) % size) for i in range(size if wrap else size - 1)]
        down = [(j, i) for i, j in up]
        last = lax.slice_in_dim(x, length - width, length, axis=dim)
        first = lax.slice_in_dim(x, 0, width, axis=dim)
        before = lax.ppermute(last, axis, up)
        after = lax.ppermute(first, axis, down)
        x = jnp.concatenate([before, x, after], axis=dim)
    return x


def small_solve(factor, target):
    extent = target.shape[0]
    forward_vals = []
    for row in range(extent):
        running = target[row]
        for inner in range(row):
            running = running - factor[row, inner] * forward_vals[inner]
        forward_vals.append(running / factor[row, row])
    backward_vals = [None] * extent
    for row in reversed(range(extent)):
        running = forward_vals[row]
        for inner in range(row + 1, extent):
            running = running - factor[inner, row] * backward_vals[inner]
        backward_vals[row] = running / factor[row, row]
    return jnp.stack(backward_vals)


def to_sequence(factor_rows, nlines, length, width):
    return jnp.swapaxes(factor_rows.reshape(nlines, length, width, width), 0, 1)


def line_solve(rhs_lines, lseq, useq, pseq):
    rseq = jnp.moveaxis(rhs_lines, 2, 0)

    def forward(prev, items):
        right, low = items
        cur = right - jnp.einsum("mab,bm->am", low, prev, precision=HIGH)
        return (cur, cur)

    start = jnp.zeros(rseq.shape[1:], F32)
    _, yseq = lax.scan(forward, start, (rseq, lseq))

    def backward(nxt, items):
        yval, upp, piv = items
        inner = yval - jnp.einsum("mab,bm->am", upp, nxt, precision=HIGH)
        cur = jnp.einsum("mab,bm->am", piv, inner, precision=HIGH)
        return (cur, cur)

    _, zseq = lax.scan(backward, start, (yseq, useq, pseq), reverse=True)
    return jnp.moveaxis(zseq, 0, 2)


def table_positions(columns, nfaces, my_span, my_plane, nspan, nplane):
    device_of = columns // nfaces
    span_of = device_of // nplane
    plane_of = device_of % nplane
    dspan = (span_of - my_span + 1 + nspan) % nspan - 1
    dplane = plane_of - my_plane
    selector = jnp.where(
        dspan == -1,
        1,
        jnp.where(dspan == 1, 2, jnp.where(dplane == -1, 3, jnp.where(dplane == 1, 4, 0))),
    )
    return selector * nfaces + columns % nfaces


def step_by_step(rhs, blocks, columns, line_slot, line_lower, line_upper, pivot_inv):
    width, nfaces = rhs.shape
    nblocks = columns.shape[0]
    nplane = lax.axis_size("plane")
    position = table_positions(
        columns, nfaces, lax.axis_index("span"), lax.axis_index("plane"), lax.axis_size("span"), nplane
    )
    slot = line_slot[0]
    lines_group = nfaces // P_SIZE
    owned = lines_group // nplane
    length = P_SIZE * nplane
    lower = to_sequence(line_lower, owned, length, width)
    upper = to_sequence(line_upper, owned, length, width)
    pivot = to_sequence(pivot_inv, owned, length, width)
    shaped_blocks = blocks.reshape(nfaces, nblocks, width, width)

    def apply_a(vec):
        shaped = vec.reshape(width, 1, 1, nfaces)
        span_side = with_halo(shaped, (("span", 1),), 1, True)
        plane_side = with_halo(shaped, (("plane", 2),), 1, False)
        below = plane_side[:, 0, 0]
        above = plane_side[:, 0, 2]
        table = jnp.concatenate([vec, span_side[:, 0, 0], span_side[:, 2, 0], below, above], axis=1)
        return jnp.einsum("ikab,bki->ai", shaped_blocks, table[:, position], precision=HIGH)

    def apply_m(vec):
        pieces = vec[:, slot].reshape(width, lines_group, P_SIZE)
        whole = lax.all_to_all(pieces, "plane", split_axis=1, concat_axis=2, tiled=True)
        solved = line_solve(whole, lower, upper, pivot)
        back = lax.all_to_all(solved, "plane", split_axis=2, concat_axis=1, tiled=True)
        return jnp.zeros_like(vec).at[:, slot].set(back.reshape(width, nfaces))

    beta = jnp.sqrt(lax.psum(jnp.sum(rhs * rhs), ("span", "plane")) + EPS)
    basis = [rhs / beta]
    hcols = []
    for step in range(ITERS):
        wvec = apply_a(apply_m(basis[step]))
        stacked = jnp.stack(basis)
        hvals = lax.psum(jnp.einsum("jai,ai->j", stacked, wvec, precision=HIGH), ("span", "plane"))
        wvec = wvec - jnp.einsum("j,jai->ai", hvals, stacked, precision=HIGH)
        hnext = jnp.sqrt(lax.psum(jnp.sum(wvec * wvec), ("span", "plane")) + EPS)
        basis.append(wvec / hnext)
        hcols.append(jnp.concatenate([hvals, hnext[None], jnp.zeros((ITERS - step - 1,), F32)]))
    hmat = jnp.stack(hcols, axis=1)
    factor = jnp.linalg.cholesky(jnp.dot(hmat.T, hmat, precision=HIGH))
    coef = small_solve(factor, beta * hmat[0])
    update = jnp.einsum("j,jai->ai", coef, jnp.stack(basis[:ITERS]), precision=HIGH)
    solution = apply_m(update)
    return solution, rhs - apply_a(solution)


def partner(me, k, size):
    if size & (size - 1) == 0:
        return me ^ k, me ^ k
    return (me + k) % size, (me + size - k) % size


def far_first(size):
    return list(reversed(range(size)))


def exchange(x, axis, k):
    size = lax.axis_size(axis)
    return lax.ppermute(x, axis, [(i, partner(i, k, size)[0]) for i in range(size)])


def split(x, parts):
    out = []
    for _ in range(parts):
        out.append(x.astype(BF16).astype(F32))
        x = x - out[-1]
    return jnp.concatenate(out, axis=0)


def start_kernel(nplane, slot_ref, u_ref, copy_ref, choose_ref, *outs):
    nfaces = u_ref.shape[0]
    per = nfaces // nplane
    me = lax.axis_index("plane")
    for k in range(nplane):
        to, _ = partner(me, k, nplane)
        for i in range(per):
            outs[k][pl.ds(i, 1), :] = u_ref[pl.ds(slot_ref[0, to * per + i], 1), :]
    copy_ref[...] = u_ref[...]
    face = lax.broadcasted_iota(jnp.int32, choose_ref.shape, 0)
    piece = lax.broadcasted_iota(jnp.int32, choose_ref.shape, 1) % nfaces
    choose = jnp.zeros(choose_ref.shape, F32)
    for n, k in enumerate(far_first(nplane)):
        _, source = partner(me, k, nplane)
        for i in range(per):
            hit = (face == slot_ref[0, source * per + i]) & (piece == n * per + i)
            choose = jnp.where(hit, 1.0, choose)
    choose_ref[...] = choose


def to_squares(src, dst):
    nrows, width = src.shape[0], dst.shape[1]
    chunk = math.lcm(width, 128)
    for c in range(width * width // chunk):
        piece = src[:, c * chunk : (c + 1) * chunk]
        for r in range(chunk // width):
            a = c * (chunk // width) + r
            dst[pl.ds(a, nrows, stride=width), :] = piece[:, r * width : (r + 1) * width]


def turn_some(squares, length, parity):
    width = squares.shape[1]
    for at in range(squares.shape[0] // width):
        if at % length % 2 == parity and at % length:
            here = slice(at * width, (at + 1) * width)
            squares[here, :] = squares[here, :].T


def first_squares_kernel(length, low, piv, upp, _, low_out, piv_out, fold_out, low_scr, piv_scr, upp_scr, upp_sq, sems):
    width = low_out.shape[1]
    fetches = []
    for n, (src, scr) in enumerate(((low, low_scr), (piv, piv_scr), (upp, upp_scr))):
        fetches.append(pltpu.make_async_copy(src, scr, sems.at[n]))
        fetches[-1].start()
    for fetch, scr, dst in zip(fetches, (low_scr, piv_scr, upp_scr), (low_out, piv_out, upp_sq)):
        fetch.wait()
        to_squares(scr, dst)
    for at in range(low.shape[0]):
        here = slice(at * width, (at + 1) * width)
        if at % length == length - 1:
            fold_out[here, :] = jnp.zeros((width, width), F32)
            continue
        (ph, pl_), (uh, ul) = [
            (x.astype(BF16), (x - x.astype(BF16).astype(F32)).astype(BF16)) for x in (piv_out[here, :], upp_sq[here, :])
        ]
        fold = sum(jnp.dot(x, y, preferred_element_type=F32) for x, y in ((pl_, uh), (ph, ul), (ph, uh)))
        fold_out[here, :] = fold.T if at % length % 2 else fold
    turn_some(low_out, length, 0)
    turn_some(piv_out, length, 1)


def next_squares_kernel(length, low, piv, fold, _, low_out, piv_out, fold_out, low_scr, piv_scr, sems):
    fetches = []
    for n, (src, scr) in enumerate(((low, low_scr), (piv, piv_scr), (fold, fold_out))):
        fetches.append(pltpu.make_async_copy(src, scr, sems.at[n]))
        fetches[-1].start()
    for fetch, scr, dst, parity in zip(fetches, (low_scr, piv_scr), (low_out, piv_out), (0, 1)):
        fetch.wait()
        to_squares(scr, dst)
        turn_some(dst, length, parity)
    fetches[2].wait()


def parities():
    return [1 if lax.axis_size(a) % 2 else lax.axis_index(a) % 2 for a in ("span", "plane")]


def pick_kernel(nspan, nplane, width, columns_ref, fold_ref, pick_ref, seg_ref, store_ref, sem):
    store = pltpu.make_async_copy(fold_ref, store_ref, sem)
    store.start()
    copies = seg_ref.shape[0] // width
    lane = lax.broadcasted_iota(jnp.int32, (width, 128), 1) % copies
    for r in range(copies):
        seg_ref[r * width : (r + 1) * width, :] = jnp.where(lane == r, 1.0, 0.0).astype(BF16)
    nblocks, nfaces = columns_ref.shape
    span, plane = lax.axis_index("span"), lax.axis_index("plane")
    position = table_positions(columns_ref[...], nfaces, span, plane, nspan, nplane)
    selector, face = position // nfaces, position % nfaces
    span_odd, plane_odd = [parity == 1 for parity in parities()]
    of_span = jnp.where((selector == 1) == span_odd, 1, 3)
    of_plane = jnp.where((selector == 3) == plane_odd, 2, 4)
    group = jnp.where(selector == 0, 0, jnp.where(selector <= 2, of_span, of_plane))
    at = (group * nfaces + face).astype(F32)
    eye = lax.broadcasted_iota(jnp.int32, (nfaces, nfaces), 0) == lax.broadcasted_iota(jnp.int32, (nfaces, nfaces), 1)
    lane = lax.broadcasted_iota(jnp.int32, (nfaces, pick_ref.shape[1]), 1) % (pick_ref.shape[1] // 3)
    for k in range(nblocks):
        column = jnp.sum(jnp.where(eye, at[k : k + 1], 0.0), axis=1, keepdims=True).astype(jnp.int32)
        pick_ref[k * nfaces : (k + 1) * nfaces, :] = jnp.where(lane == column, 1.0, 0.0).astype(BF16)
    store.wait()


def line_kernel(nplane, nlines, *refs):
    msgs, (low, piv, fold), outs, (r_scr, z_scr) = refs[:nplane], refs[nplane:-nplane-2], refs[-nplane-2:-2], refs[-2:]
    _, length, width = r_scr.shape
    me = lax.axis_index("plane")
    for k, msg in zip(far_first(nplane), msgs):
        _, source = partner(me, k, nplane)
        for m in range(nlines):
            for q in range(P_SIZE):
                r_scr[m, pl.ds(source * P_SIZE + q, 1), :] = msg[pl.ds(m * P_SIZE + q, 1), :]
    eye = lax.broadcasted_iota(jnp.int32, (width, width), 0) == lax.broadcasted_iota(jnp.int32, (width, width), 1)

    def column(row):
        return jnp.sum(jnp.where(eye, row, 0.0), axis=1, keepdims=True)

    rows = [[r_scr[m, pl.ds(j, 1), :] for m in range(nlines)] for j in range(length)]
    scaled = [[None] * nlines for _ in range(length)]
    carry = [None] * nlines
    for j in range(length):
        for m in range(nlines):
            at = m * length + j
            if j == 0:
                carry[m] = rows[j][m]
            elif j % 2:
                carry[m] = column(rows[j][m]) - jnp.sum(low[at] * carry[m], axis=1, keepdims=True)
            else:
                carry[m] = rows[j][m] - jnp.sum(low[at] * carry[m], axis=0, keepdims=True)
            scaled[j][m] = jnp.sum(piv[at] * carry[m], axis=0 if j % 2 else 1, keepdims=True)
    after = [None] * nlines
    for j in reversed(range(length)):
        for m in range(nlines):
            at = m * length + j
            value = scaled[j][m]
            if j < length - 1:
                value = value - jnp.sum(fold[at] * after[m], axis=0 if j % 2 else 1, keepdims=True)
            after[m] = value
            row = value if j % 2 else jnp.sum(jnp.where(eye, value, 0.0), axis=0, keepdims=True)
            z_scr[m, pl.ds(j, 1), :] = row
    for k in range(nplane):
        to, _ = partner(me, k, nplane)
        for m in range(nlines):
            for q in range(P_SIZE):
                outs[k][pl.ds(m * P_SIZE + q, 1), :] = z_scr[m, pl.ds(to * P_SIZE + q, 1), :]


def faces_kernel(nplane, choose, *refs):
    solved, mine_ref = refs[:nplane], refs[-1]
    table = split(jnp.concatenate([s[...] for s in solved], axis=0), 3).astype(BF16)
    mine_ref[...] = jnp.dot(choose[...].astype(BF16), table, preferred_element_type=F32)


def repeat_faces(faces, pick, copies):
    table = split(jnp.concatenate([f[...] for f in faces], axis=0), 3).astype(BF16)
    picked = jnp.dot(pick[...], table, preferred_element_type=F32)
    return jnp.concatenate([picked] * copies, axis=1)


def add_products(work, x_scr, acc_scr, parts, seg, width):
    nfaces, area = acc_scr.shape
    chunk = x_scr.shape[1]
    copies, count = chunk // width, area // chunk
    lane = lax.broadcasted_iota(jnp.int32, (1, 128), 1)
    total = jnp.zeros((nfaces, 128), F32)
    done = 0
    for n, (places, fetch) in enumerate(work):
        if fetch is not None:
            fetch.wait()
        last = n == len(work) - 1
        for half in ((0, count // 2), (count // 2, count)):
            for v in range(0, chunk, 128):
                rows = range(done * nfaces, (done + len(places)) * nfaces, nfaces)
                xs = [x_scr[row : row + nfaces, v : v + 128] for row in rows]
                for c in range(*half):
                    at = c * chunk + v
                    value = acc_scr[:, at : at + 128] if n else None
                    for (ref, column), x in zip(places, xs):
                        term = ref[:, column + at : column + at + 128] * x
                        value = term if value is None else value + term
                    if not last:
                        acc_scr[:, at : at + 128] = value
                        continue
                    for n_part in range(3):
                        part = value.astype(BF16)
                        row = (3 * c + n_part) * nfaces
                        parts[row : row + nfaces, v : v + 128] = part
                        value = value - part.astype(F32)
            if last:
                base = 3 * half[0] * nfaces
                sums = jnp.dot(parts[base : 3 * half[1] * nfaces, :], seg[...], preferred_element_type=F32)
                for c in range(*half):
                    high, middle, low = [
                        sums[at : at + nfaces] for at in range(3 * c * nfaces - base, 3 * (c + 1) * nfaces - base, nfaces)
                    ]
                    total = total + jnp.where(lane // copies == c, high + (middle + low), 0.0)
        done += len(places)
    return total[:, :width]


def hold_kernel(blocks, _, held, sem):
    fetch = pltpu.make_async_copy(blocks, held, sem)
    fetch.start()
    fetch.wait()


def late_kernel(nplane, last, *refs):
    (slot, other, pair, plane_pair, plane_other, held, pick, seg, mine), refs = refs[:9], refs[9:]
    faces = (mine, pair, plane_pair, other, plane_other)
    nold = ITERS if last else 1
    olds, refs = refs[:nold], refs[nold:]
    next_ref, outs, (x_scr, acc_scr, parts, slot_scr, slot_sem) = refs[0], refs[1:-5], refs[-5:]
    nfaces, width = faces[0].shape
    area = width * width
    if not last:
        slots = pltpu.make_async_copy(slot, slot_scr, slot_sem)
        slots.start()
    x_scr[...] = repeat_faces(faces, pick, x_scr.shape[1] // width)
    work = [([(held, column) for column in range(0, held.shape[1], area)], None)]
    u_next = add_products(work, x_scr, acc_scr, parts, seg, width) - SHIFT * olds[-1][...]
    next_ref[...] = u_next
    if last:
        gram_ref = outs[0]
        lane = lax.broadcasted_iota(jnp.int32, gram_ref.shape, 1)
        basis = [old[...] for old in olds] + [u_next]
        gram, at = jnp.zeros(gram_ref.shape, F32), 0
        for i in range(ITERS + 1):
            for j in range(i, ITERS + 1):
                value = jnp.sum(jnp.sum(basis[i] * basis[j], axis=0, keepdims=True), axis=1, keepdims=True)
                gram, at = jnp.where(lane == at, value, gram), at + 1
        gram_ref[...] = gram
    else:
        per = nfaces // nplane
        me = lax.axis_index("plane")
        slots.wait()
        for k in range(nplane):
            to, _ = partner(me, k, nplane)
            for i in range(per):
                outs[k][pl.ds(i, 1), :] = next_ref[pl.ds(slot_scr[0, to * per + i], 1), :]


def finish_kernel(gram_ref, *refs):
    us, zs = refs[: ITERS + 1], refs[ITERS + 1 : 2 * ITERS + 1]
    sol_ref, res_ref, ok_ref = refs[2 * ITERS + 1 :]
    width = sol_ref.shape[1]
    rows = jnp.sum(gram_ref[...], axis=0, keepdims=True)
    lane = lax.broadcasted_iota(jnp.int32, rows.shape, 1)
    gram, at = {}, 0
    for i in range(ITERS + 1):
        for j in range(i, ITERS + 1):
            value = jnp.sum(jnp.where(lane == at, rows, 0.0), axis=1, keepdims=True)
            gram[i, j] = gram[j, i] = jnp.broadcast_to(value, rows.shape)
            at += 1
    largest = functools.reduce(jnp.maximum, [jnp.abs(g) for g in gram.values()])
    ok = largest < 1e30
    beta = jnp.sqrt(gram[0, 0] + EPS)
    basis = [[1.0 / beta]]
    hmat = {}
    for step in range(ITERS):
        own = basis[step]
        wvec = [SHIFT * own[0]] + [own[i] + SHIFT * own[i + 1] for i in range(step)] + [own[step]]
        images = [sum(gram[i, j] * wvec[j] for j in range(step + 2)) for i in range(step + 1)]
        for i in range(step + 1):
            hmat[i, step] = sum(basis[i][m] * images[m] for m in range(i + 1))
        for i in range(step + 1):
            for m in range(i + 1):
                wvec[m] = wvec[m] - hmat[i, step] * basis[i][m]
        terms = [wvec[i] * wvec[j] * gram[i, j] for i in range(step + 2) for j in range(step + 2)]
        square = jnp.maximum(sum(terms), 0.0)
        ok = ok & (square + EPS >= 2e-3 * sum(jnp.abs(term) for term in terms))
        hmat[step + 1, step] = jnp.sqrt(square + EPS)
        scale = 1.0 / hmat[step + 1, step]
        basis.append([w * scale for w in wvec])
    normal = {
        (i, j): sum(hmat[m, i] * hmat[m, j] for m in range(j + 2) if (m, i) in hmat and (m, j) in hmat)
        for i in range(ITERS)
        for j in range(i + 1)
    }
    factor, inverse = {}, []
    for j in range(ITERS):
        diag = jnp.sqrt(normal[j, j] - sum(factor[j, m] * factor[j, m] for m in range(j)))
        inverse.append(1.0 / diag)
        for i in range(j + 1, ITERS):
            factor[i, j] = (normal[i, j] - sum(factor[i, m] * factor[j, m] for m in range(j))) * inverse[j]
    forward = []
    for i in range(ITERS):
        forward.append((beta * hmat[0, i] - sum(factor[i, m] * forward[m] for m in range(i))) * inverse[i])
    coef = [None] * ITERS
    for i in reversed(range(ITERS)):
        coef[i] = (forward[i] - sum(factor[m, i] * coef[m] for m in range(i + 1, ITERS))) * inverse[i]
    mix = [sum(coef[s] * basis[s][m] for s in range(m, ITERS))[:, :width] for m in range(ITERS)]
    sol_ref[...] = sum(mix[m] * zs[m][...] for m in range(ITERS))
    image = sum(mix[m] * (us[m + 1][...] + SHIFT * us[m][...]) for m in range(ITERS))
    res_ref[...] = us[0][...] - image
    ok = ok & (functools.reduce(jnp.maximum, [jnp.abs(c) for c in coef]) < 1e30)
    ok_ref[...] = jnp.where(ok, 1.0, 0.0)


def call(kernel, args, outs, spaces=None, scratch=(), flops=0, pinned=True, ready=True):
    spaces = [pltpu.VMEM] * len(args) if spaces is None else spaces
    if ready:
        args = [pltpu.with_memory_space_constraint(x, s) if s is pltpu.VMEM else x for x, s in zip(args, spaces)]
    size = sum(x.dtype.itemsize * math.prod(x.shape) for x in args)
    return pl.pallas_call(
        kernel,
        out_shape=[pltpu.VMEM(shape, F32) if pinned else jax.ShapeDtypeStruct(shape, F32) for shape in outs],
        in_specs=[pl.BlockSpec(memory_space=s) for s in spaces],
        out_specs=[pl.BlockSpec(memory_space=pltpu.VMEM) for _ in outs],
        scratch_shapes=scratch,
        compiler_params=pltpu.CompilerParams(vmem_limit_bytes=VMEM_LIMIT),
        cost_estimate=pl.CostEstimate(flops=flops, bytes_accessed=size, transcendentals=0),
    )(*args)


def add_up(x):
    count = lax.axis_size("span") * lax.axis_size("plane")
    rows = jnp.broadcast_to(x, (count, x.shape[1]))
    return lax.all_to_all(rows, ("span", "plane"), split_axis=0, concat_axis=0, tiled=True)


def pairings(size):
    if size % 2:
        return [(i, (i + 1) % size) for i in range(size)], [(i, (i - 1) % size) for i in range(size)]
    return [(i, i ^ 1) for i in range(size)], [(i, (i + 1 if i % 2 else i - 1) % size) for i in range(size)]


def on_device(rhs, blocks, columns, line_slot, line_lower, line_upper, pivot_inv):
    width, nfaces = rhs.shape
    nblocks = columns.shape[0]
    nspan, nplane = lax.axis_size("span"), lax.axis_size("plane")
    owned = nfaces // P_SIZE // nplane
    length = P_SIZE * nplane
    per = owned * P_SIZE
    area = width * width
    shape = (nfaces, width)
    span_pairs, span_others = pairings(nspan)
    plane_pairs, plane_others = pairings(nplane)

    u_first, choose, *send = call(
        functools.partial(start_kernel, nplane),
        [line_slot, rhs.T],
        [shape, (nfaces, 3 * nfaces)] + [(per, width)] * nplane,
        [pltpu.SMEM, pltpu.VMEM],
        ready=False,
    )
    us = [u_first]
    zs = []
    picks = held = None
    for step in range(ITERS):
        flat = pltpu.VMEM((nfaces, area), F32)
        squares = [(nfaces * width, width)] * 3
        if step == 0:
            factors = call(
                functools.partial(first_squares_kernel, length),
                [line_lower, pivot_inv, line_upper, us[-1]],
                squares,
                [pl.ANY] * 4,
                [flat] * 3 + [pltpu.VMEM(squares[0], F32), pltpu.SemaphoreType.DMA((3,))],
                flops=nfaces * area * width,
            )
        else:
            factors = call(
                functools.partial(next_squares_kernel, length),
                [line_lower, pivot_inv, fold, us[-1]],
                squares,
                [pl.ANY] * 4,
                [flat] * 2 + [pltpu.SemaphoreType.DMA((3,))],
                flops=nfaces * area,
            )
        shaped = [x.reshape(nfaces, width, width) for x in factors]
        got = [exchange(send[k], "plane", k) if k else send[0] for k in far_first(nplane)]
        solved = call(
            functools.partial(line_kernel, nplane, owned),
            [*got, *shaped],
            [(per, width)] * nplane,
            scratch=[pltpu.VMEM((owned, length, width), F32)] * 2,
            flops=6 * nfaces * area,
        )
        if step == 0:
            *picks, fold = pl.pallas_call(
                functools.partial(pick_kernel, nspan, nplane, width),
                out_shape=[
                    pltpu.VMEM((nblocks * nfaces, 15 * nfaces), BF16),
                    pltpu.VMEM((math.lcm(width, 128), 128), BF16),
                    pltpu.HBM(squares[0], F32),
                ],
                in_specs=[pl.BlockSpec(memory_space=pltpu.VMEM)] * 2,
                out_specs=[pl.BlockSpec(memory_space=pltpu.VMEM)] * 2 + [pl.BlockSpec(memory_space=pl.ANY)],
                scratch_shapes=[pltpu.SemaphoreType.DMA],
                compiler_params=pltpu.CompilerParams(vmem_limit_bytes=VMEM_LIMIT),
                cost_estimate=pl.CostEstimate(flops=0, bytes_accessed=4 * nfaces * area, transcendentals=0),
            )(
                lax.optimization_barrier((columns, solved[0]))[0],
                pltpu.with_memory_space_constraint(factors[2], pltpu.VMEM),
            )
        pieces = [exchange(solved[k], "plane", k) if k else solved[0] for k in far_first(nplane)]
        args = [choose, *pieces, *(picks if step == 0 else ())]
        spaces = [pltpu.VMEM] * (nplane + 1) + [pl.ANY] * (len(args) - nplane - 1)
        (mine,) = call(functools.partial(faces_kernel, nplane), args, [shape], spaces)
        zs.append(mine)
        other = lax.ppermute(mine, "span", span_others)
        pair = lax.ppermute(mine, "span", span_pairs)
        plane_pair = lax.ppermute(mine, "plane", plane_pairs)
        plane_other = lax.ppermute(mine, "plane", plane_others)
        chunk = math.lcm(width, 128)

        def scratch(count):
            return [
                pltpu.VMEM((count * nfaces, chunk), F32),
                pltpu.VMEM((nfaces, area), F32),
                pltpu.VMEM((3 * nfaces * area // chunk, chunk), BF16),
            ]

        if step == 0:
            (held,) = call(hold_kernel, [blocks, mine], [blocks.shape], [pl.ANY] * 2, [pltpu.SemaphoreType.DMA])
        last = step == ITERS - 1
        args = [line_slot, other, pair, plane_pair, plane_other, held, *picks, mine, *(us if last else us[-1:])]
        out = call(
            functools.partial(late_kernel, nplane, last),
            args,
            [shape] + ([(1, 128)] if last else [(per, width)] * nplane),
            [pl.ANY] + [pltpu.VMEM] * (len(args) - 1),
            scratch(nblocks) + [pltpu.SMEM(line_slot.shape, jnp.int32), pltpu.SemaphoreType.DMA],
            flops=2 * nblocks * nfaces * area,
        )
        us.append(out[0])
        send = out[1:]
    gram = add_up(send[0])
    sol, res, ok = call(finish_kernel, [gram, *us, *zs], [shape, shape, (1, 128)], pinned=False)
    given = (rhs, blocks, columns, line_slot, line_lower, line_upper, pivot_inv)
    _, sol, res = lax.while_loop(
        lambda state: state[0], lambda _: (jnp.array(False), *step_by_step(*given)), (ok[0, 0] < 0.5, sol.T, res.T)
    )
    return sol, res


def solution(mesh):
    both = ("span", "plane")
    return jax.shard_map(
        on_device,
        mesh=mesh,
        in_specs=(
            P(None, both),
            P(both, None),
            P(None, both),
            P(both, None),
            P(both, None),
            P(both, None),
            P(both, None),
        ),
        out_specs=(P(None, both), P(None, both)),
        check_vma=False,
    )
```
